32 devices in a mesh: groups: 2 (over y), tm: 4 (over z), band: 2 (over x), tmpl: 2 (over core).
Axes of the slice: x: 2, y: 2, z: 4, core: 2. Of those that a mesh axis runs over, the one named last changes fastest.
Arguments:
- sft_bins: float32 [2, 128, 2048], P(None, ('groups', 'tm'), 'band'), parts along dimension 1, may hold values from -6 to 6
- delay_code: int32 [8, 128, 1024], P(('groups', 'tmpl'), None, ('tm', 'band')), parts along dimension 0, may hold values from 0 to 16007, as said below
- antenna: float32 [8, 2, 128, 1024], P(('groups', 'tmpl'), None, None, ('tm', 'band')), parts along dimension 0, may hold values from -10 to 10
Outputs:
- f_stat: float32 [8, 128, 8, 128], P(('groups', 'tmpl'), None, ('tm', 'band')), parts along dimension 0
The draws below stay inside these ranges and needn't reach their ends.
There are 2 independent parts, one for each index of `groups`. The reference program is written for one: setup_inputs(seed, part) draws one part's arguments, and reference() takes and returns one part's arrays. A program takes and returns all parts, laid end to end along the dimension named above; each array names one. Nothing has to cross between parts.
Inputs may be any that keep to these rules, and one draw needn't show every extreme that they name: `delay_code`: the whole delay o of a template is the same for all samples n of each aligned run of 256 samples (n // 256 equal).
All inputs are finite; a program needn't handle non-finite values.
Results may differ from the reference program's by a relative error of at most 0.0003.
Values sent between devices are 32-bit elements; how exact they have to be, the bound alone decides.
A program may use at most 64 MiB of HBM per device.

```python
import math
import jax
import jax.numpy as jnp
from jax import lax

NB = 2048
NQ = 128
NP = 16
SFT_DEV = 8
MAXD = 1000
NFRAC = 8
RUN = 256
NI = 8
NSFT = 64
SAMPLES = 131072
TEMPLATES = 4


def draw_delay_code(key, part):
    blocks = SAMPLES // RUN
    offsets = jax.random.randint(jax.random.fold_in(key, 1), (TEMPLATES, blocks), -MAXD, MAXD + 1)
    block_at = jnp.arange(blocks, dtype=jnp.int32)
    span_len = SFT_DEV * NB
    first_run = (block_at * RUN % span_len == 0)[None, :]
    last_run = ((block_at + 1) * RUN % span_len == 0)[None, :]
    lead_row = (jnp.arange(TEMPLATES, dtype=jnp.int32) == 0)[:, None]
    offsets = jnp.where(first_run & lead_row, -MAXD, offsets)
    offsets = jnp.where(last_run & lead_row, MAXD, offsets)
    offsets = jnp.repeat(offsets, RUN, axis=1)
    fraction = jax.random.randint(jax.random.fold_in(key, 2), (TEMPLATES, SAMPLES), 0, NFRAC)
    fraction = fraction.at[0, 0].set(0)
    fraction = fraction.at[0, SAMPLES - 1].set(NFRAC - 1)
    coded_rows = NFRAC * (offsets + MAXD) + fraction
    coded_rows = coded_rows.reshape(TEMPLATES, NSFT, NQ, NP).transpose(0, 2, 1, 3)
    return coded_rows.reshape(TEMPLATES, NQ, NSFT * NP).astype(jnp.int32)


def draw_antenna(key, part):
    moment = (jnp.arange(SAMPLES, dtype=jnp.float32) + 0.5) / SAMPLES
    lift_ratio = 2.0
    basis_a = jnp.clip(jax.random.normal(jax.random.fold_in(key, 1), (TEMPLATES, SAMPLES), jnp.float32), -4.0, 4.0)
    basis_b = jnp.clip(jax.random.normal(jax.random.fold_in(key, 2), (TEMPLATES, SAMPLES), jnp.float32), -4.0, 4.0)
    ranked = jax.random.permutation(jax.random.fold_in(key, 3), TEMPLATES)
    strong = (ranked < TEMPLATES // 2)[:, None]
    high_coupling = jax.random.uniform(jax.random.fold_in(key, 4), (TEMPLATES, 1), jnp.float32, 0.95, 0.99)
    low_coupling = jax.random.uniform(jax.random.fold_in(key, 5), (TEMPLATES, 1), jnp.float32, -0.4, 0.4)
    coupling = jnp.where(strong, high_coupling, low_coupling)
    envelope_a = jnp.sqrt(1.0 + lift_ratio * moment)
    envelope_b = jnp.sqrt(1.0 + lift_ratio * (1.0 - moment))
    weight_a = envelope_a * basis_a
    weight_b = envelope_b * (coupling * basis_a + jnp.sqrt(1.0 - coupling * coupling) * basis_b)
    stacked = jnp.stack([weight_a, weight_b], axis=1)
    stacked = stacked.reshape(TEMPLATES, 2, NSFT, NQ, NP).transpose(0, 1, 3, 2, 4)
    return stacked.reshape(TEMPLATES, 2, NQ, NSFT * NP).astype(jnp.float32)


def shard_levels(own_key, shape, pieces, smallest, top_value):
    def one(position, parts):
        draws = jax.random.uniform(jax.random.fold_in(jax.random.fold_in(own_key, 6), position), (parts,), jnp.float32, smallest / len(pieces), top_value / len(pieces))
        return jnp.repeat(jnp.exp(draws), shape[position] // parts).reshape((-1,) + (1,) * (len(shape) - position - 1))

    gain = one(*pieces[0])
    for cut in pieces[1:]:
        gain = gain * one(*cut)
    return gain


def gaussian(own_key, extent, width, bound, shards=(), kind=jnp.bfloat16):
    entries = width * jax.random.normal(own_key, extent, jnp.float32)
    if shards:
        entries = entries * shard_levels(own_key, extent, shards, -0.22, 0.18)
    return jnp.clip(entries, -bound, bound).astype(kind)


def setup_inputs(seed: int = 0, part: int = 0) -> dict:
    arg_keys = jax.random.split(jax.random.key(seed), 4)
    part_keys = jax.random.split(jax.random.fold_in(arg_keys[3], part), 4)
    return {
        "sft_bins": gaussian(part_keys[0], (2, NSFT, NB), 1.0, 6.0, ((1, 4), (2, 2)), jnp.float32),
        "delay_code": draw_delay_code(jax.random.fold_in(jax.random.fold_in(arg_keys[3], part), 71), part),
        "antenna": draw_antenna(jax.random.fold_in(jax.random.fold_in(arg_keys[3], part), 71), part),
    }


stat_eps = 1e-06
floor_share = 0.5

def lagrange(fraction):
    return (-fraction * (fraction - 1.0) * (fraction - 2.0) / 6.0, (fraction + 1.0) * (fraction - 1.0) * (fraction - 2.0) / 2.0, -(fraction + 1.0) * fraction * (fraction - 2.0) / 2.0, (fraction + 1.0) * fraction * (fraction - 1.0) / 6.0)

def reference(sft_bins, delay_code, antenna):
    spectrum = lax.complex(sft_bins[0], sft_bins[1])
    series = (jnp.fft.ifft(spectrum, axis=1) * math.sqrt(NB)).reshape(SAMPLES)
    margin = MAXD + 2
    padding = jnp.zeros((margin,), series.dtype)
    padded = jnp.concatenate([padding, series, padding])
    code_rows = delay_code.reshape(TEMPLATES, NQ, NSFT, NP).transpose(0, 2, 1, 3).reshape(TEMPLATES, SAMPLES)
    weight_rows = antenna.reshape(TEMPLATES, 2, NQ, NSFT, NP).transpose(0, 1, 3, 2, 4).reshape(TEMPLATES, 2, SAMPLES)

    def one_template(inputs):
        code_row, weights = inputs
        offsets = code_row // NFRAC - MAXD
        fraction = (code_row % NFRAC).astype(jnp.float32) / NFRAC
        coeffs = lagrange(fraction)
        base_pos = jnp.arange(SAMPLES, dtype=jnp.int32) + offsets - 1 + margin
        resampled = coeffs[0] * padded[base_pos]
        for tap_index in range(1, 4):
            resampled = resampled + coeffs[tap_index] * padded[base_pos + tap_index]
        weight_a = weights[0]
        weight_b = weights[1]
        spec_a = jnp.fft.fft(weight_a * resampled) / math.sqrt(SAMPLES)
        spec_b = jnp.fft.fft(weight_b * resampled) / math.sqrt(SAMPLES)
        power_a = jnp.mean(weight_a * weight_a) + stat_eps
        power_b = jnp.mean(weight_b * weight_b) + stat_eps
        cross_ab = jnp.mean(weight_a * weight_b)
        det_floor = jnp.maximum(power_a * power_b - cross_ab * cross_ab, floor_share * power_a * power_b)
        a_real, a_imag = (jnp.real(spec_a), jnp.imag(spec_a))
        b_real, b_imag = (jnp.real(spec_b), jnp.imag(spec_b))
        f_stat = (power_b * (a_real * a_real + a_imag * a_imag) + power_a * (b_real * b_real + b_imag * b_imag) - 2.0 * cross_ab * (a_real * b_real + a_imag * b_imag)) / det_floor
        return f_stat.reshape(NP, NQ, SFT_DEV, NI).transpose(1, 3, 2, 0).reshape(NQ, NI, SFT_DEV * NP)
    return lax.map(one_template, (code_rows, weight_rows))
```

```python
import functools
import math

import jax
import jax.numpy as jnp
import ml_dtypes
import numpy as np
from jax import lax
from jax.experimental import pallas as pl
from jax.experimental.pallas import tpu as pltpu
from jax.sharding import PartitionSpec as P

NB = 2048
NQ = 128
NP = 16
SFT_DEV = 8
MAXD = 1000
NFRAC = 8
RUN = 256
LANES = 128

stat_eps = 1e-06
floor_share = 0.5
MESH = pl.DeviceIdType.MESH


def shifted(value, axis, by):
    length = lax.axis_size(axis)
    pairs = [(i, i + by) for i in range(length) if 0 <= i + by < length]
    return lax.ppermute(value, axis, pairs)


def lagrange(fraction):
    return (
        -fraction * (fraction - 1.0) * (fraction - 2.0) / 6.0,
        (fraction + 1.0) * (fraction - 1.0) * (fraction - 2.0) / 2.0,
        -(fraction + 1.0) * fraction * (fraction - 2.0) / 2.0,
        (fraction + 1.0) * fraction * (fraction - 1.0) / 6.0,
    )


def phase_pair(product, modulus, direction):
    angles = direction * 2.0 * math.pi / modulus * (product % modulus).astype(jnp.float32)
    return (jnp.cos(angles), jnp.sin(angles))


def dft_table(length, direction):
    rows_at = lax.broadcasted_iota(jnp.int32, (length, length), 0)
    cols_at = lax.broadcasted_iota(jnp.int32, (length, length), 1)
    return phase_pair(rows_at * cols_at, length, direction)


def complex_einsum(pattern, lhs_pair, rhs_pair):
    lhs_real, lhs_imag = lhs_pair
    rhs_real, rhs_imag = rhs_pair
    high = lax.Precision.HIGHEST
    out_real = jnp.einsum(pattern, lhs_real, rhs_real, precision=high) - jnp.einsum(
        pattern, lhs_imag, rhs_imag, precision=high
    )
    out_imag = jnp.einsum(pattern, lhs_real, rhs_imag, precision=high) + jnp.einsum(
        pattern, lhs_imag, rhs_real, precision=high
    )
    return (out_real, out_imag)


def rotate(values, phases):
    val_real, val_imag = values
    cos_part, sin_part = phases
    return (val_real * cos_part - val_imag * sin_part, val_real * sin_part + val_imag * cos_part)


def split2(value):
    high = value.astype(jnp.bfloat16)
    return high, (value - high.astype(jnp.float32)).astype(jnp.bfloat16)


def dot3(lhs, rhs):
    lhs_hi, lhs_lo = lhs
    rhs_hi, rhs_lo = rhs
    dot = functools.partial(jnp.dot, preferred_element_type=jnp.float32)
    return dot(lhs_hi, rhs_hi) + (dot(lhs_hi, rhs_lo) + dot(lhs_lo, rhs_hi))


def swap_blocks(blocks):
    count = len(blocks)
    width = LANES // count
    blocks = list(blocks)
    lane_block = lax.broadcasted_iota(jnp.int32, blocks[0].shape, 1) // width
    half = count // 2
    while half:
        keep = (lane_block & half) == 0
        for i in range(count):
            if i & half == 0:
                low, high = blocks[i], blocks[i + half]
                blocks[i] = jnp.where(keep, low, pltpu.roll(high, half * width, 1))
                blocks[i + half] = jnp.where(
                    keep, pltpu.roll(low, LANES - half * width, 1), high
                )
        half //= 2
    return blocks


def grid_to_time(ref, index, out_ref, out_index):
    rows = ref.shape[-2]
    per = rows // SFT_DEV
    blocks = [ref[index + (pl.ds(i, per, stride=SFT_DEV),)] for i in range(SFT_DEV)]
    for j, block in enumerate(swap_blocks(blocks)):
        out_ref[out_index + (slice(j * per, (j + 1) * per),)] = block


def resample_kernel(start_ref, buf_ref, code_ref, ant_ref, x_ref, sums_ref, code_t, ant_t, seg):
    tmpl_local = code_ref.shape[0]
    rows = code_ref.shape[1]
    runs = start_ref.shape[1]
    lane = lax.broadcasted_iota(jnp.int32, (8, LANES), 1)
    wide_lane = lax.broadcasted_iota(jnp.int32, (runs, LANES), 1)
    sums_ref[...] = jnp.zeros_like(sums_ref)
    for t in range(tmpl_local):
        for r in range(runs):
            start = start_ref[t, r]
            row = start // LANES
            shift = start % LANES
            held = buf_ref[pl.ds(2 * row, 8), :]
            turned = pltpu.roll(held, LANES - shift, 1)
            below = pltpu.roll(turned, 6, 0)
            seg[8 * r : 8 * r + 8, :] = jnp.where(lane < LANES - shift, turned, below)
        grid_to_time(code_ref, (t,), code_t, ())
        for w in range(2):
            grid_to_time(ant_ref, (t, w), ant_t, (w,))
        wa = ant_t[0]
        wb = ant_t[1]
        for k, product in enumerate((wa * wa, wb * wb, wa * wb)):
            sums_ref[3 * t + k : 3 * t + k + 1, :] = jnp.sum(product, axis=0, keepdims=True)
        taps = []
        for c in range(2):
            lines = [seg[pl.ds(2 * r + c, runs, stride=8), :] for r in range(3)]
            moved = [lines] + [
                [pltpu.roll(line, LANES - k, 1) for line in lines] for k in range(1, 4)
            ]
            taps.append(moved)
        for r in range(2):
            code = code_t[pl.ds(r, runs, stride=2), :]
            fraction = (code & (NFRAC - 1)).astype(jnp.float32) * (1.0 / NFRAC)
            coeffs = lagrange(fraction)
            wts = [ant_t[w, pl.ds(r, runs, stride=2), :] for w in range(2)]
            for c in range(2):
                moved = taps[c]
                total = coeffs[0] * moved[0][r]
                for k in range(1, 4):
                    total = total + coeffs[k] * jnp.where(
                        wide_lane < LANES - k, moved[k][r], moved[k][r + 1]
                    )
                for w in range(2):
                    x_ref[2 * t + w, c, pl.ds(r, runs, stride=2), :] = total * wts[w]


def bit_reverse(index, bits):
    out = 0
    for k in range(bits):
        out = out + ((index // (1 << k)) % 2) * (1 << (bits - 1 - k))
    return out


def spectrum_kernel(
    band_size,
    bits,
    sample_total,
    fact_ref,
    x_ref,
    sums_ref,
    left_ref,
    twid_ref,
    right_hi_ref,
    right_lo_ref,
    out_ref,
    cur,
    got,
    cur_sums,
    got_sums,
    stat,
    stat_got,
    send_sem,
    recv_sem,
    last_send,
    last_recv,
):
    chunks = x_ref.shape[0]
    tmpl_local = chunks // 2
    me = lax.axis_index("tm") * band_size + lax.axis_index("band")

    def place(rank):
        return {"tm": rank // band_size, "band": rank % band_size}

    home = bit_reverse(me, bits)
    partners = []
    for st in range(bits):
        half = 1 << (bits - 1 - st)
        partners.append(me + half - 2 * half * ((me // half) % 2))
    barrier = pltpu.get_barrier_semaphore()
    for partner in partners:
        pl.semaphore_signal(barrier, inc=1, device_id=place(partner), device_id_type=MESH)

    @pl.when(home != me)
    def _():
        pl.semaphore_signal(barrier, inc=1, device_id=place(home), device_id_type=MESH)
        pl.semaphore_wait(barrier, bits + 1)

    @pl.when(home == me)
    def _():
        pl.semaphore_wait(barrier, bits)

    def data_copy(st, ch):
        return pltpu.make_async_remote_copy(
            src_ref=x_ref.at[ch] if st == 0 else cur.at[st - 1, ch],
            dst_ref=got.at[st, ch],
            send_sem=send_sem.at[st, ch],
            recv_sem=recv_sem.at[st, ch],
            device_id=place(partners[st]),
            device_id_type=MESH,
        )

    def sums_copy(st):
        return pltpu.make_async_remote_copy(
            src_ref=sums_ref if st == 0 else cur_sums.at[st - 1],
            dst_ref=got_sums.at[st],
            send_sem=send_sem.at[st, chunks],
            recv_sem=recv_sem.at[st, chunks],
            device_id=place(partners[st]),
            device_id_type=MESH,
        )

    copies = {}
    for ch in range(chunks):
        copies[0, ch] = data_copy(0, ch)
        copies[0, ch].start()
    sums_copies = [sums_copy(0)]
    sums_copies[0].start()
    left = split2(left_ref[...])
    spectra = {}
    norm = 1.0 / math.sqrt(sample_total)

    def transform(ch):
        value = cur[bits - 1, ch].reshape(2 * NQ, LANES)
        mixed = dot3(left, split2(value))
        real, imag = mixed[:NQ], mixed[NQ:]
        cos_part, sin_part = twid_ref[0], twid_ref[1]
        line = jnp.concatenate(
            [real * cos_part - imag * sin_part, real * sin_part + imag * cos_part], axis=1
        )
        out = dot3(split2(line), (right_hi_ref[...], right_lo_ref[...])) * norm
        spectra[ch] = (out[:, :LANES], out[:, LANES:])

    totals = []
    last = []

    def last_copy(t):
        return pltpu.make_async_remote_copy(
            src_ref=stat.at[t],
            dst_ref=stat_got.at[t],
            send_sem=last_send.at[t],
            recv_sem=last_recv.at[t],
            device_id=place(home),
            device_id_type=MESH,
        )

    def statistic(t):
        if not totals:
            for st in range(bits):
                sums_copies[st].wait()
                before = sums_ref[...] if st == 0 else cur_sums[st - 1]
                cur_sums[st] = before + got_sums[st]
                if st + 1 < bits:
                    sums_copies.append(sums_copy(st + 1))
                    sums_copies[st + 1].start()
            totals.append(jnp.sum(cur_sums[bits - 1], axis=1, keepdims=True) / sample_total)
        total = totals[0]
        power_a = total[3 * t : 3 * t + 1] + stat_eps
        power_b = total[3 * t + 1 : 3 * t + 2] + stat_eps
        cross_ab = total[3 * t + 2 : 3 * t + 3]
        det = jnp.maximum(
            power_a * power_b - cross_ab * cross_ab, floor_share * power_a * power_b
        )
        (a_real, a_imag), (b_real, b_imag) = spectra[2 * t], spectra[2 * t + 1]
        value = (
            power_b * (a_real * a_real + a_imag * a_imag)
            + power_a * (b_real * b_real + b_imag * b_imag)
            - 2.0 * cross_ab * (a_real * b_real + a_imag * b_imag)
        ) / det
        per = NQ // SFT_DEV
        blocks = swap_blocks([value[i * per : (i + 1) * per] for i in range(SFT_DEV)])
        for j, block in enumerate(blocks):
            stat[t, j * per : (j + 1) * per, :] = block

        @pl.when(home != me)
        def _():
            last_copy(t).start()

        @pl.when(home == me)
        def _():
            out_ref[t] = stat[t]

    order = sorted(
        ((st, ch) for st in range(bits) for ch in range(chunks)), key=lambda p: (p[0] + p[1], p[0])
    )
    for st, ch in order:
        copies[st, ch].wait_recv()
        own = x_ref[ch] if st == 0 else cur[st - 1, ch]
        other = got[st, ch]
        base = (me * bits + st) * 3
        sign, w_real, w_imag = (fact_ref[base + k] for k in range(3))
        mixed = sign * own + other
        cur[st, ch, 0] = mixed[0] * w_real - mixed[1] * w_imag
        cur[st, ch, 1] = mixed[0] * w_imag + mixed[1] * w_real
        if st + 1 < bits:
            copies[st + 1, ch] = data_copy(st + 1, ch)
            copies[st + 1, ch].start()
        else:
            transform(ch)
            if ch % 2:
                statistic(ch // 2)

    for t in range(tmpl_local):

        @pl.when(home != me)
        def _():
            last_copy(t).wait()
            out_ref[t] = stat_got[t]

    for copy in copies.values():
        copy.wait_send()


def butterfly_factors(owners, bits):
    table = np.zeros((owners, bits, 3), np.float32)
    for i in range(owners):
        for st in range(bits):
            half = owners >> (st + 1)
            upper = (i // half) % 2
            angle = -2.0 * math.pi * (i % half) / (2 * half) if upper else 0.0
            table[i, st] = (-1.0 if upper else 1.0, math.cos(angle), math.sin(angle))
    return table.reshape(-1)


def per_device(sft_bins, delay_code, antenna):
    band_size = lax.axis_size("band")
    owners = lax.axis_size("tm") * band_size
    bits = owners.bit_length() - 1
    sample_total = SFT_DEV * owners * NB
    me = lax.axis_index("tm") * band_size + lax.axis_index("band")
    spectra = lax.all_to_all(sft_bins, "band", split_axis=1, concat_axis=2, tiled=True)
    bin_grid = spectra.reshape(2, SFT_DEV, NP, NQ)
    section_one = complex_einsum("pk,skl->spl", dft_table(NP, 1.0), (bin_grid[0], bin_grid[1]))
    p_rows = lax.broadcasted_iota(jnp.int32, (NP, NQ), 0)
    l_cols = lax.broadcasted_iota(jnp.int32, (NP, NQ), 1)
    section_one = rotate(section_one, phase_pair(p_rows * l_cols, NB, 1.0))
    series_pair = complex_einsum("spl,lq->spq", section_one, dft_table(NQ, 1.0))
    norm_scale = 1.0 / math.sqrt(NB)
    stacked = jnp.stack([series_pair[0] * norm_scale, series_pair[1] * norm_scale])
    rim_cols = 72
    head_rim = stacked[:, 0, :, :rim_cols]
    tail_rim = stacked[:, SFT_DEV - 1, :, NQ - rim_cols :]
    after_rim = shifted(head_rim, ("tm", "band"), -1)
    before = shifted(tail_rim, ("tm", "band"), 1)
    rim_size = NP * rim_cols
    span_len = SFT_DEV * NB
    timed = stacked.transpose(0, 1, 3, 2).reshape(2, span_len)
    before_timed = before.transpose(0, 2, 1).reshape(2, rim_size)
    after_timed = after_rim.transpose(0, 2, 1).reshape(2, rim_size)
    buffer = jnp.concatenate([before_timed, timed, after_timed], axis=1)
    buffer = buffer.reshape(2, -1, LANES).transpose(1, 0, 2).reshape(-1, LANES)
    tmpl_local = delay_code.shape[0]
    run_count = span_len // RUN
    run_cols = RUN // NP
    offsets = delay_code[:, ::run_cols, ::NP].transpose(0, 2, 1).reshape(tmpl_local, run_count)
    offsets = offsets // NFRAC - MAXD
    starts = (jnp.arange(run_count, dtype=jnp.int32) * RUN)[None, :] + offsets + (rim_size - 1)

    vmem = pl.BlockSpec(memory_space=pltpu.VMEM)
    smem = pl.BlockSpec(memory_space=pltpu.SMEM)
    planes = (2 * tmpl_local, 2, NQ, LANES)
    x, sums = pl.pallas_call(
        resample_kernel,
        out_shape=(
            jax.ShapeDtypeStruct(planes, jnp.float32),
            jax.ShapeDtypeStruct((8, LANES), jnp.float32),
        ),
        in_specs=[smem, vmem, vmem, vmem],
        out_specs=(vmem, vmem),
        scratch_shapes=[
            pltpu.VMEM((NQ, LANES), jnp.int32),
            pltpu.VMEM((2, NQ, LANES), jnp.float32),
            pltpu.VMEM((8 * run_count, LANES), jnp.float32),
        ],
        compiler_params=pltpu.CompilerParams(vmem_limit_bytes=32 * 1024 * 1024),
    )(starts, buffer, delay_code, antenna)

    home = bit_reverse(me, bits)
    per = NQ // SFT_DEV
    row_at = lax.broadcasted_iota(jnp.int32, (NQ, LANES), 0)
    col_at = lax.broadcasted_iota(jnp.int32, (NQ, LANES), 1)
    coarse = (row_at // per + SFT_DEV * (row_at % per)) * owners + home
    cos_left, sin_left = phase_pair(coarse * col_at, NQ * owners, -1.0)
    left = jnp.concatenate(
        [
            jnp.concatenate([cos_left, -sin_left], axis=1),
            jnp.concatenate([sin_left, cos_left], axis=1),
        ],
        axis=0,
    )
    twid = jnp.stack(phase_pair(coarse * col_at, sample_total, -1.0))
    col = np.arange(LANES)
    fine = col // NP + SFT_DEV * (col % NP)
    angles = -2.0 * np.pi / LANES * ((np.arange(LANES)[:, None] * fine[None, :]) % LANES)
    right = np.block([[np.cos(angles), np.sin(angles)], [-np.sin(angles), np.cos(angles)]])
    right_hi = right.astype(ml_dtypes.bfloat16)
    right_lo = (right - right_hi.astype(np.float64)).astype(ml_dtypes.bfloat16)
    out = pl.pallas_call(
        functools.partial(spectrum_kernel, band_size, bits, sample_total),
        out_shape=jax.ShapeDtypeStruct((tmpl_local, NQ, LANES), jnp.float32),
        in_specs=[smem] + [vmem] * 6,
        out_specs=vmem,
        scratch_shapes=[
            pltpu.VMEM((bits,) + planes, jnp.float32),
            pltpu.VMEM((bits,) + planes, jnp.float32),
            pltpu.VMEM((bits, 8, LANES), jnp.float32),
            pltpu.VMEM((bits, 8, LANES), jnp.float32),
            pltpu.VMEM((tmpl_local, NQ, LANES), jnp.float32),
            pltpu.VMEM((tmpl_local, NQ, LANES), jnp.float32),
            pltpu.SemaphoreType.DMA((bits, planes[0] + 1)),
            pltpu.SemaphoreType.DMA((bits, planes[0] + 1)),
            pltpu.SemaphoreType.DMA((tmpl_local,)),
            pltpu.SemaphoreType.DMA((tmpl_local,)),
        ],
        compiler_params=pltpu.CompilerParams(
            collective_id=0, has_side_effects=True, vmem_limit_bytes=40 * 1024 * 1024
        ),
    )(
        jnp.asarray(butterfly_factors(owners, bits)),
        x,
        sums,
        left,
        twid,
        jnp.asarray(right_hi),
        jnp.asarray(right_lo),
    )
    return out[:, :, None, :]


def solution(mesh):
    in_specs = (
        P(None, ("groups", "tm"), "band"),
        P(("groups", "tmpl"), None, ("tm", "band")),
        P(("groups", "tmpl"), None, None, ("tm", "band")),
    )
    out_specs = P(("groups", "tmpl"), None, ("tm", "band"), None)
    return jax.shard_map(
        per_device, mesh=mesh, in_specs=in_specs, out_specs=out_specs, check_vma=False
    )
```

```python
import functools
import math

import jax
import jax.numpy as jnp
import ml_dtypes
import numpy as np
from jax import lax
from jax.experimental import pallas as pl
from jax.experimental.pallas import tpu as pltpu
from jax.sharding import PartitionSpec as P

NB = 2048
NQ = 128
NP = 16
SFT_DEV = 8
MAXD = 1000
NFRAC = 8
RUN = 256
LANES = 128

stat_eps = 1e-06
floor_share = 0.5
MESH = pl.DeviceIdType.MESH


def lagrange(fraction):
    return (
        -fraction * (fraction - 1.0) * (fraction - 2.0) / 6.0,
        (fraction + 1.0) * (fraction - 1.0) * (fraction - 2.0) / 2.0,
        -(fraction + 1.0) * fraction * (fraction - 2.0) / 2.0,
        (fraction + 1.0) * fraction * (fraction - 1.0) / 6.0,
    )


def phase_pair(product, modulus, direction):
    angles = direction * 2.0 * math.pi / modulus * (product % modulus).astype(jnp.float32)
    return (jnp.cos(angles), jnp.sin(angles))


def split2(value):
    high = value.astype(jnp.bfloat16)
    return high, (value - high.astype(jnp.float32)).astype(jnp.bfloat16)


def dot3(lhs, rhs):
    lhs_hi, lhs_lo = lhs
    rhs_hi, rhs_lo = rhs
    dot = functools.partial(jnp.dot, preferred_element_type=jnp.float32)
    return dot(lhs_hi, rhs_hi) + (dot(lhs_hi, rhs_lo) + dot(lhs_lo, rhs_hi))


def swap_blocks(blocks):
    count = len(blocks)
    width = LANES // count
    blocks = list(blocks)
    lane_block = lax.broadcasted_iota(jnp.int32, blocks[0].shape, 1) // width
    half = count // 2
    while half:
        keep = (lane_block & half) == 0
        for i in range(count):
            if i & half == 0:
                low, high = blocks[i], blocks[i + half]
                blocks[i] = jnp.where(keep, low, pltpu.roll(high, half * width, 1))
                blocks[i + half] = jnp.where(
                    keep, pltpu.roll(low, LANES - half * width, 1), high
                )
        half //= 2
    return blocks


def grid_to_time(plane):
    return jnp.concatenate(swap_blocks([plane(i) for i in range(SFT_DEV)]), axis=0)


def owner_dft(real, imag):
    count = len(real)
    if count == 1:
        return real, imag
    half = count // 2
    sum_real = [real[k] + real[k + half] for k in range(half)]
    sum_imag = [imag[k] + imag[k + half] for k in range(half)]
    dif_real, dif_imag = [], []
    for k in range(half):
        d_real, d_imag = real[k] - real[k + half], imag[k] - imag[k + half]
        if k == 0:
            dif_real.append(d_real)
            dif_imag.append(d_imag)
        elif 2 * k == half:
            dif_real.append(d_imag)
            dif_imag.append(-d_real)
        else:
            cos_part = math.cos(2.0 * math.pi * k / count)
            sin_part = math.sin(2.0 * math.pi * k / count)
            dif_real.append(d_real * cos_part + d_imag * sin_part)
            dif_imag.append(d_imag * cos_part - d_real * sin_part)
    even = owner_dft(sum_real, sum_imag)
    odd = owner_dft(dif_real, dif_imag)
    out_real, out_imag = [], []
    for k in range(half):
        out_real += [even[0][k], odd[0][k]]
        out_imag += [even[1][k], odd[1][k]]
    return out_real, out_imag


def search_kernel(
    band_size,
    owners,
    sample_total,
    start_ref,
    bins_ref,
    code_ref,
    ant_ref,
    bins_hi_ref,
    bins_lo_ref,
    bins_twid_ref,
    cols_hi_ref,
    cols_lo_ref,
    left_ref,
    twid_ref,
    right_hi_ref,
    right_lo_ref,
    out_ref,
    grid,
    edge,
    halo,
    buf,
    seg,
    code_t,
    line,
    w_out,
    w_got,
    r_out,
    r_got,
    z_out,
    z_got,
    sums,
    sums_got,
    bin_send,
    bin_recv,
    edge_send,
    edge_recv,
    w_send,
    w_recv,
    s_send,
    s_recv,
    r_send,
    r_recv,
    z_send,
    z_recv,
):
    tmpl_local, grid_rows = code_ref.shape[:2]
    runs = start_ref.shape[1]
    pieces = edge.shape[3]
    per = NQ // SFT_DEV
    block_rows = NQ // owners
    my_tm = lax.axis_index("tm")
    my_band = lax.axis_index("band")
    me = my_tm * band_size + my_band

    def place(rank):
        return {"tm": rank // band_size, "band": rank % band_size}

    def peers(body):
        def step(d, carry):
            body((me + d) % owners)
            return carry

        lax.fori_loop(1, owners, step, 0, unroll=owners <= 8)

    def remote(src, dst, send, recv, rank):
        return pltpu.make_async_remote_copy(
            src_ref=src,
            dst_ref=dst,
            send_sem=send,
            recv_sem=recv,
            device_id=place(rank),
            device_id_type=MESH,
        )

    barrier = pltpu.get_barrier_semaphore()
    peers(
        lambda rank: pl.semaphore_signal(
            barrier, inc=1, device_id=place(rank), device_id_type=MESH
        )
    )

    for e in range(band_size):
        for side in range(2):
            row = SFT_DEV * e + (SFT_DEV - 1 if side == 0 else 0)
            for c in range(2):
                for k in range(pieces):
                    edge[e, side, c, k : k + 1, :] = bins_ref[
                        c, row : row + 1, k * LANES : (k + 1) * LANES
                    ]

    @pl.when(me == 0)
    def _():
        halo[0] = jnp.zeros(halo.shape[1:], jnp.float32)

    @pl.when(me == owners - 1)
    def _():
        halo[1] = jnp.zeros(halo.shape[1:], jnp.float32)

    pl.semaphore_wait(barrier, owners - 1)

    def bins_rows(band):
        return pl.ds(pl.multiple_of(SFT_DEV * band, SFT_DEV), SFT_DEV)

    def bins_copy(d):
        band = (my_band + d) % band_size
        return remote(
            bins_ref.at[:, bins_rows(band), :],
            grid.at[my_band],
            bin_send.at[band],
            bin_recv.at[my_band],
            my_tm * band_size + band,
        )

    def bins_arrival(d):
        band = (my_band + d) % band_size
        return remote(
            bins_ref.at[:, bins_rows(band), :],
            grid.at[band],
            bin_send.at[band],
            bin_recv.at[band],
            my_tm * band_size + band,
        )

    for d in range(1, band_size):
        bins_copy(d).start()

    def edge_target(e, side):
        return my_tm * band_size + e + (1 if side == 0 else -1)

    def edge_copy(e, side):
        return remote(
            edge.at[e, side],
            halo.at[side, my_band],
            edge_send.at[e, side],
            edge_recv.at[side, my_band],
            edge_target(e, side),
        )

    def edge_is_sent(e, side):
        rank = edge_target(e, side)
        return jnp.logical_and(rank != me, jnp.logical_and(rank >= 0, rank < owners))

    for e in range(band_size):
        for side in range(2):

            @pl.when(edge_is_sent(e, side))
            def _():
                edge_copy(e, side).start()

            @pl.when(edge_target(e, side) == me)
            def _():
                halo[side, my_band] = edge[e, side]

    grid[my_band] = bins_ref[:, bins_rows(my_band), :]

    def blocked(value):
        return value.reshape(owners, block_rows, LANES)

    sums[...] = jnp.zeros_like(sums)
    for t in range(tmpl_local):
        wts = []
        for w in range(2):
            value = grid_to_time(lambda i: ant_ref[t, w, pl.ds(i, per, stride=SFT_DEV), :])
            w_out[t, :, w] = blocked(value)
            wts.append(value)
        wa, wb = wts
        for k, product in enumerate((wa * wa, wb * wb, wa * wb)):
            sums[3 * t + k : 3 * t + k + 1, :] = jnp.sum(product, axis=0, keepdims=True)

        def send_w(rank):
            remote(
                w_out.at[t, rank], w_got.at[t, me], w_send.at[t, rank], w_recv.at[t, me], rank
            ).start()

        peers(send_w)
        w_got[t, me] = w_out[t, me]

    peers(
        lambda rank: remote(
            sums, sums_got.at[me], s_send.at[rank], s_recv.at[me], rank
        ).start()
    )
    sums_got[me] = sums[...]

    for t in range(tmpl_local):
        code_t[t] = grid_to_time(lambda i: code_ref[t, pl.ds(i, per, stride=SFT_DEV), :])

    for d in range(1, band_size):
        bins_arrival(d).wait_recv()
    for side in range(2):
        source = (me - 1 if side == 0 else me + 1) // band_size

        @pl.when(jnp.logical_and(me > 0 if side == 0 else me < owners - 1, source != my_tm))
        def _():
            for band in range(band_size):
                remote(
                    edge.at[0, side],
                    halo.at[side, band],
                    edge_send.at[0, side],
                    edge_recv.at[side, band],
                    source * band_size + band,
                ).wait_recv()

        @pl.when(jnp.logical_and(me > 0 if side == 0 else me < owners - 1, source == my_tm))
        def _():
            for d in range(1, band_size):
                band = (my_band + d) % band_size
                remote(
                    edge.at[0, side],
                    halo.at[side, band],
                    edge_send.at[0, side],
                    edge_recv.at[side, band],
                    my_tm * band_size + band,
                ).wait_recv()

    sub = lax.broadcasted_iota(jnp.int32, (SFT_DEV, LANES), 0)
    main_rows, rim_rows = [], []
    for c in range(2):
        for band in range(band_size):
            for k in range(pieces):
                main_rows.append(grid[band, c, :, k * LANES : (k + 1) * LANES])
                first = jnp.broadcast_to(halo[1, band, c, k : k + 1, :], (SFT_DEV, LANES))
                final = jnp.broadcast_to(halo[0, band, c, k : k + 1, :], (SFT_DEV, LANES))
                rim_rows.append(
                    jnp.where(sub == 0, first, jnp.where(sub == SFT_DEV - 1, final, 0.0))
                )
    turned = jnp.concatenate(
        [
            jnp.transpose(jnp.concatenate(main_rows, axis=0)),
            jnp.transpose(jnp.concatenate(rim_rows, axis=0)),
        ],
        axis=0,
    )
    mixed = dot3(split2(turned), (bins_hi_ref[...], bins_lo_ref[...]))
    halves = []
    for h in range(2):
        real = mixed[h * LANES : (h + 1) * LANES, :LANES]
        imag = mixed[h * LANES : (h + 1) * LANES, LANES:]
        cos_part, sin_part = bins_twid_ref[0], bins_twid_ref[1]
        halves.append(
            jnp.concatenate(
                [real * cos_part - imag * sin_part, real * sin_part + imag * cos_part], axis=0
            )
        )
    series = dot3(
        (cols_hi_ref[...], cols_lo_ref[...]), split2(jnp.concatenate(halves, axis=1))
    )
    for c in range(2):
        for h in range(2):
            part = series[c * NQ : (c + 1) * NQ, h * LANES : (h + 1) * LANES]
            blocks = swap_blocks([part[i * per : (i + 1) * per] for i in range(SFT_DEV)])
            if h == 0:
                for s in range(SFT_DEV):
                    buf[pl.ds(2 * per * (s + 1) + c, per, stride=2), :] = blocks[s]
            else:
                buf[pl.ds(c, per, stride=2), :] = blocks[SFT_DEV - 1]
                buf[pl.ds(2 * per * (SFT_DEV + 1) + c, per, stride=2), :] = blocks[0]

    lane = lax.broadcasted_iota(jnp.int32, (8, LANES), 1)
    wide_lane = lax.broadcasted_iota(jnp.int32, (runs, LANES), 1)
    for t in range(tmpl_local):
        for r in range(runs):
            start = start_ref[t, r]
            shift = start & (LANES - 1)
            held = buf[pl.ds(2 * (start >> 7), 8), :]
            rolled = pltpu.roll(held, LANES - shift, 1)
            below = pltpu.roll(rolled, 6, 0)
            seg[8 * r : 8 * r + 8, :] = jnp.where(lane < LANES - shift, rolled, below)
        taps = []
        for c in range(2):
            lines = [seg[pl.ds(2 * r + c, runs, stride=8), :] for r in range(3)]
            moved = [lines] + [
                [pltpu.roll(item, LANES - k, 1) for item in lines] for k in range(1, 4)
            ]
            taps.append(moved)
        for r in range(2):
            code = code_t[t, pl.ds(r, runs, stride=2), :]
            fraction = (code & (NFRAC - 1)).astype(jnp.float32) * (1.0 / NFRAC)
            coeffs = lagrange(fraction)
            for c in range(2):
                moved = taps[c]
                total = coeffs[0] * moved[0][r]
                for k in range(1, 4):
                    total = total + coeffs[k] * jnp.where(
                        wide_lane < LANES - k, moved[k][r], moved[k][r + 1]
                    )
                line[c, pl.ds(r, runs, stride=2), :] = total
        for c in range(2):
            r_out[t, :, c] = blocked(line[c])

        def send_r(rank):
            remote(
                r_out.at[t, rank], r_got.at[t, me], r_send.at[t, rank], r_recv.at[t, me], rank
            ).start()

        peers(send_r)
        r_got[t, me] = r_out[t, me]

    def arrival(out, got, send, recv, t, rank):
        return remote(out.at[t, rank], got.at[t, rank], send.at[t, rank], recv.at[t, rank], rank)

    for t in range(tmpl_local):
        peers(lambda rank: arrival(w_out, w_got, w_send, w_recv, t, rank).wait())
        peers(lambda rank: arrival(r_out, r_got, r_send, r_recv, t, rank).wait())
        for w in range(2):
            real = [r_got[t, i, 0] * w_got[t, i, w] for i in range(owners)]
            imag = [r_got[t, i, 1] * w_got[t, i, w] for i in range(owners)]
            real, imag = owner_dft(real, imag)
            for i in range(owners):
                z_out[t, i, 2 * w] = real[i]
                z_out[t, i, 2 * w + 1] = imag[i]

        def send_z(rank):
            remote(
                z_out.at[t, rank], z_got.at[t, me], z_send.at[t, rank], z_recv.at[t, me], rank
            ).start()

        peers(send_z)
        z_got[t, me] = z_out[t, me]

    def sums_arrival(rank):
        remote(sums, sums_got.at[rank], s_send.at[rank], s_recv.at[rank], rank).wait()

    peers(sums_arrival)
    total = jnp.sum(sums_got[...], axis=0)
    total = jnp.sum(total, axis=1, keepdims=True) / sample_total
    left = split2(left_ref[...])
    norm = 1.0 / math.sqrt(sample_total)
    for t in range(tmpl_local):
        peers(lambda rank: arrival(z_out, z_got, z_send, z_recv, t, rank).wait())
        value = jnp.concatenate(
            [
                jnp.concatenate(
                    [z_got[t, :, 2 * w + c].reshape(NQ, LANES) for c in range(2)], axis=0
                )
                for w in range(2)
            ],
            axis=1,
        )
        mixed = dot3(left, split2(value))
        lines = []
        for w in range(2):
            real = mixed[:NQ, w * LANES : (w + 1) * LANES]
            imag = mixed[NQ:, w * LANES : (w + 1) * LANES]
            cos_part, sin_part = twid_ref[0], twid_ref[1]
            lines.append(
                jnp.concatenate(
                    [real * cos_part - imag * sin_part, real * sin_part + imag * cos_part], axis=1
                )
            )
        spectra = dot3(
            split2(jnp.concatenate(lines, axis=0)), (right_hi_ref[...], right_lo_ref[...])
        ) * norm
        a_real, a_imag = spectra[:NQ, :LANES], spectra[:NQ, LANES:]
        b_real, b_imag = spectra[NQ:, :LANES], spectra[NQ:, LANES:]
        power_a = total[3 * t : 3 * t + 1] + stat_eps
        power_b = total[3 * t + 1 : 3 * t + 2] + stat_eps
        cross_ab = total[3 * t + 2 : 3 * t + 3]
        det = jnp.maximum(
            power_a * power_b - cross_ab * cross_ab, floor_share * power_a * power_b
        )
        stat = (
            power_b * (a_real * a_real + a_imag * a_imag)
            + power_a * (b_real * b_real + b_imag * b_imag)
            - 2.0 * cross_ab * (a_real * b_real + a_imag * b_imag)
        ) / det
        blocks = swap_blocks([stat[i * per : (i + 1) * per] for i in range(SFT_DEV)])
        for j, block in enumerate(blocks):
            out_ref[t, j * per : (j + 1) * per, :] = block

    for d in range(1, band_size):
        bins_copy(d).wait_send()
    for e in range(band_size):
        for side in range(2):

            @pl.when(edge_is_sent(e, side))
            def _():
                edge_copy(e, side).wait_send()


def halves_of(table):
    high = table.astype(ml_dtypes.bfloat16)
    low = (table - high.astype(np.float64)).astype(ml_dtypes.bfloat16)
    return jnp.asarray(high), jnp.asarray(low)


def turns(product, modulus):
    angles = 2.0 * np.pi / modulus * (product % modulus)
    return np.cos(angles), np.sin(angles)


def constant_tables():
    per = NQ // SFT_DEV
    at = np.arange(LANES)
    bin_cos, bin_sin = turns(np.arange(NP)[:, None] * np.arange(NP)[None, :], NP)
    same = np.eye(SFT_DEV)
    wide = [
        np.einsum("kp,st->kstp", part, same).reshape(LANES, LANES) for part in (bin_cos, bin_sin)
    ]
    bins = np.block([[wide[0], wide[1]], [-wide[1], wide[0]]])
    bins_twid = np.stack(turns(at[:, None] * (at % NP)[None, :], NB)).astype(np.float32)
    col_order = at // per + SFT_DEV * (at % per)
    col_cos, col_sin = turns(col_order[:, None] * at[None, :], NQ)
    cols = np.block([[col_cos, -col_sin], [col_sin, col_cos]]) / math.sqrt(NB)
    fine = at // NP + SFT_DEV * (at % NP)
    fine_cos, fine_sin = turns(at[:, None] * fine[None, :], LANES)
    right = np.block([[fine_cos, -fine_sin], [fine_sin, fine_cos]])
    return halves_of(bins) + (jnp.asarray(bins_twid),) + halves_of(cols), halves_of(right)


def per_device(sft_bins, delay_code, antenna):
    band_size = lax.axis_size("band")
    owners = lax.axis_size("tm") * band_size
    sample_total = SFT_DEV * owners * NB
    me = lax.axis_index("tm") * band_size + lax.axis_index("band")
    span_len = SFT_DEV * NB
    tmpl_local = delay_code.shape[0]
    run_count = span_len // RUN
    run_cols = RUN // NP
    offsets = delay_code[:, ::run_cols, ::NP].transpose(0, 2, 1).reshape(tmpl_local, run_count)
    offsets = offsets // NFRAC - MAXD
    starts = (jnp.arange(run_count, dtype=jnp.int32) * RUN)[None, :] + offsets + (NB - 1)
    per = NQ // SFT_DEV
    row_at = lax.broadcasted_iota(jnp.int32, (NQ, LANES), 0)
    col_at = lax.broadcasted_iota(jnp.int32, (NQ, LANES), 1)
    coarse = (row_at // per + SFT_DEV * (row_at % per)) * owners + me
    cos_left, sin_left = phase_pair(coarse * col_at, NQ * owners, -1.0)
    left = jnp.concatenate(
        [
            jnp.concatenate([cos_left, -sin_left], axis=1),
            jnp.concatenate([sin_left, cos_left], axis=1),
        ],
        axis=0,
    )
    twid = jnp.stack(phase_pair(coarse * col_at, sample_total, -1.0))
    first_tables, last_tables = constant_tables()
    vmem = pl.BlockSpec(memory_space=pltpu.VMEM)
    smem = pl.BlockSpec(memory_space=pltpu.SMEM)
    bin_width = sft_bins.shape[2]
    pieces = bin_width // LANES
    block_rows = NQ // owners
    f32 = jnp.float32
    dma = pltpu.SemaphoreType.DMA
    out = pl.pallas_call(
        functools.partial(search_kernel, band_size, owners, sample_total),
        out_shape=jax.ShapeDtypeStruct((tmpl_local, NQ, LANES), f32),
        in_specs=[smem] + [vmem] * 12,
        out_specs=vmem,
        scratch_shapes=[
            pltpu.VMEM((band_size, 2, SFT_DEV, bin_width), f32),
            pltpu.VMEM((band_size, 2, 2, pieces, LANES), f32),
            pltpu.VMEM((2, band_size, 2, pieces, LANES), f32),
            pltpu.VMEM((2 * per * (SFT_DEV + 2), LANES), f32),
            pltpu.VMEM((8 * run_count, LANES), f32),
            pltpu.VMEM((tmpl_local, NQ, LANES), jnp.int32),
            pltpu.VMEM((2, NQ, LANES), f32),
        ]
        + [pltpu.VMEM((tmpl_local, owners, 2, block_rows, LANES), f32)] * 4
        + [pltpu.VMEM((tmpl_local, owners, 4, block_rows, LANES), f32)] * 2
        + [
            pltpu.VMEM((8, LANES), f32),
            pltpu.VMEM((owners, 8, LANES), f32),
            dma((band_size,)),
            dma((band_size,)),
            dma((band_size, 2)),
            dma((2, band_size)),
            dma((tmpl_local, owners)),
            dma((tmpl_local, owners)),
            dma((owners,)),
            dma((owners,)),
        ]
        + [dma((tmpl_local, owners))] * 4,
        compiler_params=pltpu.CompilerParams(
            collective_id=0, has_side_effects=True, vmem_limit_bytes=48 * 1024 * 1024
        ),
    )(starts, sft_bins, delay_code, antenna, *first_tables, left, twid, *last_tables)
    return out[:, :, None, :]


def solution(mesh):
    in_specs = (
        P(None, ("groups", "tm"), "band"),
        P(("groups", "tmpl"), None, ("tm", "band")),
        P(("groups", "tmpl"), None, None, ("tm", "band")),
    )
    out_specs = P(("groups", "tmpl"), None, ("tm", "band"), None)
    return jax.shard_map(
        per_device, mesh=mesh, in_specs=in_specs, out_specs=out_specs, check_vma=False
    )
```

```python
import functools
import math

import jax
import jax.numpy as jnp
import numpy as np
from jax import lax
from jax.experimental import pallas as pl
from jax.experimental.pallas import tpu as pltpu
from jax.sharding import PartitionSpec as P

NB = 2048
NQ = 128
NP = 16
SFT_DEV = 8
MAXD = 1000
NFRAC = 8
RUN = 256
LANES = 128

stat_eps = 1e-06
floor_share = 0.5
MESH = pl.DeviceIdType.MESH


def lagrange(fraction):
    return (
        -fraction * (fraction - 1.0) * (fraction - 2.0) / 6.0,
        (fraction + 1.0) * (fraction - 1.0) * (fraction - 2.0) / 2.0,
        -(fraction + 1.0) * fraction * (fraction - 2.0) / 2.0,
        (fraction + 1.0) * fraction * (fraction - 1.0) / 6.0,
    )


def split2(value):
    high = value.astype(jnp.bfloat16)
    return high, (value - high.astype(jnp.float32)).astype(jnp.bfloat16)


def dot3(lhs, rhs):
    lhs_hi, lhs_lo = lhs
    rhs_hi, rhs_lo = rhs
    dot = functools.partial(jnp.dot, preferred_element_type=jnp.float32)
    return dot(lhs_hi, rhs_hi) + (dot(lhs_hi, rhs_lo) + dot(lhs_lo, rhs_hi))


def swap_blocks(blocks):
    count = len(blocks)
    width = LANES // count
    blocks = list(blocks)
    lane_block = lax.broadcasted_iota(jnp.int32, blocks[0].shape, 1) // width
    half = count // 2
    while half:
        keep = (lane_block & half) == 0
        for i in range(count):
            if i & half == 0:
                low, high = blocks[i], blocks[i + half]
                blocks[i] = jnp.where(keep, low, pltpu.roll(high, half * width, 1))
                blocks[i + half] = jnp.where(
                    keep, pltpu.roll(low, LANES - half * width, 1), high
                )
        half //= 2
    return blocks


def grid_to_time(plane):
    return jnp.concatenate(swap_blocks([plane(i) for i in range(SFT_DEV)]), axis=0)


def owner_dft(real, imag):
    count = len(real)
    if count == 1:
        return real, imag
    half = count // 2
    sum_real = [real[k] + real[k + half] for k in range(half)]
    sum_imag = [imag[k] + imag[k + half] for k in range(half)]
    dif_real, dif_imag = [], []
    for k in range(half):
        d_real, d_imag = real[k] - real[k + half], imag[k] - imag[k + half]
        if k == 0:
            dif_real.append(d_real)
            dif_imag.append(d_imag)
        elif 2 * k == half:
            dif_real.append(d_imag)
            dif_imag.append(-d_real)
        else:
            cos_part = math.cos(2.0 * math.pi * k / count)
            sin_part = math.sin(2.0 * math.pi * k / count)
            dif_real.append(d_real * cos_part + d_imag * sin_part)
            dif_imag.append(d_imag * cos_part - d_real * sin_part)
    even = owner_dft(sum_real, sum_imag)
    odd = owner_dft(dif_real, dif_imag)
    out_real, out_imag = [], []
    for k in range(half):
        out_real += [even[0][k], odd[0][k]]
        out_imag += [even[1][k], odd[1][k]]
    return out_real, out_imag


def search_kernel(
    band_size,
    owners,
    sample_total,
    far_refs,
    out_ref,
    near_refs,
    start_ref,
    left_hi,
    left_lo,
    right_hi,
    right_lo,
    twid,
    grid,
    edge,
    halo,
    buf,
    seg,
    code_t,
    line,
    w_out,
    w_got,
    r_out,
    r_got,
    z_out,
    z_got,
    sums,
    sums_got,
    bin_send,
    bin_recv,
    edge_send,
    edge_recv,
    w_send,
    w_recv,
    s_send,
    s_recv,
    r_send,
    r_recv,
    z_send,
    z_recv,
    load_sem,
    start_sem,
):
    loads = [
        pltpu.make_async_copy(far, near, load_sem.at[k])
        for k, (far, near) in enumerate(zip(far_refs, near_refs))
    ]
    for load in loads:
        load.start()
    (
        bins_ref,
        ant_ref,
        code_ref,
        bins_table_ref,
        bins_twid_ref,
        cols_table_ref,
        left_ref,
        twid_ref,
        right_table_ref,
    ) = near_refs
    tmpl_local, run_rows, run_cols, _ = code_ref.shape
    starts_load = pltpu.make_async_copy(far_refs[2].at[:, :, 0, :], start_ref, start_sem)
    starts_load.start()
    runs = SFT_DEV * run_rows
    code_flat = code_ref.reshape(tmpl_local, NQ, LANES)
    pieces = edge.shape[3]
    per = NQ // SFT_DEV
    block_rows = NQ // owners
    my_tm = lax.axis_index("tm")
    my_band = lax.axis_index("band")
    me = my_tm * band_size + my_band

    def place(rank):
        return {"tm": rank // band_size, "band": rank % band_size}

    def peers(body):
        def step(d, carry):
            body((me + d) % owners)
            return carry

        lax.fori_loop(1, owners, step, 0, unroll=owners <= 8)

    def remote(src, dst, send, recv, rank):
        return pltpu.make_async_remote_copy(
            src_ref=src,
            dst_ref=dst,
            send_sem=send,
            recv_sem=recv,
            device_id=place(rank),
            device_id_type=MESH,
        )

    barrier = pltpu.get_barrier_semaphore()
    peers(
        lambda rank: pl.semaphore_signal(
            barrier, inc=1, device_id=place(rank), device_id_type=MESH
        )
    )

    loads[0].wait()
    for e in range(band_size):
        for side in range(2):
            row = SFT_DEV * e + (SFT_DEV - 1 if side == 0 else 0)
            for c in range(2):
                for k in range(pieces):
                    edge[e, side, c, k : k + 1, :] = bins_ref[
                        c, row : row + 1, k * LANES : (k + 1) * LANES
                    ]

    @pl.when(me == 0)
    def _():
        halo[0] = jnp.zeros(halo.shape[1:], jnp.float32)

    @pl.when(me == owners - 1)
    def _():
        halo[1] = jnp.zeros(halo.shape[1:], jnp.float32)

    pl.semaphore_wait(barrier, owners - 1)

    def bins_rows(band):
        return pl.ds(pl.multiple_of(SFT_DEV * band, SFT_DEV), SFT_DEV)

    def bins_copy(d):
        band = (my_band + d) % band_size
        return remote(
            bins_ref.at[:, bins_rows(band), :],
            grid.at[my_band],
            bin_send.at[band],
            bin_recv.at[my_band],
            my_tm * band_size + band,
        )

    def bins_arrival(d):
        band = (my_band + d) % band_size
        return remote(
            bins_ref.at[:, bins_rows(band), :],
            grid.at[band],
            bin_send.at[band],
            bin_recv.at[band],
            my_tm * band_size + band,
        )

    for d in range(1, band_size):
        bins_copy(d).start()

    def edge_target(e, side):
        return my_tm * band_size + e + (1 if side == 0 else -1)

    def edge_copy(e, side):
        return remote(
            edge.at[e, side],
            halo.at[side, my_band],
            edge_send.at[e, side],
            edge_recv.at[side, my_band],
            edge_target(e, side),
        )

    def edge_is_sent(e, side):
        rank = edge_target(e, side)
        return jnp.logical_and(rank != me, jnp.logical_and(rank >= 0, rank < owners))

    for e in range(band_size):
        for side in range(2):

            @pl.when(edge_is_sent(e, side))
            def _():
                edge_copy(e, side).start()

            @pl.when(edge_target(e, side) == me)
            def _():
                halo[side, my_band] = edge[e, side]

    grid[my_band] = bins_ref[:, bins_rows(my_band), :]

    def blocked(value):
        return value.reshape(owners, block_rows, LANES)

    sums[...] = jnp.zeros_like(sums)
    loads[1].wait()
    for t in range(tmpl_local):
        wts = []
        for w in range(2):
            value = grid_to_time(lambda i: ant_ref[t, w, pl.ds(i, per, stride=SFT_DEV), :])
            w_out[t, :, w] = blocked(value)
            wts.append(value)
        wa, wb = wts
        for k, product in enumerate((wa * wa, wb * wb, wa * wb)):
            sums[3 * t + k : 3 * t + k + 1, :] = jnp.sum(product, axis=0, keepdims=True)

        def send_w(rank):
            remote(
                w_out.at[t, rank], w_got.at[t, me], w_send.at[t, rank], w_recv.at[t, me], rank
            ).start()

        peers(send_w)
        w_got[t, me] = w_out[t, me]

    peers(
        lambda rank: remote(
            sums, sums_got.at[me], s_send.at[rank], s_recv.at[me], rank
        ).start()
    )
    sums_got[me] = sums[...]

    loads[2].wait()
    for t in range(tmpl_local):
        code_t[t] = grid_to_time(lambda i: code_flat[t, pl.ds(i, per, stride=SFT_DEV), :])
    starts_load.wait()
    for load in loads[3:]:
        load.wait()

    for d in range(1, band_size):
        bins_arrival(d).wait_recv()
    for side in range(2):
        source = (me - 1 if side == 0 else me + 1) // band_size

        @pl.when(jnp.logical_and(me > 0 if side == 0 else me < owners - 1, source != my_tm))
        def _():
            for band in range(band_size):
                remote(
                    edge.at[0, side],
                    halo.at[side, band],
                    edge_send.at[0, side],
                    edge_recv.at[side, band],
                    source * band_size + band,
                ).wait_recv()

        @pl.when(jnp.logical_and(me > 0 if side == 0 else me < owners - 1, source == my_tm))
        def _():
            for d in range(1, band_size):
                band = (my_band + d) % band_size
                remote(
                    edge.at[0, side],
                    halo.at[side, band],
                    edge_send.at[0, side],
                    edge_recv.at[side, band],
                    my_tm * band_size + band,
                ).wait_recv()

    sub = lax.broadcasted_iota(jnp.int32, (SFT_DEV, LANES), 0)
    main_rows, rim_rows = [], []
    for c in range(2):
        for band in range(band_size):
            for k in range(pieces):
                main_rows.append(grid[band, c, :, k * LANES : (k + 1) * LANES])
                first = jnp.broadcast_to(halo[1, band, c, k : k + 1, :], (SFT_DEV, LANES))
                final = jnp.broadcast_to(halo[0, band, c, k : k + 1, :], (SFT_DEV, LANES))
                rim_rows.append(
                    jnp.where(sub == 0, first, jnp.where(sub == SFT_DEV - 1, final, 0.0))
                )
    turned = jnp.concatenate(
        [
            jnp.transpose(jnp.concatenate(main_rows, axis=0)),
            jnp.transpose(jnp.concatenate(rim_rows, axis=0)),
        ],
        axis=0,
    )
    mixed = dot3(split2(turned), split2(bins_table_ref[...]))
    halves = []
    for h in range(2):
        real = mixed[h * LANES : (h + 1) * LANES, :LANES]
        imag = mixed[h * LANES : (h + 1) * LANES, LANES:]
        cos_part, sin_part = bins_twid_ref[0], bins_twid_ref[1]
        halves.append(
            jnp.concatenate(
                [real * cos_part - imag * sin_part, real * sin_part + imag * cos_part], axis=0
            )
        )
    series = dot3(
        split2(cols_table_ref[...]), split2(jnp.concatenate(halves, axis=1))
    )
    for c in range(2):
        for h in range(2):
            part = series[c * NQ : (c + 1) * NQ, h * LANES : (h + 1) * LANES]
            blocks = swap_blocks([part[i * per : (i + 1) * per] for i in range(SFT_DEV)])
            if h == 0:
                for s in range(SFT_DEV):
                    buf[pl.ds(2 * per * (s + 1) + c, per, stride=2), :] = blocks[s]
            else:
                buf[pl.ds(c, per, stride=2), :] = blocks[SFT_DEV - 1]
                buf[pl.ds(2 * per * (SFT_DEV + 1) + c, per, stride=2), :] = blocks[0]

    lane = lax.broadcasted_iota(jnp.int32, (8, LANES), 1)
    wide_lane = lax.broadcasted_iota(jnp.int32, (runs, LANES), 1)
    for t in range(tmpl_local):
        for r in range(runs):
            offset = (start_ref[t, r % run_rows, NP * (r // run_rows)] >> 3) - MAXD
            start = offset + (RUN * r + NB - 1)
            shift = start & (LANES - 1)
            held = buf[pl.ds(2 * (start >> 7), 8), :]
            rolled = pltpu.roll(held, LANES - shift, 1)
            below = pltpu.roll(rolled, 6, 0)
            seg[8 * r : 8 * r + 8, :] = jnp.where(lane < LANES - shift, rolled, below)
        taps = []
        for c in range(2):
            lines = [seg[pl.ds(2 * r + c, runs, stride=8), :] for r in range(3)]
            moved = [lines] + [
                [pltpu.roll(item, LANES - k, 1) for item in lines] for k in range(1, 4)
            ]
            taps.append(moved)
        for r in range(2):
            code = code_t[t, pl.ds(r, runs, stride=2), :]
            fraction = (code & (NFRAC - 1)).astype(jnp.float32) * (1.0 / NFRAC)
            coeffs = lagrange(fraction)
            for c in range(2):
                moved = taps[c]
                total = coeffs[0] * moved[0][r]
                for k in range(1, 4):
                    total = total + coeffs[k] * jnp.where(
                        wide_lane < LANES - k, moved[k][r], moved[k][r + 1]
                    )
                line[c, pl.ds(r, runs, stride=2), :] = total
        for c in range(2):
            r_out[t, :, c] = blocked(line[c])

        def send_r(rank):
            remote(
                r_out.at[t, rank], r_got.at[t, me], r_send.at[t, rank], r_recv.at[t, me], rank
            ).start()

        peers(send_r)
        r_got[t, me] = r_out[t, me]

    at = lax.broadcasted_iota(jnp.int32, (1, LANES), 1) * me

    def advanced(table, modulus):
        angle = at.astype(jnp.float32) * (2.0 * math.pi / modulus)
        cos_step, sin_step = jnp.cos(angle), jnp.sin(angle)
        cos_base, sin_base = table[0], table[1]
        return (
            cos_base * cos_step - sin_base * sin_step,
            sin_base * cos_step + cos_base * sin_step,
        )

    cos_left, sin_left = advanced(left_ref, NQ * owners)
    parts = [[cos_left, sin_left], [-sin_left, cos_left]]
    for i in range(2):
        for j in range(2):
            spot = (slice(i * NQ, (i + 1) * NQ), slice(j * NQ, (j + 1) * NQ))
            left_hi[spot], left_lo[spot] = split2(parts[i][j])
    right_hi[...], right_lo[...] = split2(right_table_ref[...])
    cos_part, sin_part = advanced(twid_ref, sample_total)
    twid[0] = cos_part
    twid[1] = -sin_part

    def arrival(out, got, send, recv, t, rank):
        return remote(out.at[t, rank], got.at[t, rank], send.at[t, rank], recv.at[t, rank], rank)

    for t in range(tmpl_local):
        peers(lambda rank: arrival(w_out, w_got, w_send, w_recv, t, rank).wait())
        peers(lambda rank: arrival(r_out, r_got, r_send, r_recv, t, rank).wait())
        for w in range(2):
            real = [r_got[t, i, 0] * w_got[t, i, w] for i in range(owners)]
            imag = [r_got[t, i, 1] * w_got[t, i, w] for i in range(owners)]
            real, imag = owner_dft(real, imag)
            for i in range(owners):
                z_out[t, i, 2 * w] = real[i]
                z_out[t, i, 2 * w + 1] = imag[i]

        def send_z(rank):
            remote(
                z_out.at[t, rank], z_got.at[t, me], z_send.at[t, rank], z_recv.at[t, me], rank
            ).start()

        peers(send_z)
        z_got[t, me] = z_out[t, me]

    def sums_arrival(rank):
        remote(sums, sums_got.at[rank], s_send.at[rank], s_recv.at[rank], rank).wait()

    peers(sums_arrival)
    total = jnp.sum(sums_got[...], axis=0)
    total = jnp.sum(total, axis=1, keepdims=True) / sample_total
    norm = 1.0 / math.sqrt(sample_total)
    for t in range(tmpl_local):
        peers(lambda rank: arrival(z_out, z_got, z_send, z_recv, t, rank).wait())
        value = jnp.concatenate(
            [
                jnp.concatenate(
                    [z_got[t, :, 2 * w + c].reshape(NQ, LANES) for c in range(2)], axis=0
                )
                for w in range(2)
            ],
            axis=1,
        )
        mixed = dot3((left_hi[...], left_lo[...]), split2(value))
        lines = []
        for w in range(2):
            real = mixed[:NQ, w * LANES : (w + 1) * LANES]
            imag = mixed[NQ:, w * LANES : (w + 1) * LANES]
            cos_part, sin_part = twid[0], twid[1]
            lines.append(
                jnp.concatenate(
                    [real * cos_part - imag * sin_part, real * sin_part + imag * cos_part], axis=1
                )
            )
        spectra = dot3(
            split2(jnp.concatenate(lines, axis=0)), (right_hi[...], right_lo[...])
        ) * norm
        a_real, a_imag = spectra[:NQ, :LANES], spectra[:NQ, LANES:]
        b_real, b_imag = spectra[NQ:, :LANES], spectra[NQ:, LANES:]
        power_a = total[3 * t : 3 * t + 1] + stat_eps
        power_b = total[3 * t + 1 : 3 * t + 2] + stat_eps
        cross_ab = total[3 * t + 2 : 3 * t + 3]
        det = jnp.maximum(
            power_a * power_b - cross_ab * cross_ab, floor_share * power_a * power_b
        )
        stat = (
            power_b * (a_real * a_real + a_imag * a_imag)
            + power_a * (b_real * b_real + b_imag * b_imag)
            - 2.0 * cross_ab * (a_real * b_real + a_imag * b_imag)
        ) / det
        blocks = swap_blocks([stat[i * per : (i + 1) * per] for i in range(SFT_DEV)])
        for j, block in enumerate(blocks):
            out_ref[t, j * per : (j + 1) * per, :] = block

    for d in range(1, band_size):
        bins_copy(d).wait_send()
    for e in range(band_size):
        for side in range(2):

            @pl.when(edge_is_sent(e, side))
            def _():
                edge_copy(e, side).wait_send()


def turns(product, modulus):
    angles = 2.0 * np.pi / modulus * (product % modulus)
    return np.cos(angles), np.sin(angles)


def constant_tables():
    per = NQ // SFT_DEV
    at = np.arange(LANES)
    bin_cos, bin_sin = turns(np.arange(NP)[:, None] * np.arange(NP)[None, :], NP)
    same = np.eye(SFT_DEV)
    wide = [
        np.einsum("kp,st->kstp", part, same).reshape(LANES, LANES) for part in (bin_cos, bin_sin)
    ]
    bins = np.block([[wide[0], wide[1]], [-wide[1], wide[0]]])
    bins_twid = np.stack(turns(at[:, None] * (at % NP)[None, :], NB))
    col_order = at // per + SFT_DEV * (at % per)
    col_cos, col_sin = turns(col_order[:, None] * at[None, :], NQ)
    cols = np.block([[col_cos, -col_sin], [col_sin, col_cos]]) / math.sqrt(NB)
    fine = at // NP + SFT_DEV * (at % NP)
    fine_cos, fine_sin = turns(at[:, None] * fine[None, :], LANES)
    right = np.block([[fine_cos, -fine_sin], [fine_sin, fine_cos]])
    left = np.stack(turns(col_order[:, None] * at[None, :], NQ))
    twid = np.stack(turns(col_order[:, None] * at[None, :], NQ * LANES))
    tables = (bins, bins_twid, cols, left, twid, right)
    return tuple(jnp.asarray(table.astype(np.float32)) for table in tables)


def per_device(sft_bins, delay_code, antenna):
    band_size = lax.axis_size("band")
    owners = lax.axis_size("tm") * band_size
    sample_total = SFT_DEV * owners * NB
    tmpl_local = delay_code.shape[0]
    run_cols = RUN // NP
    runs_down = NQ // run_cols
    run_count = SFT_DEV * runs_down
    per = NQ // SFT_DEV
    code = delay_code.reshape(tmpl_local, runs_down, run_cols, LANES)
    operands = (sft_bins, antenna, code) + constant_tables()
    bin_width = sft_bins.shape[2]
    pieces = bin_width // LANES
    block_rows = NQ // owners
    f32 = jnp.float32
    dma = pltpu.SemaphoreType.DMA
    count = len(operands)

    def kernel(*refs):
        near = refs[count + 1 : 2 * count + 1]
        search_kernel(
            band_size,
            owners,
            sample_total,
            refs[:count],
            refs[count],
            near,
            *refs[2 * count + 1 :],
        )

    out = pl.pallas_call(
        kernel,
        out_shape=jax.ShapeDtypeStruct((tmpl_local, NQ, LANES), f32),
        in_specs=[pl.BlockSpec(memory_space=pl.ANY)] * count,
        out_specs=pl.BlockSpec(memory_space=pltpu.VMEM),
        scratch_shapes=[pltpu.VMEM(item.shape, item.dtype) for item in operands]
        + [
            pltpu.SMEM((tmpl_local, runs_down, LANES), jnp.int32),
        ]
        + [pltpu.VMEM((2 * NQ, 2 * NQ), jnp.bfloat16)] * 4
        + [
            pltpu.VMEM((2, NQ, LANES), f32),
            pltpu.VMEM((band_size, 2, SFT_DEV, bin_width), f32),
            pltpu.VMEM((band_size, 2, 2, pieces, LANES), f32),
            pltpu.VMEM((2, band_size, 2, pieces, LANES), f32),
            pltpu.VMEM((2 * per * (SFT_DEV + 2), LANES), f32),
            pltpu.VMEM((8 * run_count, LANES), f32),
            pltpu.VMEM((tmpl_local, NQ, LANES), jnp.int32),
            pltpu.VMEM((2, NQ, LANES), f32),
        ]
        + [pltpu.VMEM((tmpl_local, owners, 2, block_rows, LANES), f32)] * 4
        + [pltpu.VMEM((tmpl_local, owners, 4, block_rows, LANES), f32)] * 2
        + [
            pltpu.VMEM((8, LANES), f32),
            pltpu.VMEM((owners, 8, LANES), f32),
            dma((band_size,)),
            dma((band_size,)),
            dma((band_size, 2)),
            dma((2, band_size)),
            dma((tmpl_local, owners)),
            dma((tmpl_local, owners)),
            dma((owners,)),
            dma((owners,)),
        ]
        + [dma((tmpl_local, owners))] * 4
        + [dma((count,)), dma],
        compiler_params=pltpu.CompilerParams(
            collective_id=0, has_side_effects=True, vmem_limit_bytes=60 * 1024 * 1024
        ),
    )(*operands)
    return out[:, :, None, :]


def solution(mesh):
    in_specs = (
        P(None, ("groups", "tm"), "band"),
        P(("groups", "tmpl"), None, ("tm", "band")),
        P(("groups", "tmpl"), None, None, ("tm", "band")),
    )
    out_specs = P(("groups", "tmpl"), None, ("tm", "band"), None)
    return jax.shard_map(
        per_device, mesh=mesh, in_specs=in_specs, out_specs=out_specs, check_vma=False
    )
```

```python
import functools
import math

import jax
import jax.numpy as jnp
import numpy as np
from jax import lax
from jax.experimental import pallas as pl
from jax.experimental.pallas import tpu as pltpu
from jax.sharding import PartitionSpec as P

NB = 2048
NQ = 128
NP = 16
SFT_DEV = 8
MAXD = 1000
NFRAC = 8
RUN = 256
LANES = 128

stat_eps = 1e-06
floor_share = 0.5
MESH = pl.DeviceIdType.MESH


def lagrange(fraction):
    return (
        -fraction * (fraction - 1.0) * (fraction - 2.0) / 6.0,
        (fraction + 1.0) * (fraction - 1.0) * (fraction - 2.0) / 2.0,
        -(fraction + 1.0) * fraction * (fraction - 2.0) / 2.0,
        (fraction + 1.0) * fraction * (fraction - 1.0) / 6.0,
    )


def split2(value):
    high = value.astype(jnp.bfloat16)
    return high, (value - high.astype(jnp.float32)).astype(jnp.bfloat16)


def dot3(lhs, rhs):
    lhs_hi, lhs_lo = lhs
    rhs_hi, rhs_lo = rhs
    dot = functools.partial(jnp.dot, preferred_element_type=jnp.float32)
    return dot(lhs_hi, rhs_hi) + (dot(lhs_hi, rhs_lo) + dot(lhs_lo, rhs_hi))


def swap_blocks(blocks):
    count = len(blocks)
    width = LANES // count
    blocks = list(blocks)
    lane_block = lax.broadcasted_iota(jnp.int32, blocks[0].shape, 1) // width
    half = count // 2
    while half:
        keep = (lane_block & half) == 0
        for i in range(count):
            if i & half == 0:
                low, high = blocks[i], blocks[i + half]
                blocks[i] = jnp.where(keep, low, pltpu.roll(high, half * width, 1))
                blocks[i + half] = jnp.where(
                    keep, pltpu.roll(low, LANES - half * width, 1), high
                )
        half //= 2
    return blocks


def grid_to_time(plane):
    return jnp.concatenate(swap_blocks([plane(i) for i in range(SFT_DEV)]), axis=0)


def owner_dft(real, imag):
    count = len(real)
    if count == 1:
        return real, imag
    half = count // 2
    sum_real = [real[k] + real[k + half] for k in range(half)]
    sum_imag = [imag[k] + imag[k + half] for k in range(half)]
    dif_real, dif_imag = [], []
    for k in range(half):
        d_real, d_imag = real[k] - real[k + half], imag[k] - imag[k + half]
        if k == 0:
            dif_real.append(d_real)
            dif_imag.append(d_imag)
        elif 2 * k == half:
            dif_real.append(d_imag)
            dif_imag.append(-d_real)
        else:
            cos_part = math.cos(2.0 * math.pi * k / count)
            sin_part = math.sin(2.0 * math.pi * k / count)
            dif_real.append(d_real * cos_part + d_imag * sin_part)
            dif_imag.append(d_imag * cos_part - d_real * sin_part)
    even = owner_dft(sum_real, sum_imag)
    odd = owner_dft(dif_real, dif_imag)
    out_real, out_imag = [], []
    for k in range(half):
        out_real += [even[0][k], odd[0][k]]
        out_imag += [even[1][k], odd[1][k]]
    return out_real, out_imag


def search_kernel(
    band_size,
    owners,
    sample_total,
    far_refs,
    out_ref,
    near_refs,
    start_ref,
    left_hi,
    left_lo,
    right_hi,
    right_lo,
    twid,
    grid,
    edge,
    halo,
    buf,
    seg,
    code_t,
    line,
    w_out,
    w_got,
    r_out,
    r_got,
    z_out,
    z_got,
    sums,
    sums_got,
    bin_send,
    bin_recv,
    edge_send,
    edge_recv,
    w_send,
    w_recv,
    s_send,
    s_recv,
    r_send,
    r_recv,
    z_send,
    z_recv,
    load_sem,
    start_sem,
):
    loads = [
        pltpu.make_async_copy(far, near, load_sem.at[k])
        for k, (far, near) in enumerate(zip(far_refs, near_refs))
    ]
    for load in loads:
        load.start()
    (
        bins_ref,
        ant_ref,
        code_ref,
        bins_table_ref,
        bins_twid_ref,
        cols_table_ref,
        left_ref,
        twid_ref,
        right_table_ref,
    ) = near_refs
    tmpl_local, run_rows, run_cols, _ = code_ref.shape
    starts_load = pltpu.make_async_copy(far_refs[2].at[:, :, 0, :], start_ref, start_sem)
    starts_load.start()
    runs = SFT_DEV * run_rows
    code_flat = code_ref.reshape(tmpl_local, NQ, LANES)
    pieces = edge.shape[3]
    per = NQ // SFT_DEV
    block_rows = NQ // owners
    my_tm = lax.axis_index("tm")
    my_band = lax.axis_index("band")
    me = my_tm * band_size + my_band

    def place(rank):
        return {"tm": rank // band_size, "band": rank % band_size}

    def peers(body):
        def step(d, carry):
            body((me + d) % owners)
            return carry

        lax.fori_loop(1, owners, step, 0, unroll=owners <= 8)

    def remote(src, dst, send, recv, rank):
        return pltpu.make_async_remote_copy(
            src_ref=src,
            dst_ref=dst,
            send_sem=send,
            recv_sem=recv,
            device_id=place(rank),
            device_id_type=MESH,
        )

    barrier = pltpu.get_barrier_semaphore()
    peers(
        lambda rank: pl.semaphore_signal(
            barrier, inc=1, device_id=place(rank), device_id_type=MESH
        )
    )

    loads[0].wait()
    for e in range(band_size):
        for side in range(2):
            row = SFT_DEV * e + (SFT_DEV - 1 if side == 0 else 0)
            for c in range(2):
                for k in range(pieces):
                    edge[e, side, c, k : k + 1, :] = bins_ref[
                        c, row : row + 1, k * LANES : (k + 1) * LANES
                    ]

    @pl.when(me == 0)
    def _():
        halo[0] = jnp.zeros(halo.shape[1:], jnp.float32)

    @pl.when(me == owners - 1)
    def _():
        halo[1] = jnp.zeros(halo.shape[1:], jnp.float32)

    def blocked(value):
        return value.reshape(owners, block_rows, LANES)

    sums[...] = jnp.zeros_like(sums)
    loads[1].wait()
    for t in range(tmpl_local):
        wts = []
        for w in range(2):
            value = grid_to_time(lambda i: ant_ref[t, w, pl.ds(i, per, stride=SFT_DEV), :])
            w_out[t, :, w] = blocked(value)
            wts.append(value)
        wa, wb = wts
        for k, product in enumerate((wa * wa, wb * wb, wa * wb)):
            sums[3 * t + k : 3 * t + k + 1, :] = jnp.sum(product, axis=0, keepdims=True)
        w_got[t, me] = w_out[t, me]
    sums_got[me] = sums[...]

    pl.semaphore_wait(barrier, owners - 1)

    def bins_rows(band):
        return pl.ds(pl.multiple_of(SFT_DEV * band, SFT_DEV), SFT_DEV)

    def bins_copy(d):
        band = (my_band + d) % band_size
        return remote(
            bins_ref.at[:, bins_rows(band), :],
            grid.at[my_band],
            bin_send.at[band],
            bin_recv.at[my_band],
            my_tm * band_size + band,
        )

    def bins_arrival(d):
        band = (my_band + d) % band_size
        return remote(
            bins_ref.at[:, bins_rows(band), :],
            grid.at[band],
            bin_send.at[band],
            bin_recv.at[band],
            my_tm * band_size + band,
        )

    for d in range(1, band_size):
        bins_copy(d).start()

    def edge_target(e, side):
        return my_tm * band_size + e + (1 if side == 0 else -1)

    def edge_copy(e, side):
        return remote(
            edge.at[e, side],
            halo.at[side, my_band],
            edge_send.at[e, side],
            edge_recv.at[side, my_band],
            edge_target(e, side),
        )

    def edge_is_sent(e, side):
        rank = edge_target(e, side)
        return jnp.logical_and(rank != me, jnp.logical_and(rank >= 0, rank < owners))

    for e in range(band_size):
        for side in range(2):

            @pl.when(edge_is_sent(e, side))
            def _():
                edge_copy(e, side).start()

            @pl.when(edge_target(e, side) == me)
            def _():
                halo[side, my_band] = edge[e, side]

    grid[my_band] = bins_ref[:, bins_rows(my_band), :]

    for t in range(tmpl_local):

        def send_w(rank):
            remote(
                w_out.at[t, rank], w_got.at[t, me], w_send.at[t, rank], w_recv.at[t, me], rank
            ).start()

        peers(send_w)

    peers(
        lambda rank: remote(
            sums, sums_got.at[me], s_send.at[rank], s_recv.at[me], rank
        ).start()
    )

    loads[2].wait()
    for t in range(tmpl_local):
        code_t[t] = grid_to_time(lambda i: code_flat[t, pl.ds(i, per, stride=SFT_DEV), :])
    starts_load.wait()
    for load in loads[3:]:
        load.wait()

    for d in range(1, band_size):
        bins_arrival(d).wait_recv()
    for side in range(2):
        source = (me - 1 if side == 0 else me + 1) // band_size

        @pl.when(jnp.logical_and(me > 0 if side == 0 else me < owners - 1, source != my_tm))
        def _():
            for band in range(band_size):
                remote(
                    edge.at[0, side],
                    halo.at[side, band],
                    edge_send.at[0, side],
                    edge_recv.at[side, band],
                    source * band_size + band,
                ).wait_recv()

        @pl.when(jnp.logical_and(me > 0 if side == 0 else me < owners - 1, source == my_tm))
        def _():
            for d in range(1, band_size):
                band = (my_band + d) % band_size
                remote(
                    edge.at[0, side],
                    halo.at[side, band],
                    edge_send.at[0, side],
                    edge_recv.at[side, band],
                    my_tm * band_size + band,
                ).wait_recv()

    sub = lax.broadcasted_iota(jnp.int32, (SFT_DEV, LANES), 0)
    main_rows, rim_rows = [], []
    for c in range(2):
        for band in range(band_size):
            for k in range(pieces):
                main_rows.append(grid[band, c, :, k * LANES : (k + 1) * LANES])
                first = jnp.broadcast_to(halo[1, band, c, k : k + 1, :], (SFT_DEV, LANES))
                final = jnp.broadcast_to(halo[0, band, c, k : k + 1, :], (SFT_DEV, LANES))
                rim_rows.append(
                    jnp.where(sub == 0, first, jnp.where(sub == SFT_DEV - 1, final, 0.0))
                )
    turned = jnp.concatenate(
        [
            jnp.transpose(jnp.concatenate(main_rows, axis=0)),
            jnp.transpose(jnp.concatenate(rim_rows, axis=0)),
        ],
        axis=0,
    )
    mixed = dot3(split2(turned), split2(bins_table_ref[...]))
    halves = []
    for h in range(2):
        real = mixed[h * LANES : (h + 1) * LANES, :LANES]
        imag = mixed[h * LANES : (h + 1) * LANES, LANES:]
        cos_part, sin_part = bins_twid_ref[0], bins_twid_ref[1]
        halves.append(
            jnp.concatenate(
                [real * cos_part - imag * sin_part, real * sin_part + imag * cos_part], axis=0
            )
        )
    series = dot3(
        split2(cols_table_ref[...]), split2(jnp.concatenate(halves, axis=1))
    )
    for c in range(2):
        for h in range(2):
            part = series[c * NQ : (c + 1) * NQ, h * LANES : (h + 1) * LANES]
            blocks = swap_blocks([part[i * per : (i + 1) * per] for i in range(SFT_DEV)])
            if h == 0:
                for s in range(SFT_DEV):
                    buf[pl.ds(2 * per * (s + 1) + c, per, stride=2), :] = blocks[s]
            else:
                buf[pl.ds(c, per, stride=2), :] = blocks[SFT_DEV - 1]
                buf[pl.ds(2 * per * (SFT_DEV + 1) + c, per, stride=2), :] = blocks[0]

    lane = lax.broadcasted_iota(jnp.int32, (8, LANES), 1)
    wide_lane = lax.broadcasted_iota(jnp.int32, (runs, LANES), 1)
    for t in range(tmpl_local):
        for r in range(runs):
            offset = (start_ref[t, r % run_rows, NP * (r // run_rows)] >> 3) - MAXD
            start = offset + (RUN * r + NB - 1)
            shift = start & (LANES - 1)
            held = buf[pl.ds(2 * (start >> 7), 8), :]
            rolled = pltpu.roll(held, LANES - shift, 1)
            below = pltpu.roll(rolled, 6, 0)
            seg[8 * r : 8 * r + 8, :] = jnp.where(lane < LANES - shift, rolled, below)
        taps = []
        for c in range(2):
            lines = [seg[pl.ds(2 * r + c, runs, stride=8), :] for r in range(3)]
            moved = [lines] + [
                [pltpu.roll(item, LANES - k, 1) for item in lines] for k in range(1, 4)
            ]
            taps.append(moved)
        for r in range(2):
            code = code_t[t, pl.ds(r, runs, stride=2), :]
            fraction = (code & (NFRAC - 1)).astype(jnp.float32) * (1.0 / NFRAC)
            coeffs = lagrange(fraction)
            for c in range(2):
                moved = taps[c]
                total = coeffs[0] * moved[0][r]
                for k in range(1, 4):
                    total = total + coeffs[k] * jnp.where(
                        wide_lane < LANES - k, moved[k][r], moved[k][r + 1]
                    )
                line[c, pl.ds(r, runs, stride=2), :] = total
        for c in range(2):
            r_out[t, :, c] = blocked(line[c])

        def send_r(rank):
            remote(
                r_out.at[t, rank], r_got.at[t, me], r_send.at[t, rank], r_recv.at[t, me], rank
            ).start()

        peers(send_r)
        r_got[t, me] = r_out[t, me]

    at = lax.broadcasted_iota(jnp.int32, (1, LANES), 1) * me

    def advanced(table, modulus):
        angle = at.astype(jnp.float32) * (2.0 * math.pi / modulus)
        cos_step, sin_step = jnp.cos(angle), jnp.sin(angle)
        cos_base, sin_base = table[0], table[1]
        return (
            cos_base * cos_step - sin_base * sin_step,
            sin_base * cos_step + cos_base * sin_step,
        )

    cos_left, sin_left = advanced(left_ref, NQ * owners)
    parts = [[cos_left, sin_left], [-sin_left, cos_left]]
    for i in range(2):
        for j in range(2):
            spot = (slice(i * NQ, (i + 1) * NQ), slice(j * NQ, (j + 1) * NQ))
            left_hi[spot], left_lo[spot] = split2(parts[i][j])
    right_hi[...], right_lo[...] = split2(right_table_ref[...])
    cos_part, sin_part = advanced(twid_ref, sample_total)
    twid[0] = cos_part
    twid[1] = -sin_part

    def arrival(out, got, send, recv, t, rank):
        return remote(out.at[t, rank], got.at[t, rank], send.at[t, rank], recv.at[t, rank], rank)

    for t in range(tmpl_local):
        peers(lambda rank: arrival(w_out, w_got, w_send, w_recv, t, rank).wait())
        peers(lambda rank: arrival(r_out, r_got, r_send, r_recv, t, rank).wait())
        for w in range(2):
            real = [r_got[t, i, 0] * w_got[t, i, w] for i in range(owners)]
            imag = [r_got[t, i, 1] * w_got[t, i, w] for i in range(owners)]
            real, imag = owner_dft(real, imag)
            for i in range(owners):
                z_out[t, i, 2 * w] = real[i]
                z_out[t, i, 2 * w + 1] = imag[i]

        def send_z(rank):
            remote(
                z_out.at[t, rank], z_got.at[t, me], z_send.at[t, rank], z_recv.at[t, me], rank
            ).start()

        peers(send_z)
        z_got[t, me] = z_out[t, me]

    def sums_arrival(rank):
        remote(sums, sums_got.at[rank], s_send.at[rank], s_recv.at[rank], rank).wait()

    peers(sums_arrival)
    total = jnp.sum(sums_got[...], axis=0)
    total = jnp.sum(total, axis=1, keepdims=True) / sample_total
    norm = 1.0 / math.sqrt(sample_total)
    for t in range(tmpl_local):
        peers(lambda rank: arrival(z_out, z_got, z_send, z_recv, t, rank).wait())
        value = jnp.concatenate(
            [
                jnp.concatenate(
                    [z_got[t, :, 2 * w + c].reshape(NQ, LANES) for c in range(2)], axis=0
                )
                for w in range(2)
            ],
            axis=1,
        )
        mixed = dot3((left_hi[...], left_lo[...]), split2(value))
        lines = []
        for w in range(2):
            real = mixed[:NQ, w * LANES : (w + 1) * LANES]
            imag = mixed[NQ:, w * LANES : (w + 1) * LANES]
            cos_part, sin_part = twid[0], twid[1]
            lines.append(
                jnp.concatenate(
                    [real * cos_part - imag * sin_part, real * sin_part + imag * cos_part], axis=1
                )
            )
        spectra = dot3(
            split2(jnp.concatenate(lines, axis=0)), (right_hi[...], right_lo[...])
        ) * norm
        a_real, a_imag = spectra[:NQ, :LANES], spectra[:NQ, LANES:]
        b_real, b_imag = spectra[NQ:, :LANES], spectra[NQ:, LANES:]
        power_a = total[3 * t : 3 * t + 1] + stat_eps
        power_b = total[3 * t + 1 : 3 * t + 2] + stat_eps
        cross_ab = total[3 * t + 2 : 3 * t + 3]
        det = jnp.maximum(
            power_a * power_b - cross_ab * cross_ab, floor_share * power_a * power_b
        )
        stat = (
            power_b * (a_real * a_real + a_imag * a_imag)
            + power_a * (b_real * b_real + b_imag * b_imag)
            - 2.0 * cross_ab * (a_real * b_real + a_imag * b_imag)
        ) / det
        blocks = swap_blocks([stat[i * per : (i + 1) * per] for i in range(SFT_DEV)])
        for j, block in enumerate(blocks):
            out_ref[t, j * per : (j + 1) * per, :] = block

    for d in range(1, band_size):
        bins_copy(d).wait_send()
    for e in range(band_size):
        for side in range(2):

            @pl.when(edge_is_sent(e, side))
            def _():
                edge_copy(e, side).wait_send()


def turns(product, modulus):
    angles = 2.0 * np.pi / modulus * (product % modulus)
    return np.cos(angles), np.sin(angles)


def constant_tables():
    per = NQ // SFT_DEV
    at = np.arange(LANES)
    bin_cos, bin_sin = turns(np.arange(NP)[:, None] * np.arange(NP)[None, :], NP)
    same = np.eye(SFT_DEV)
    wide = [
        np.einsum("kp,st->kstp", part, same).reshape(LANES, LANES) for part in (bin_cos, bin_sin)
    ]
    bins = np.block([[wide[0], wide[1]], [-wide[1], wide[0]]])
    bins_twid = np.stack(turns(at[:, None] * (at % NP)[None, :], NB))
    col_order = at // per + SFT_DEV * (at % per)
    col_cos, col_sin = turns(col_order[:, None] * at[None, :], NQ)
    cols = np.block([[col_cos, -col_sin], [col_sin, col_cos]]) / math.sqrt(NB)
    fine = at // NP + SFT_DEV * (at % NP)
    fine_cos, fine_sin = turns(at[:, None] * fine[None, :], LANES)
    right = np.block([[fine_cos, -fine_sin], [fine_sin, fine_cos]])
    left = np.stack(turns(col_order[:, None] * at[None, :], NQ))
    twid = np.stack(turns(col_order[:, None] * at[None, :], NQ * LANES))
    tables = (bins, bins_twid, cols, left, twid, right)
    return tuple(jnp.asarray(table.astype(np.float32)) for table in tables)


def per_device(sft_bins, delay_code, antenna):
    band_size = lax.axis_size("band")
    owners = lax.axis_size("tm") * band_size
    sample_total = SFT_DEV * owners * NB
    tmpl_local = delay_code.shape[0]
    run_cols = RUN // NP
    runs_down = NQ // run_cols
    run_count = SFT_DEV * runs_down
    per = NQ // SFT_DEV
    code = delay_code.reshape(tmpl_local, runs_down, run_cols, LANES)
    operands = tuple(
        pltpu.with_memory_space_constraint(item, pltpu.HBM)
        for item in (sft_bins, antenna, code) + constant_tables()
    )
    bin_width = sft_bins.shape[2]
    pieces = bin_width // LANES
    block_rows = NQ // owners
    f32 = jnp.float32
    dma = pltpu.SemaphoreType.DMA
    count = len(operands)

    def kernel(*refs):
        near = refs[count + 1 : 2 * count + 1]
        search_kernel(
            band_size,
            owners,
            sample_total,
            refs[:count],
            refs[count],
            near,
            *refs[2 * count + 1 :],
        )

    out = pl.pallas_call(
        kernel,
        out_shape=pltpu.VMEM((tmpl_local, NQ, LANES), f32),
        in_specs=[pl.BlockSpec(memory_space=pltpu.HBM)] * count,
        out_specs=pl.BlockSpec(memory_space=pltpu.VMEM),
        scratch_shapes=[pltpu.VMEM(item.shape, item.dtype) for item in operands]
        + [
            pltpu.SMEM((tmpl_local, runs_down, LANES), jnp.int32),
        ]
        + [pltpu.VMEM((2 * NQ, 2 * NQ), jnp.bfloat16)] * 4
        + [
            pltpu.VMEM((2, NQ, LANES), f32),
            pltpu.VMEM((band_size, 2, SFT_DEV, bin_width), f32),
            pltpu.VMEM((band_size, 2, 2, pieces, LANES), f32),
            pltpu.VMEM((2, band_size, 2, pieces, LANES), f32),
            pltpu.VMEM((2 * per * (SFT_DEV + 2), LANES), f32),
            pltpu.VMEM((8 * run_count, LANES), f32),
            pltpu.VMEM((tmpl_local, NQ, LANES), jnp.int32),
            pltpu.VMEM((2, NQ, LANES), f32),
        ]
        + [pltpu.VMEM((tmpl_local, owners, 2, block_rows, LANES), f32)] * 4
        + [pltpu.VMEM((tmpl_local, owners, 4, block_rows, LANES), f32)] * 2
        + [
            pltpu.VMEM((8, LANES), f32),
            pltpu.VMEM((owners, 8, LANES), f32),
            dma((band_size,)),
            dma((band_size,)),
            dma((band_size, 2)),
            dma((2, band_size)),
            dma((tmpl_local, owners)),
            dma((tmpl_local, owners)),
            dma((owners,)),
            dma((owners,)),
        ]
        + [dma((tmpl_local, owners))] * 4
        + [dma((count,)), dma],
        compiler_params=pltpu.CompilerParams(
            collective_id=0, has_side_effects=True, vmem_limit_bytes=48 * 1024 * 1024
        ),
    )(*operands)
    return out[:, :, None, :]


def solution(mesh):
    in_specs = (
        P(None, ("groups", "tm"), "band"),
        P(("groups", "tmpl"), None, ("tm", "band")),
        P(("groups", "tmpl"), None, None, ("tm", "band")),
    )
    out_specs = P(("groups", "tmpl"), None, ("tm", "band"), None)
    return jax.shard_map(
        per_device, mesh=mesh, in_specs=in_specs, out_specs=out_specs, check_vma=False
    )
```

```python
import functools
import math

import jax
import jax.numpy as jnp
import numpy as np
from jax import lax
from jax.experimental import pallas as pl
from jax.experimental.pallas import tpu as pltpu
from jax.sharding import PartitionSpec as P

NB = 2048
NQ = 128
NP = 16
SFT_DEV = 8
MAXD = 1000
NFRAC = 8
RUN = 256
LANES = 128

stat_eps = 1e-06
floor_share = 0.5
MESH = pl.DeviceIdType.MESH


def lagrange(fraction):
    return (
        -fraction * (fraction - 1.0) * (fraction - 2.0) / 6.0,
        (fraction + 1.0) * (fraction - 1.0) * (fraction - 2.0) / 2.0,
        -(fraction + 1.0) * fraction * (fraction - 2.0) / 2.0,
        (fraction + 1.0) * fraction * (fraction - 1.0) / 6.0,
    )


def split2(value):
    high = value.astype(jnp.bfloat16)
    return high, (value - high.astype(jnp.float32)).astype(jnp.bfloat16)


def dot3(lhs, rhs):
    lhs_hi, lhs_lo = lhs
    rhs_hi, rhs_lo = rhs
    dot = functools.partial(jnp.dot, preferred_element_type=jnp.float32)
    return dot(lhs_hi, rhs_hi) + (dot(lhs_hi, rhs_lo) + dot(lhs_lo, rhs_hi))


def swap_blocks(blocks):
    count = len(blocks)
    width = LANES // count
    blocks = list(blocks)
    lane_block = lax.broadcasted_iota(jnp.int32, blocks[0].shape, 1) // width
    half = count // 2
    while half:
        keep = (lane_block & half) == 0
        for i in range(count):
            if i & half == 0:
                low, high = blocks[i], blocks[i + half]
                blocks[i] = jnp.where(keep, low, pltpu.roll(high, half * width, 1))
                blocks[i + half] = jnp.where(
                    keep, pltpu.roll(low, LANES - half * width, 1), high
                )
        half //= 2
    return blocks


def grid_to_time(plane):
    return jnp.concatenate(swap_blocks([plane(i) for i in range(SFT_DEV)]), axis=0)


def owner_dft(real, imag):
    count = len(real)
    if count == 1:
        return real, imag
    half = count // 2
    sum_real = [real[k] + real[k + half] for k in range(half)]
    sum_imag = [imag[k] + imag[k + half] for k in range(half)]
    dif_real, dif_imag = [], []
    for k in range(half):
        d_real, d_imag = real[k] - real[k + half], imag[k] - imag[k + half]
        if k == 0:
            dif_real.append(d_real)
            dif_imag.append(d_imag)
        elif 2 * k == half:
            dif_real.append(d_imag)
            dif_imag.append(-d_real)
        else:
            cos_part = math.cos(2.0 * math.pi * k / count)
            sin_part = math.sin(2.0 * math.pi * k / count)
            dif_real.append(d_real * cos_part + d_imag * sin_part)
            dif_imag.append(d_imag * cos_part - d_real * sin_part)
    even = owner_dft(sum_real, sum_imag)
    odd = owner_dft(dif_real, dif_imag)
    out_real, out_imag = [], []
    for k in range(half):
        out_real += [even[0][k], odd[0][k]]
        out_imag += [even[1][k], odd[1][k]]
    return out_real, out_imag


def far_first(count):
    return sorted(range(1, count), key=lambda d: abs(2 * d - count))


def search_kernel(
    band_size,
    owners,
    sample_total,
    far_refs,
    out_ref,
    near_refs,
    start_ref,
    left_hi,
    left_lo,
    right_hi,
    right_lo,
    twid,
    grid,
    edge,
    halo,
    buf,
    seg,
    code_t,
    line,
    w_out,
    w_got,
    r_out,
    r_got,
    z_out,
    z_got,
    sums,
    sums_got,
    bin_send,
    bin_recv,
    edge_send,
    edge_recv,
    w_send,
    w_recv,
    s_send,
    s_recv,
    r_send,
    r_recv,
    z_send,
    z_recv,
    load_sem,
    start_sem,
):
    loads = [
        pltpu.make_async_copy(far, near, load_sem.at[k])
        for k, (far, near) in enumerate(zip(far_refs, near_refs))
    ]
    for load in loads:
        load.start()
    (
        bins_ref,
        ant_ref,
        code_ref,
        bins_table_ref,
        bins_twid_ref,
        cols_table_ref,
        left_ref,
        twid_ref,
        right_table_ref,
    ) = near_refs
    tmpl_local, run_rows, run_cols, _ = code_ref.shape
    starts_load = pltpu.make_async_copy(far_refs[2].at[:, :, 0, :], start_ref, start_sem)
    starts_load.start()
    code_flat = code_ref.reshape(tmpl_local, NQ, LANES)
    pieces = edge.shape[3]
    per = NQ // SFT_DEV
    block_rows = NQ // owners
    my_tm = lax.axis_index("tm")
    my_band = lax.axis_index("band")
    me = my_tm * band_size + my_band

    def place(rank):
        return {"tm": rank // band_size, "band": rank % band_size}

    def peers(body):
        def step(d, carry):
            body((me + d) % owners)
            return carry

        if owners <= SFT_DEV:
            for d in far_first(owners):
                body((me + d) % owners)
        else:
            lax.fori_loop(1, owners, step, 0)

    def remote(src, dst, send, recv, rank):
        return pltpu.make_async_remote_copy(
            src_ref=src,
            dst_ref=dst,
            send_sem=send,
            recv_sem=recv,
            device_id=place(rank),
            device_id_type=MESH,
        )

    barrier = pltpu.get_barrier_semaphore()
    peers(
        lambda rank: pl.semaphore_signal(
            barrier, inc=1, device_id=place(rank), device_id_type=MESH
        )
    )

    loads[0].wait()
    for e in range(band_size):
        for side in range(2):
            row = SFT_DEV * e + (SFT_DEV - 1 if side == 0 else 0)
            for c in range(2):
                for k in range(pieces):
                    edge[e, side, c, k : k + 1, :] = bins_ref[
                        c, row : row + 1, k * LANES : (k + 1) * LANES
                    ]

    @pl.when(me == 0)
    def _():
        halo[0] = jnp.zeros(halo.shape[1:], jnp.float32)

    @pl.when(me == owners - 1)
    def _():
        halo[1] = jnp.zeros(halo.shape[1:], jnp.float32)

    def blocked(value):
        return value.reshape(owners, block_rows, LANES)

    sums[...] = jnp.zeros_like(sums)
    loads[1].wait()
    for t in range(tmpl_local):
        wts = []
        for w in range(2):
            value = grid_to_time(lambda i: ant_ref[t, w, pl.ds(i, per, stride=SFT_DEV), :])
            w_out[t, :, w] = blocked(value)
            wts.append(value)
        wa, wb = wts
        for k, product in enumerate((wa * wa, wb * wb, wa * wb)):
            sums[3 * t + k : 3 * t + k + 1, :] = jnp.sum(product, axis=0, keepdims=True)
        w_got[t, me] = w_out[t, me]
    sums_got[me] = sums[...]

    pl.semaphore_wait(barrier, owners - 1)

    def bins_rows(band):
        return pl.ds(pl.multiple_of(SFT_DEV * band, SFT_DEV), SFT_DEV)

    def bins_copy(d):
        band = (my_band + d) % band_size
        return remote(
            bins_ref.at[:, bins_rows(band), :],
            grid.at[my_band],
            bin_send.at[band],
            bin_recv.at[my_band],
            my_tm * band_size + band,
        )

    def bins_arrival(d):
        band = (my_band + d) % band_size
        return remote(
            bins_ref.at[:, bins_rows(band), :],
            grid.at[band],
            bin_send.at[band],
            bin_recv.at[band],
            my_tm * band_size + band,
        )

    for d in range(1, band_size):
        bins_copy(d).start()

    def edge_target(e, side):
        return my_tm * band_size + e + (1 if side == 0 else -1)

    def edge_copy(e, side):
        return remote(
            edge.at[e, side],
            halo.at[side, my_band],
            edge_send.at[e, side],
            edge_recv.at[side, my_band],
            edge_target(e, side),
        )

    def edge_is_sent(e, side):
        rank = edge_target(e, side)
        return jnp.logical_and(rank != me, jnp.logical_and(rank >= 0, rank < owners))

    for e in range(band_size):
        for side in range(2):

            @pl.when(edge_is_sent(e, side))
            def _():
                edge_copy(e, side).start()

            @pl.when(edge_target(e, side) == me)
            def _():
                halo[side, my_band] = edge[e, side]

    grid[my_band] = bins_ref[:, bins_rows(my_band), :]

    for t in range(tmpl_local):

        def send_w(rank):
            remote(
                w_out.at[t, rank], w_got.at[t, me], w_send.at[t, rank], w_recv.at[t, me], rank
            ).start()

        peers(send_w)

    peers(
        lambda rank: remote(
            sums, sums_got.at[me], s_send.at[rank], s_recv.at[me], rank
        ).start()
    )

    loads[2].wait()
    for t in range(tmpl_local):
        value = grid_to_time(lambda i: code_flat[t, pl.ds(i, per, stride=SFT_DEV), :])
        code_t[t] = value.reshape(SFT_DEV, per, LANES)
    starts_load.wait()
    for load in loads[3:]:
        load.wait()

    for d in range(1, band_size):
        bins_arrival(d).wait_recv()
    for side in range(2):
        source = (me - 1 if side == 0 else me + 1) // band_size

        @pl.when(jnp.logical_and(me > 0 if side == 0 else me < owners - 1, source != my_tm))
        def _():
            for band in range(band_size):
                remote(
                    edge.at[0, side],
                    halo.at[side, band],
                    edge_send.at[0, side],
                    edge_recv.at[side, band],
                    source * band_size + band,
                ).wait_recv()

        @pl.when(jnp.logical_and(me > 0 if side == 0 else me < owners - 1, source == my_tm))
        def _():
            for d in range(1, band_size):
                band = (my_band + d) % band_size
                remote(
                    edge.at[0, side],
                    halo.at[side, band],
                    edge_send.at[0, side],
                    edge_recv.at[side, band],
                    my_tm * band_size + band,
                ).wait_recv()

    sub = lax.broadcasted_iota(jnp.int32, (SFT_DEV, LANES), 0)
    main_rows, rim_rows = [], []
    for c in range(2):
        for band in range(band_size):
            for k in range(pieces):
                main_rows.append(grid[band, c, :, k * LANES : (k + 1) * LANES])
                first = jnp.broadcast_to(halo[1, band, c, k : k + 1, :], (SFT_DEV, LANES))
                final = jnp.broadcast_to(halo[0, band, c, k : k + 1, :], (SFT_DEV, LANES))
                rim_rows.append(
                    jnp.where(sub == 0, first, jnp.where(sub == SFT_DEV - 1, final, 0.0))
                )
    turned = jnp.concatenate(
        [
            jnp.transpose(jnp.concatenate(main_rows, axis=0)),
            jnp.transpose(jnp.concatenate(rim_rows, axis=0)),
        ],
        axis=0,
    )
    mixed = dot3(split2(turned), split2(bins_table_ref[...]))
    halves = []
    for h in range(2):
        real = mixed[h * LANES : (h + 1) * LANES, :LANES]
        imag = mixed[h * LANES : (h + 1) * LANES, LANES:]
        cos_part, sin_part = bins_twid_ref[0], bins_twid_ref[1]
        halves.append(
            jnp.concatenate(
                [real * cos_part - imag * sin_part, real * sin_part + imag * cos_part], axis=0
            )
        )
    series = dot3(
        split2(cols_table_ref[...]), split2(jnp.concatenate(halves, axis=1))
    )
    for c in range(2):
        for h in range(2):
            part = series[c * NQ : (c + 1) * NQ, h * LANES : (h + 1) * LANES]
            blocks = swap_blocks([part[i * per : (i + 1) * per] for i in range(SFT_DEV)])
            if h == 0:
                for s in range(SFT_DEV):
                    buf[pl.ds(2 * per * (s + 1) + c, per, stride=2), :] = blocks[s]
            else:
                buf[pl.ds(c, per, stride=2), :] = blocks[SFT_DEV - 1]
                buf[pl.ds(2 * per * (SFT_DEV + 1) + c, per, stride=2), :] = blocks[0]

    lane = lax.broadcasted_iota(jnp.int32, (8, LANES), 1)
    share = owners // SFT_DEV
    for t in range(tmpl_local):
        for d in far_first(SFT_DEV) + [0]:
            sft = (me // share + d) % SFT_DEV
            base = d * 8 * run_rows
            for r in range(run_rows):
                offset = (start_ref[t, r, NP * sft] >> 3) - MAXD
                start = offset + (RUN * r + NB - 1) + NB * sft
                shift = start & (LANES - 1)
                held = buf[pl.ds(2 * (start >> 7), 8), :]
                rolled = pltpu.roll(held, LANES - shift, 1)
                below = pltpu.roll(rolled, 6, 0)
                seg[base + 8 * r : base + 8 * r + 8, :] = jnp.where(
                    lane < LANES - shift, rolled, below
                )
            coeffs = []
            for r in range(2):
                code = code_t[t, sft, pl.ds(r, run_rows, stride=2), :]
                coeffs.append(
                    lagrange((code & (NFRAC - 1)).astype(jnp.float32) * (1.0 / NFRAC))
                )
            for c in range(2):
                lines = [seg[pl.ds(base + 2 * r + c, run_rows, stride=8), :] for r in range(3)]
                moved = [lines] + [
                    [pltpu.roll(item, LANES - k, 1) for item in lines] for k in range(1, 4)
                ]
                for r in range(2):
                    total = coeffs[r][0] * moved[0][r]
                    for k in range(1, 4):
                        total = total + coeffs[r][k] * jnp.where(
                            lane < LANES - k, moved[k][r], moved[k][r + 1]
                        )
                    line[d, c, pl.ds(r, run_rows, stride=2), :] = total
                r_out[t, pl.ds(sft * share, share), c] = line[d, c].reshape(
                    share, block_rows, LANES
                )

            def send_r(k, carry):
                rank = sft * share + k

                @pl.when(rank != me)
                def _():
                    remote(
                        r_out.at[t, rank],
                        r_got.at[t, me],
                        r_send.at[t, rank],
                        r_recv.at[t, me],
                        rank,
                    ).start()

                return carry

            lax.fori_loop(0, share, send_r, 0)
        r_got[t, me] = r_out[t, me]

    at = lax.broadcasted_iota(jnp.int32, (1, LANES), 1) * me

    def advanced(table, modulus):
        angle = at.astype(jnp.float32) * (2.0 * math.pi / modulus)
        cos_step, sin_step = jnp.cos(angle), jnp.sin(angle)
        cos_base, sin_base = table[0], table[1]
        return (
            cos_base * cos_step - sin_base * sin_step,
            sin_base * cos_step + cos_base * sin_step,
        )

    cos_left, sin_left = advanced(left_ref, NQ * owners)
    parts = [[cos_left, sin_left], [-sin_left, cos_left]]
    for i in range(2):
        for j in range(2):
            spot = (slice(i * NQ, (i + 1) * NQ), slice(j * NQ, (j + 1) * NQ))
            left_hi[spot], left_lo[spot] = split2(parts[i][j])
    right_hi[...], right_lo[...] = split2(right_table_ref[...])
    cos_part, sin_part = advanced(twid_ref, sample_total)
    twid[0] = cos_part
    twid[1] = -sin_part

    def arrival(out, got, send, recv, t, rank):
        return remote(out.at[t, rank], got.at[t, rank], send.at[t, rank], recv.at[t, rank], rank)

    for t in range(tmpl_local):
        peers(lambda rank: arrival(w_out, w_got, w_send, w_recv, t, rank).wait())
        peers(lambda rank: arrival(r_out, r_got, r_send, r_recv, t, rank).wait())
        for w in range(2):
            real = [r_got[t, i, 0] * w_got[t, i, w] for i in range(owners)]
            imag = [r_got[t, i, 1] * w_got[t, i, w] for i in range(owners)]
            real, imag = owner_dft(real, imag)
            for i in range(owners):
                z_out[t, i, 2 * w] = real[i]
                z_out[t, i, 2 * w + 1] = imag[i]

        def send_z(rank):
            remote(
                z_out.at[t, rank], z_got.at[t, me], z_send.at[t, rank], z_recv.at[t, me], rank
            ).start()

        peers(send_z)
        z_got[t, me] = z_out[t, me]

    def sums_arrival(rank):
        remote(sums, sums_got.at[rank], s_send.at[rank], s_recv.at[rank], rank).wait()

    peers(sums_arrival)
    total = jnp.sum(sums_got[...], axis=0)
    total = jnp.sum(total, axis=1, keepdims=True) / sample_total
    norm = 1.0 / math.sqrt(sample_total)
    for t in range(tmpl_local):
        peers(lambda rank: arrival(z_out, z_got, z_send, z_recv, t, rank).wait())
        value = jnp.concatenate(
            [
                jnp.concatenate(
                    [z_got[t, :, 2 * w + c].reshape(NQ, LANES) for c in range(2)], axis=0
                )
                for w in range(2)
            ],
            axis=1,
        )
        mixed = dot3((left_hi[...], left_lo[...]), split2(value))
        lines = []
        for w in range(2):
            real = mixed[:NQ, w * LANES : (w + 1) * LANES]
            imag = mixed[NQ:, w * LANES : (w + 1) * LANES]
            cos_part, sin_part = twid[0], twid[1]
            lines.append(
                jnp.concatenate(
                    [real * cos_part - imag * sin_part, real * sin_part + imag * cos_part], axis=1
                )
            )
        spectra = dot3(
            split2(jnp.concatenate(lines, axis=0)), (right_hi[...], right_lo[...])
        ) * norm
        a_real, a_imag = spectra[:NQ, :LANES], spectra[:NQ, LANES:]
        b_real, b_imag = spectra[NQ:, :LANES], spectra[NQ:, LANES:]
        power_a = total[3 * t : 3 * t + 1] + stat_eps
        power_b = total[3 * t + 1 : 3 * t + 2] + stat_eps
        cross_ab = total[3 * t + 2 : 3 * t + 3]
        det = jnp.maximum(
            power_a * power_b - cross_ab * cross_ab, floor_share * power_a * power_b
        )
        stat = (
            power_b * (a_real * a_real + a_imag * a_imag)
            + power_a * (b_real * b_real + b_imag * b_imag)
            - 2.0 * cross_ab * (a_real * b_real + a_imag * b_imag)
        ) / det
        blocks = swap_blocks([stat[i * per : (i + 1) * per] for i in range(SFT_DEV)])
        for j, block in enumerate(blocks):
            out_ref[t, j * per : (j + 1) * per, :] = block

    for d in range(1, band_size):
        bins_copy(d).wait_send()
    for e in range(band_size):
        for side in range(2):

            @pl.when(edge_is_sent(e, side))
            def _():
                edge_copy(e, side).wait_send()


def turns(product, modulus):
    angles = 2.0 * np.pi / modulus * (product % modulus)
    return np.cos(angles), np.sin(angles)


def constant_tables():
    per = NQ // SFT_DEV
    at = np.arange(LANES)
    bin_cos, bin_sin = turns(np.arange(NP)[:, None] * np.arange(NP)[None, :], NP)
    same = np.eye(SFT_DEV)
    wide = [
        np.einsum("kp,st->kstp", part, same).reshape(LANES, LANES) for part in (bin_cos, bin_sin)
    ]
    bins = np.block([[wide[0], wide[1]], [-wide[1], wide[0]]])
    bins_twid = np.stack(turns(at[:, None] * (at % NP)[None, :], NB))
    col_order = at // per + SFT_DEV * (at % per)
    col_cos, col_sin = turns(col_order[:, None] * at[None, :], NQ)
    cols = np.block([[col_cos, -col_sin], [col_sin, col_cos]]) / math.sqrt(NB)
    fine = at // NP + SFT_DEV * (at % NP)
    fine_cos, fine_sin = turns(at[:, None] * fine[None, :], LANES)
    right = np.block([[fine_cos, -fine_sin], [fine_sin, fine_cos]])
    left = np.stack(turns(col_order[:, None] * at[None, :], NQ))
    twid = np.stack(turns(col_order[:, None] * at[None, :], NQ * LANES))
    tables = (bins, bins_twid, cols, left, twid, right)
    return tuple(jnp.asarray(table.astype(np.float32)) for table in tables)


def per_device(sft_bins, delay_code, antenna):
    band_size = lax.axis_size("band")
    owners = lax.axis_size("tm") * band_size
    sample_total = SFT_DEV * owners * NB
    tmpl_local = delay_code.shape[0]
    run_cols = RUN // NP
    runs_down = NQ // run_cols
    run_count = SFT_DEV * runs_down
    per = NQ // SFT_DEV
    code = delay_code.reshape(tmpl_local, runs_down, run_cols, LANES)
    operands = tuple(
        pltpu.with_memory_space_constraint(item, pltpu.HBM)
        for item in (sft_bins, antenna, code) + constant_tables()
    )
    bin_width = sft_bins.shape[2]
    pieces = bin_width // LANES
    block_rows = NQ // owners
    f32 = jnp.float32
    dma = pltpu.SemaphoreType.DMA
    count = len(operands)

    def kernel(*refs):
        near = refs[count + 1 : 2 * count + 1]
        search_kernel(
            band_size,
            owners,
            sample_total,
            refs[:count],
            refs[count],
            near,
            *refs[2 * count + 1 :],
        )

    out = pl.pallas_call(
        kernel,
        out_shape=pltpu.VMEM((tmpl_local, NQ, LANES), f32),
        in_specs=[pl.BlockSpec(memory_space=pltpu.HBM)] * count,
        out_specs=pl.BlockSpec(memory_space=pltpu.VMEM),
        scratch_shapes=[pltpu.VMEM(item.shape, item.dtype) for item in operands]
        + [
            pltpu.SMEM((tmpl_local, runs_down, LANES), jnp.int32),
        ]
        + [pltpu.VMEM((2 * NQ, 2 * NQ), jnp.bfloat16)] * 4
        + [
            pltpu.VMEM((2, NQ, LANES), f32),
            pltpu.VMEM((band_size, 2, SFT_DEV, bin_width), f32),
            pltpu.VMEM((band_size, 2, 2, pieces, LANES), f32),
            pltpu.VMEM((2, band_size, 2, pieces, LANES), f32),
            pltpu.VMEM((2 * per * (SFT_DEV + 2), LANES), f32),
            pltpu.VMEM((8 * run_count, LANES), f32),
            pltpu.VMEM((tmpl_local, SFT_DEV, per, LANES), jnp.int32),
            pltpu.VMEM((SFT_DEV, 2, per, LANES), f32),
        ]
        + [pltpu.VMEM((tmpl_local, owners, 2, block_rows, LANES), f32)] * 4
        + [pltpu.VMEM((tmpl_local, owners, 4, block_rows, LANES), f32)] * 2
        + [
            pltpu.VMEM((8, LANES), f32),
            pltpu.VMEM((owners, 8, LANES), f32),
            dma((band_size,)),
            dma((band_size,)),
            dma((band_size, 2)),
            dma((2, band_size)),
            dma((tmpl_local, owners)),
            dma((tmpl_local, owners)),
            dma((owners,)),
            dma((owners,)),
        ]
        + [dma((tmpl_local, owners))] * 4
        + [dma((count,)), dma],
        compiler_params=pltpu.CompilerParams(
            collective_id=0, has_side_effects=True, vmem_limit_bytes=48 * 1024 * 1024
        ),
    )(*operands)
    return out[:, :, None, :]


def solution(mesh):
    in_specs = (
        P(None, ("groups", "tm"), "band"),
        P(("groups", "tmpl"), None, ("tm", "band")),
        P(("groups", "tmpl"), None, None, ("tm", "band")),
    )
    out_specs = P(("groups", "tmpl"), None, ("tm", "band"), None)
    return jax.shard_map(
        per_device, mesh=mesh, in_specs=in_specs, out_specs=out_specs, check_vma=False
    )
```

```python
import functools
import math

import jax
import jax.numpy as jnp
import numpy as np
from jax import lax
from jax.experimental import pallas as pl
from jax.experimental.pallas import tpu as pltpu
from jax.sharding import PartitionSpec as P

NB = 2048
NQ = 128
NP = 16
SFT_DEV = 8
MAXD = 1000
NFRAC = 8
RUN = 256
LANES = 128

stat_eps = 1e-06
floor_share = 0.5
MESH = pl.DeviceIdType.MESH


def lagrange(fraction):
    return (
        -fraction * (fraction - 1.0) * (fraction - 2.0) / 6.0,
        (fraction + 1.0) * (fraction - 1.0) * (fraction - 2.0) / 2.0,
        -(fraction + 1.0) * fraction * (fraction - 2.0) / 2.0,
        (fraction + 1.0) * fraction * (fraction - 1.0) / 6.0,
    )


def split2(value):
    high = value.astype(jnp.bfloat16)
    return high, (value - high.astype(jnp.float32)).astype(jnp.bfloat16)


def dot3(lhs, rhs):
    lhs_hi, lhs_lo = lhs
    rhs_hi, rhs_lo = rhs
    dot = functools.partial(jnp.dot, preferred_element_type=jnp.float32)
    return dot(lhs_hi, rhs_hi) + (dot(lhs_hi, rhs_lo) + dot(lhs_lo, rhs_hi))


def swap_blocks(blocks):
    count = len(blocks)
    width = LANES // count
    blocks = list(blocks)
    lane_block = lax.broadcasted_iota(jnp.int32, blocks[0].shape, 1) // width
    half = count // 2
    while half:
        keep = (lane_block & half) == 0
        for i in range(count):
            if i & half == 0:
                low, high = blocks[i], blocks[i + half]
                blocks[i] = jnp.where(keep, low, pltpu.roll(high, half * width, 1))
                blocks[i + half] = jnp.where(
                    keep, pltpu.roll(low, LANES - half * width, 1), high
                )
        half //= 2
    return blocks


def grid_to_time(plane):
    return jnp.concatenate(swap_blocks([plane(i) for i in range(SFT_DEV)]), axis=0)


def owner_dft(real, imag):
    count = len(real)
    if count == 1:
        return real, imag
    half = count // 2
    sum_real = [real[k] + real[k + half] for k in range(half)]
    sum_imag = [imag[k] + imag[k + half] for k in range(half)]
    dif_real, dif_imag = [], []
    for k in range(half):
        d_real, d_imag = real[k] - real[k + half], imag[k] - imag[k + half]
        if k == 0:
            dif_real.append(d_real)
            dif_imag.append(d_imag)
        elif 2 * k == half:
            dif_real.append(d_imag)
            dif_imag.append(-d_real)
        else:
            cos_part = math.cos(2.0 * math.pi * k / count)
            sin_part = math.sin(2.0 * math.pi * k / count)
            dif_real.append(d_real * cos_part + d_imag * sin_part)
            dif_imag.append(d_imag * cos_part - d_real * sin_part)
    even = owner_dft(sum_real, sum_imag)
    odd = owner_dft(dif_real, dif_imag)
    out_real, out_imag = [], []
    for k in range(half):
        out_real += [even[0][k], odd[0][k]]
        out_imag += [even[1][k], odd[1][k]]
    return out_real, out_imag


def search_kernel(
    band_size,
    owners,
    sample_total,
    far_refs,
    out_ref,
    near_refs,
    start_ref,
    left_hi,
    left_lo,
    right_hi,
    right_lo,
    twid,
    grid,
    edge,
    halo,
    buf,
    seg,
    code_t,
    line,
    w_out,
    w_got,
    r_out,
    r_got,
    z_out,
    z_got,
    sums,
    sums_got,
    bin_send,
    bin_recv,
    edge_send,
    edge_recv,
    w_send,
    w_recv,
    s_send,
    s_recv,
    r_send,
    r_recv,
    z_send,
    z_recv,
    load_sem,
    start_sem,
):
    loads = [
        pltpu.make_async_copy(far, near, load_sem.at[k])
        for k, (far, near) in enumerate(zip(far_refs, near_refs))
    ]
    for load in loads:
        load.start()
    (
        bins_ref,
        ant_ref,
        code_ref,
        bins_table_ref,
        bins_twid_ref,
        cols_table_ref,
        left_ref,
        twid_ref,
        right_table_ref,
    ) = near_refs
    tmpl_local, run_rows, run_cols, _ = code_ref.shape
    starts_load = pltpu.make_async_copy(far_refs[2].at[:, :, 0, :], start_ref, start_sem)
    starts_load.start()
    code_flat = code_ref.reshape(tmpl_local, NQ, LANES)
    pieces = edge.shape[3]
    per = NQ // SFT_DEV
    block_rows = NQ // owners
    my_tm = lax.axis_index("tm")
    my_band = lax.axis_index("band")
    me = my_tm * band_size + my_band

    def place(rank):
        return {"tm": rank // band_size, "band": rank % band_size}

    def peers(body):
        def step(d, carry):
            body((me + d) % owners)
            return carry

        if owners <= SFT_DEV:
            for d in range(1, owners):
                body((me + d) % owners)
        else:
            lax.fori_loop(1, owners, step, 0)

    def remote(src, dst, send, recv, rank):
        return pltpu.make_async_remote_copy(
            src_ref=src,
            dst_ref=dst,
            send_sem=send,
            recv_sem=recv,
            device_id=place(rank),
            device_id_type=MESH,
        )

    barrier = pltpu.get_barrier_semaphore()
    peers(
        lambda rank: pl.semaphore_signal(
            barrier, inc=1, device_id=place(rank), device_id_type=MESH
        )
    )

    loads[0].wait()
    for e in range(band_size):
        for side in range(2):
            row = SFT_DEV * e + (SFT_DEV - 1 if side == 0 else 0)
            for c in range(2):
                for k in range(pieces):
                    edge[e, side, c, k : k + 1, :] = bins_ref[
                        c, row : row + 1, k * LANES : (k + 1) * LANES
                    ]

    @pl.when(me == 0)
    def _():
        halo[0] = jnp.zeros(halo.shape[1:], jnp.float32)

    @pl.when(me == owners - 1)
    def _():
        halo[1] = jnp.zeros(halo.shape[1:], jnp.float32)

    def blocked(value):
        return value.reshape(owners, block_rows, LANES)

    sums[...] = jnp.zeros_like(sums)
    loads[1].wait()
    for t in range(tmpl_local):
        wts = []
        for w in range(2):
            value = grid_to_time(lambda i: ant_ref[t, w, pl.ds(i, per, stride=SFT_DEV), :])
            w_out[t, :, w] = blocked(value)
            wts.append(value)
        wa, wb = wts
        for k, product in enumerate((wa * wa, wb * wb, wa * wb)):
            sums[3 * t + k : 3 * t + k + 1, :] = jnp.sum(product, axis=0, keepdims=True)
        w_got[t, me] = w_out[t, me]
    sums_got[me] = sums[...]

    pl.semaphore_wait(barrier, owners - 1)

    def bins_rows(band):
        return pl.ds(pl.multiple_of(SFT_DEV * band, SFT_DEV), SFT_DEV)

    def bins_copy(d):
        band = (my_band + d) % band_size
        return remote(
            bins_ref.at[:, bins_rows(band), :],
            grid.at[my_band],
            bin_send.at[band],
            bin_recv.at[my_band],
            my_tm * band_size + band,
        )

    def bins_arrival(d):
        band = (my_band + d) % band_size
        return remote(
            bins_ref.at[:, bins_rows(band), :],
            grid.at[band],
            bin_send.at[band],
            bin_recv.at[band],
            my_tm * band_size + band,
        )

    for d in range(1, band_size):
        bins_copy(d).start()

    def edge_target(e, side):
        return my_tm * band_size + e + (1 if side == 0 else -1)

    def edge_copy(e, side):
        return remote(
            edge.at[e, side],
            halo.at[side, my_band],
            edge_send.at[e, side],
            edge_recv.at[side, my_band],
            edge_target(e, side),
        )

    def edge_is_sent(e, side):
        rank = edge_target(e, side)
        return jnp.logical_and(rank != me, jnp.logical_and(rank >= 0, rank < owners))

    for e in range(band_size):
        for side in range(2):

            @pl.when(edge_is_sent(e, side))
            def _():
                edge_copy(e, side).start()

            @pl.when(edge_target(e, side) == me)
            def _():
                halo[side, my_band] = edge[e, side]

    grid[my_band] = bins_ref[:, bins_rows(my_band), :]

    for t in range(tmpl_local):

        def send_w(rank):
            remote(
                w_out.at[t, rank], w_got.at[t, me], w_send.at[t, rank], w_recv.at[t, me], rank
            ).start()

        peers(send_w)

    peers(
        lambda rank: remote(
            sums, sums_got.at[me], s_send.at[rank], s_recv.at[me], rank
        ).start()
    )

    loads[2].wait()
    for t in range(tmpl_local):
        value = grid_to_time(lambda i: code_flat[t, pl.ds(i, per, stride=SFT_DEV), :])
        code_t[t] = value.reshape(SFT_DEV, per, LANES)
    starts_load.wait()
    for load in loads[3:]:
        load.wait()

    for d in range(1, band_size):
        bins_arrival(d).wait_recv()
    for side in range(2):
        source = (me - 1 if side == 0 else me + 1) // band_size

        @pl.when(jnp.logical_and(me > 0 if side == 0 else me < owners - 1, source != my_tm))
        def _():
            for band in range(band_size):
                remote(
                    edge.at[0, side],
                    halo.at[side, band],
                    edge_send.at[0, side],
                    edge_recv.at[side, band],
                    source * band_size + band,
                ).wait_recv()

        @pl.when(jnp.logical_and(me > 0 if side == 0 else me < owners - 1, source == my_tm))
        def _():
            for d in range(1, band_size):
                band = (my_band + d) % band_size
                remote(
                    edge.at[0, side],
                    halo.at[side, band],
                    edge_send.at[0, side],
                    edge_recv.at[side, band],
                    my_tm * band_size + band,
                ).wait_recv()

    sub = lax.broadcasted_iota(jnp.int32, (SFT_DEV, LANES), 0)
    main_rows, rim_rows = [], []
    for c in range(2):
        for band in range(band_size):
            for k in range(pieces):
                main_rows.append(grid[band, c, :, k * LANES : (k + 1) * LANES])
                first = jnp.broadcast_to(halo[1, band, c, k : k + 1, :], (SFT_DEV, LANES))
                final = jnp.broadcast_to(halo[0, band, c, k : k + 1, :], (SFT_DEV, LANES))
                rim_rows.append(
                    jnp.where(sub == 0, first, jnp.where(sub == SFT_DEV - 1, final, 0.0))
                )
    turned = jnp.concatenate(
        [
            jnp.transpose(jnp.concatenate(main_rows, axis=0)),
            jnp.transpose(jnp.concatenate(rim_rows, axis=0)),
        ],
        axis=0,
    )
    mixed = dot3(split2(turned), split2(bins_table_ref[...]))
    halves = []
    for h in range(2):
        real = mixed[h * LANES : (h + 1) * LANES, :LANES]
        imag = mixed[h * LANES : (h + 1) * LANES, LANES:]
        cos_part, sin_part = bins_twid_ref[0], bins_twid_ref[1]
        halves.append(
            jnp.concatenate(
                [real * cos_part - imag * sin_part, real * sin_part + imag * cos_part], axis=0
            )
        )
    series = dot3(
        split2(cols_table_ref[...]), split2(jnp.concatenate(halves, axis=1))
    )
    for c in range(2):
        for h in range(2):
            part = series[c * NQ : (c + 1) * NQ, h * LANES : (h + 1) * LANES]
            blocks = swap_blocks([part[i * per : (i + 1) * per] for i in range(SFT_DEV)])
            if h == 0:
                for s in range(SFT_DEV):
                    buf[pl.ds(2 * per * (s + 1) + c, per, stride=2), :] = blocks[s]
            else:
                buf[pl.ds(c, per, stride=2), :] = blocks[SFT_DEV - 1]
                buf[pl.ds(2 * per * (SFT_DEV + 1) + c, per, stride=2), :] = blocks[0]

    lane = lax.broadcasted_iota(jnp.int32, (8, LANES), 1)
    share = owners // SFT_DEV
    for t in range(tmpl_local):
        for d in list(range(1, SFT_DEV)) + [0]:
            sft = (me // share + d) % SFT_DEV
            base = d * 8 * run_rows
            for r in range(run_rows):
                offset = (start_ref[t, r, NP * sft] >> 3) - MAXD
                start = offset + (RUN * r + NB - 1) + NB * sft
                shift = start & (LANES - 1)
                held = buf[pl.ds(2 * (start >> 7), 8), :]
                rolled = pltpu.roll(held, LANES - shift, 1)
                below = pltpu.roll(rolled, 6, 0)
                seg[base + 8 * r : base + 8 * r + 8, :] = jnp.where(
                    lane < LANES - shift, rolled, below
                )
            coeffs = []
            for r in range(2):
                code = code_t[t, sft, pl.ds(r, run_rows, stride=2), :]
                coeffs.append(
                    lagrange((code & (NFRAC - 1)).astype(jnp.float32) * (1.0 / NFRAC))
                )
            for c in range(2):
                lines = [seg[pl.ds(base + 2 * r + c, run_rows, stride=8), :] for r in range(3)]
                moved = [lines] + [
                    [pltpu.roll(item, LANES - k, 1) for item in lines] for k in range(1, 4)
                ]
                for r in range(2):
                    total = coeffs[r][0] * moved[0][r]
                    for k in range(1, 4):
                        total = total + coeffs[r][k] * jnp.where(
                            lane < LANES - k, moved[k][r], moved[k][r + 1]
                        )
                    line[d, c, pl.ds(r, run_rows, stride=2), :] = total
                r_out[t, pl.ds(sft * share, share), c] = line[d, c].reshape(
                    share, block_rows, LANES
                )

            def send_r(k, carry):
                rank = sft * share + k

                @pl.when(rank != me)
                def _():
                    remote(
                        r_out.at[t, rank],
                        r_got.at[t, me],
                        r_send.at[t, rank],
                        r_recv.at[t, me],
                        rank,
                    ).start()

                return carry

            lax.fori_loop(0, share, send_r, 0)
        r_got[t, me] = r_out[t, me]

    at = lax.broadcasted_iota(jnp.int32, (1, LANES), 1) * me

    def advanced(table, modulus):
        angle = at.astype(jnp.float32) * (2.0 * math.pi / modulus)
        cos_step, sin_step = jnp.cos(angle), jnp.sin(angle)
        cos_base, sin_base = table[0], table[1]
        return (
            cos_base * cos_step - sin_base * sin_step,
            sin_base * cos_step + cos_base * sin_step,
        )

    cos_left, sin_left = advanced(left_ref, NQ * owners)
    parts = [[cos_left, sin_left], [-sin_left, cos_left]]
    for i in range(2):
        for j in range(2):
            spot = (slice(i * NQ, (i + 1) * NQ), slice(j * NQ, (j + 1) * NQ))
            left_hi[spot], left_lo[spot] = split2(parts[i][j])
    right_hi[...], right_lo[...] = split2(right_table_ref[...])
    cos_part, sin_part = advanced(twid_ref, sample_total)
    twid[0] = cos_part
    twid[1] = -sin_part

    def arrival(out, got, send, recv, t, rank):
        return remote(out.at[t, rank], got.at[t, rank], send.at[t, rank], recv.at[t, rank], rank)

    for t in range(tmpl_local):
        peers(lambda rank: arrival(w_out, w_got, w_send, w_recv, t, rank).wait_recv())
        peers(lambda rank: arrival(r_out, r_got, r_send, r_recv, t, rank).wait_recv())
        for w in range(2):
            real = [r_got[t, i, 0] * w_got[t, i, w] for i in range(owners)]
            imag = [r_got[t, i, 1] * w_got[t, i, w] for i in range(owners)]
            real, imag = owner_dft(real, imag)
            for i in range(owners):
                z_out[t, i, 2 * w] = real[i]
                z_out[t, i, 2 * w + 1] = imag[i]

        def send_z(rank):
            remote(
                z_out.at[t, rank], z_got.at[t, me], z_send.at[t, rank], z_recv.at[t, me], rank
            ).start()

        peers(send_z)
        z_got[t, me] = z_out[t, me]

    def sums_arrival(rank):
        remote(sums, sums_got.at[rank], s_send.at[rank], s_recv.at[rank], rank).wait_recv()

    peers(sums_arrival)
    total = jnp.sum(sums_got[...], axis=0)
    total = jnp.sum(total, axis=1, keepdims=True) / sample_total
    norm = 1.0 / math.sqrt(sample_total)
    for t in range(tmpl_local):
        peers(lambda rank: arrival(z_out, z_got, z_send, z_recv, t, rank).wait_recv())
        value = jnp.concatenate(
            [
                jnp.concatenate(
                    [z_got[t, :, 2 * w + c].reshape(NQ, LANES) for c in range(2)], axis=0
                )
                for w in range(2)
            ],
            axis=1,
        )
        mixed = dot3((left_hi[...], left_lo[...]), split2(value))
        lines = []
        for w in range(2):
            real = mixed[:NQ, w * LANES : (w + 1) * LANES]
            imag = mixed[NQ:, w * LANES : (w + 1) * LANES]
            cos_part, sin_part = twid[0], twid[1]
            lines.append(
                jnp.concatenate(
                    [real * cos_part - imag * sin_part, real * sin_part + imag * cos_part], axis=1
                )
            )
        spectra = dot3(
            split2(jnp.concatenate(lines, axis=0)), (right_hi[...], right_lo[...])
        ) * norm
        a_real, a_imag = spectra[:NQ, :LANES], spectra[:NQ, LANES:]
        b_real, b_imag = spectra[NQ:, :LANES], spectra[NQ:, LANES:]
        power_a = total[3 * t : 3 * t + 1] + stat_eps
        power_b = total[3 * t + 1 : 3 * t + 2] + stat_eps
        cross_ab = total[3 * t + 2 : 3 * t + 3]
        det = jnp.maximum(
            power_a * power_b - cross_ab * cross_ab, floor_share * power_a * power_b
        )
        stat = (
            power_b * (a_real * a_real + a_imag * a_imag)
            + power_a * (b_real * b_real + b_imag * b_imag)
            - 2.0 * cross_ab * (a_real * b_real + a_imag * b_imag)
        ) / det
        blocks = swap_blocks([stat[i * per : (i + 1) * per] for i in range(SFT_DEV)])
        for j, block in enumerate(blocks):
            out_ref[t, j * per : (j + 1) * per, :] = block

    def departures(rank):
        remote(sums, sums_got.at[rank], s_send.at[rank], s_recv.at[rank], rank).wait_send()
        for t in range(tmpl_local):
            arrival(w_out, w_got, w_send, w_recv, t, rank).wait_send()
            arrival(r_out, r_got, r_send, r_recv, t, rank).wait_send()
            arrival(z_out, z_got, z_send, z_recv, t, rank).wait_send()

    peers(departures)
    for d in range(1, band_size):
        bins_copy(d).wait_send()
    for e in range(band_size):
        for side in range(2):

            @pl.when(edge_is_sent(e, side))
            def _():
                edge_copy(e, side).wait_send()


def turns(product, modulus):
    angles = 2.0 * np.pi / modulus * (product % modulus)
    return np.cos(angles), np.sin(angles)


def constant_tables():
    per = NQ // SFT_DEV
    at = np.arange(LANES)
    bin_cos, bin_sin = turns(np.arange(NP)[:, None] * np.arange(NP)[None, :], NP)
    same = np.eye(SFT_DEV)
    wide = [
        np.einsum("kp,st->kstp", part, same).reshape(LANES, LANES) for part in (bin_cos, bin_sin)
    ]
    bins = np.block([[wide[0], wide[1]], [-wide[1], wide[0]]])
    bins_twid = np.stack(turns(at[:, None] * (at % NP)[None, :], NB))
    col_order = at // per + SFT_DEV * (at % per)
    col_cos, col_sin = turns(col_order[:, None] * at[None, :], NQ)
    cols = np.block([[col_cos, -col_sin], [col_sin, col_cos]]) / math.sqrt(NB)
    fine = at // NP + SFT_DEV * (at % NP)
    fine_cos, fine_sin = turns(at[:, None] * fine[None, :], LANES)
    right = np.block([[fine_cos, -fine_sin], [fine_sin, fine_cos]])
    left = np.stack(turns(col_order[:, None] * at[None, :], NQ))
    twid = np.stack(turns(col_order[:, None] * at[None, :], NQ * LANES))
    tables = (bins, bins_twid, cols, left, twid, right)
    return tuple(jnp.asarray(table.astype(np.float32)) for table in tables)


def per_device(sft_bins, delay_code, antenna):
    band_size = lax.axis_size("band")
    owners = lax.axis_size("tm") * band_size
    sample_total = SFT_DEV * owners * NB
    tmpl_local = delay_code.shape[0]
    run_cols = RUN // NP
    runs_down = NQ // run_cols
    run_count = SFT_DEV * runs_down
    per = NQ // SFT_DEV
    code = delay_code.reshape(tmpl_local, runs_down, run_cols, LANES)
    operands = tuple(
        pltpu.with_memory_space_constraint(item, pltpu.HBM)
        for item in (sft_bins, antenna, code) + constant_tables()
    )
    bin_width = sft_bins.shape[2]
    pieces = bin_width // LANES
    block_rows = NQ // owners
    f32 = jnp.float32
    dma = pltpu.SemaphoreType.DMA
    count = len(operands)

    def kernel(*refs):
        near = refs[count + 1 : 2 * count + 1]
        search_kernel(
            band_size,
            owners,
            sample_total,
            refs[:count],
            refs[count],
            near,
            *refs[2 * count + 1 :],
        )

    out = pl.pallas_call(
        kernel,
        out_shape=pltpu.VMEM((tmpl_local, NQ, LANES), f32),
        in_specs=[pl.BlockSpec(memory_space=pltpu.HBM)] * count,
        out_specs=pl.BlockSpec(memory_space=pltpu.VMEM),
        scratch_shapes=[pltpu.VMEM(item.shape, item.dtype) for item in operands]
        + [
            pltpu.SMEM((tmpl_local, runs_down, LANES), jnp.int32),
        ]
        + [pltpu.VMEM((2 * NQ, 2 * NQ), jnp.bfloat16)] * 4
        + [
            pltpu.VMEM((2, NQ, LANES), f32),
            pltpu.VMEM((band_size, 2, SFT_DEV, bin_width), f32),
            pltpu.VMEM((band_size, 2, 2, pieces, LANES), f32),
            pltpu.VMEM((2, band_size, 2, pieces, LANES), f32),
            pltpu.VMEM((2 * per * (SFT_DEV + 2), LANES), f32),
            pltpu.VMEM((8 * run_count, LANES), f32),
            pltpu.VMEM((tmpl_local, SFT_DEV, per, LANES), jnp.int32),
            pltpu.VMEM((SFT_DEV, 2, per, LANES), f32),
        ]
        + [pltpu.VMEM((tmpl_local, owners, 2, block_rows, LANES), f32)] * 4
        + [pltpu.VMEM((tmpl_local, owners, 4, block_rows, LANES), f32)] * 2
        + [
            pltpu.VMEM((8, LANES), f32),
            pltpu.VMEM((owners, 8, LANES), f32),
            dma((band_size,)),
            dma((band_size,)),
            dma((band_size, 2)),
            dma((2, band_size)),
            dma((tmpl_local, owners)),
            dma((tmpl_local, owners)),
            dma((owners,)),
            dma((owners,)),
        ]
        + [dma((tmpl_local, owners))] * 4
        + [dma((count,)), dma],
        compiler_params=pltpu.CompilerParams(
            collective_id=0, has_side_effects=True, vmem_limit_bytes=48 * 1024 * 1024
        ),
    )(*operands)
    return out[:, :, None, :]


def solution(mesh):
    in_specs = (
        P(None, ("groups", "tm"), "band"),
        P(("groups", "tmpl"), None, ("tm", "band")),
        P(("groups", "tmpl"), None, None, ("tm", "band")),
    )
    out_specs = P(("groups", "tmpl"), None, ("tm", "band"), None)
    return jax.shard_map(
        per_device, mesh=mesh, in_specs=in_specs, out_specs=out_specs, check_vma=False
    )
```

```python
import functools
import math

import jax
import jax.numpy as jnp
import numpy as np
from jax import lax
from jax.experimental import pallas as pl
from jax.experimental.pallas import tpu as pltpu
from jax.sharding import PartitionSpec as P

NB = 2048
NQ = 128
NP = 16
SFT_DEV = 8
MAXD = 1000
NFRAC = 8
RUN = 256
LANES = 128

stat_eps = 1e-06
floor_share = 0.5
MESH = pl.DeviceIdType.MESH


def lagrange(fraction):
    return (
        -fraction * (fraction - 1.0) * (fraction - 2.0) / 6.0,
        (fraction + 1.0) * (fraction - 1.0) * (fraction - 2.0) / 2.0,
        -(fraction + 1.0) * fraction * (fraction - 2.0) / 2.0,
        (fraction + 1.0) * fraction * (fraction - 1.0) / 6.0,
    )


def split2(value):
    high = value.astype(jnp.bfloat16)
    return high, (value - high.astype(jnp.float32)).astype(jnp.bfloat16)


def dot3(lhs, rhs):
    lhs_hi, lhs_lo = lhs
    rhs_hi, rhs_lo = rhs
    dot = functools.partial(jnp.dot, preferred_element_type=jnp.float32)
    return dot(lhs_hi, rhs_hi) + (dot(lhs_hi, rhs_lo) + dot(lhs_lo, rhs_hi))


def swap_blocks(blocks):
    count = len(blocks)
    width = LANES // count
    blocks = list(blocks)
    lane_block = lax.broadcasted_iota(jnp.int32, blocks[0].shape, 1) // width
    half = count // 2
    while half:
        keep = (lane_block & half) == 0
        for i in range(count):
            if i & half == 0:
                low, high = blocks[i], blocks[i + half]
                blocks[i] = jnp.where(keep, low, pltpu.roll(high, half * width, 1))
                blocks[i + half] = jnp.where(
                    keep, pltpu.roll(low, LANES - half * width, 1), high
                )
        half //= 2
    return blocks


def grid_to_time(plane):
    return jnp.concatenate(swap_blocks([plane(i) for i in range(SFT_DEV)]), axis=0)


def owner_dft(real, imag):
    count = len(real)
    if count == 1:
        return real, imag
    half = count // 2
    sum_real = [real[k] + real[k + half] for k in range(half)]
    sum_imag = [imag[k] + imag[k + half] for k in range(half)]
    dif_real, dif_imag = [], []
    for k in range(half):
        d_real, d_imag = real[k] - real[k + half], imag[k] - imag[k + half]
        if k == 0:
            dif_real.append(d_real)
            dif_imag.append(d_imag)
        elif 2 * k == half:
            dif_real.append(d_imag)
            dif_imag.append(-d_real)
        else:
            cos_part = math.cos(2.0 * math.pi * k / count)
            sin_part = math.sin(2.0 * math.pi * k / count)
            dif_real.append(d_real * cos_part + d_imag * sin_part)
            dif_imag.append(d_imag * cos_part - d_real * sin_part)
    even = owner_dft(sum_real, sum_imag)
    odd = owner_dft(dif_real, dif_imag)
    out_real, out_imag = [], []
    for k in range(half):
        out_real += [even[0][k], odd[0][k]]
        out_imag += [even[1][k], odd[1][k]]
    return out_real, out_imag


def search_kernel(
    band_size,
    owners,
    sample_total,
    far_refs,
    out_ref,
    near_refs,
    start_ref,
    left_hi,
    left_lo,
    right_hi,
    right_lo,
    twid,
    grid,
    edge,
    halo,
    buf,
    seg,
    code_t,
    line,
    w_out,
    w_got,
    r_out,
    r_got,
    z_out,
    z_got,
    sums,
    sums_got,
    bin_send,
    bin_recv,
    edge_send,
    edge_recv,
    w_send,
    w_recv,
    s_send,
    s_recv,
    r_send,
    r_recv,
    z_send,
    z_recv,
    load_sem,
    start_sem,
):
    loads = [
        pltpu.make_async_copy(far, near, load_sem.at[k])
        for k, (far, near) in enumerate(zip(far_refs, near_refs))
    ]
    for load in loads:
        load.start()
    (
        bins_ref,
        ant_ref,
        code_ref,
        bins_table_ref,
        bins_twid_ref,
        cols_table_ref,
        left_ref,
        twid_ref,
        right_table_ref,
    ) = near_refs
    tmpl_local, run_rows, run_cols, _ = code_ref.shape
    starts_load = pltpu.make_async_copy(far_refs[2].at[:, :, 0, :], start_ref, start_sem)
    starts_load.start()
    code_flat = code_ref.reshape(tmpl_local, NQ, LANES)
    pieces = edge.shape[3]
    per = NQ // SFT_DEV
    block_rows = NQ // owners
    my_tm = lax.axis_index("tm")
    my_band = lax.axis_index("band")
    me = my_tm * band_size + my_band

    def place(rank):
        return {"tm": rank // band_size, "band": rank % band_size}

    def peers(body):
        def step(d, carry):
            body((me + d) % owners)
            return carry

        if owners <= SFT_DEV:
            for d in range(1, owners):
                body((me + d) % owners)
        else:
            lax.fori_loop(1, owners, step, 0)

    def remote(src, dst, send, recv, rank):
        return pltpu.make_async_remote_copy(
            src_ref=src,
            dst_ref=dst,
            send_sem=send,
            recv_sem=recv,
            device_id=place(rank),
            device_id_type=MESH,
        )

    barrier = pltpu.get_barrier_semaphore()
    peers(
        lambda rank: pl.semaphore_signal(
            barrier, inc=1, device_id=place(rank), device_id_type=MESH
        )
    )

    loads[0].wait()
    for e in range(band_size):
        for side in range(2):
            row = SFT_DEV * e + (SFT_DEV - 1 if side == 0 else 0)
            for c in range(2):
                for k in range(pieces):
                    edge[e, side, c, k : k + 1, :] = bins_ref[
                        c, row : row + 1, k * LANES : (k + 1) * LANES
                    ]

    @pl.when(me == 0)
    def _():
        halo[0] = jnp.zeros(halo.shape[1:], jnp.float32)

    @pl.when(me == owners - 1)
    def _():
        halo[1] = jnp.zeros(halo.shape[1:], jnp.float32)

    def blocked(value):
        return value.reshape(owners, block_rows, LANES)

    sums[...] = jnp.zeros_like(sums)
    loads[1].wait()
    for t in range(tmpl_local):
        wts = []
        for w in range(2):
            value = grid_to_time(lambda i: ant_ref[t, w, pl.ds(i, per, stride=SFT_DEV), :])
            w_out[t, :, w] = blocked(value)
            wts.append(value)
        wa, wb = wts
        for k, product in enumerate((wa * wa, wb * wb, wa * wb)):
            sums[3 * t + k : 3 * t + k + 1, :] = jnp.sum(product, axis=0, keepdims=True)
        w_got[t, me] = w_out[t, me]
    sums_got[me] = sums[...]

    pl.semaphore_wait(barrier, owners - 1)

    def bins_rows(band):
        return pl.ds(pl.multiple_of(SFT_DEV * band, SFT_DEV), SFT_DEV)

    def bins_copy(d):
        band = (my_band + d) % band_size
        return remote(
            bins_ref.at[:, bins_rows(band), :],
            grid.at[my_band],
            bin_send.at[band],
            bin_recv.at[my_band],
            my_tm * band_size + band,
        )

    def bins_arrival(d):
        band = (my_band + d) % band_size
        return remote(
            bins_ref.at[:, bins_rows(band), :],
            grid.at[band],
            bin_send.at[band],
            bin_recv.at[band],
            my_tm * band_size + band,
        )

    for d in range(1, band_size):
        bins_copy(d).start()

    def edge_target(e, side):
        return my_tm * band_size + e + (1 if side == 0 else -1)

    def edge_copy(e, side):
        return remote(
            edge.at[e, side],
            halo.at[side, my_band],
            edge_send.at[e, side],
            edge_recv.at[side, my_band],
            edge_target(e, side),
        )

    def edge_is_sent(e, side):
        rank = edge_target(e, side)
        return jnp.logical_and(rank != me, jnp.logical_and(rank >= 0, rank < owners))

    for e in range(band_size):
        for side in range(2):

            @pl.when(edge_is_sent(e, side))
            def _():
                edge_copy(e, side).start()

            @pl.when(edge_target(e, side) == me)
            def _():
                halo[side, my_band] = edge[e, side]

    grid[my_band] = bins_ref[:, bins_rows(my_band), :]

    def w_copy(t, w, rank, origin):
        return remote(
            w_out.at[t, rank, w],
            w_got.at[t, origin, w],
            w_send.at[t, w, rank],
            w_recv.at[t, w, origin],
            rank,
        )

    pairs = [(t, w) for t in range(tmpl_local) for w in range(2)]
    for t, w in pairs[:-1]:
        peers(lambda rank: w_copy(t, w, rank, me).start())

    peers(
        lambda rank: remote(
            sums, sums_got.at[me], s_send.at[rank], s_recv.at[me], rank
        ).start()
    )

    loads[2].wait()
    for t in range(tmpl_local):
        value = grid_to_time(lambda i: code_flat[t, pl.ds(i, per, stride=SFT_DEV), :])
        code_t[t] = value.reshape(SFT_DEV, per, LANES)
    starts_load.wait()
    for load in loads[3:]:
        load.wait()

    for d in range(1, band_size):
        bins_arrival(d).wait_recv()
    for side in range(2):
        source = (me - 1 if side == 0 else me + 1) // band_size

        @pl.when(jnp.logical_and(me > 0 if side == 0 else me < owners - 1, source != my_tm))
        def _():
            for band in range(band_size):
                remote(
                    edge.at[0, side],
                    halo.at[side, band],
                    edge_send.at[0, side],
                    edge_recv.at[side, band],
                    source * band_size + band,
                ).wait_recv()

        @pl.when(jnp.logical_and(me > 0 if side == 0 else me < owners - 1, source == my_tm))
        def _():
            for d in range(1, band_size):
                band = (my_band + d) % band_size
                remote(
                    edge.at[0, side],
                    halo.at[side, band],
                    edge_send.at[0, side],
                    edge_recv.at[side, band],
                    my_tm * band_size + band,
                ).wait_recv()

    sub = lax.broadcasted_iota(jnp.int32, (SFT_DEV, LANES), 0)
    main_rows, rim_rows = [], []
    for c in range(2):
        for band in range(band_size):
            for k in range(pieces):
                main_rows.append(grid[band, c, :, k * LANES : (k + 1) * LANES])
                first = jnp.broadcast_to(halo[1, band, c, k : k + 1, :], (SFT_DEV, LANES))
                final = jnp.broadcast_to(halo[0, band, c, k : k + 1, :], (SFT_DEV, LANES))
                rim_rows.append(
                    jnp.where(sub == 0, first, jnp.where(sub == SFT_DEV - 1, final, 0.0))
                )
    turned = jnp.concatenate(
        [
            jnp.transpose(jnp.concatenate(main_rows, axis=0)),
            jnp.transpose(jnp.concatenate(rim_rows, axis=0)),
        ],
        axis=0,
    )
    mixed = dot3(split2(turned), split2(bins_table_ref[...]))
    halves = []
    for h in range(2):
        real = mixed[h * LANES : (h + 1) * LANES, :LANES]
        imag = mixed[h * LANES : (h + 1) * LANES, LANES:]
        cos_part, sin_part = bins_twid_ref[0], bins_twid_ref[1]
        halves.append(
            jnp.concatenate(
                [real * cos_part - imag * sin_part, real * sin_part + imag * cos_part], axis=0
            )
        )
    series = dot3(
        split2(cols_table_ref[...]), split2(jnp.concatenate(halves, axis=1))
    )
    for c in range(2):
        for h in range(2):
            part = series[c * NQ : (c + 1) * NQ, h * LANES : (h + 1) * LANES]
            blocks = swap_blocks([part[i * per : (i + 1) * per] for i in range(SFT_DEV)])
            if h == 0:
                for s in range(SFT_DEV):
                    buf[pl.ds(2 * per * (s + 1) + c, per, stride=2), :] = blocks[s]
            else:
                buf[pl.ds(c, per, stride=2), :] = blocks[SFT_DEV - 1]
                buf[pl.ds(2 * per * (SFT_DEV + 1) + c, per, stride=2), :] = blocks[0]

    lane = lax.broadcasted_iota(jnp.int32, (8, LANES), 1)
    share = owners // SFT_DEV
    for t in range(tmpl_local):
        for d in list(range(1, SFT_DEV)) + [0]:
            sft = (me // share + d) % SFT_DEV
            base = d * 8 * run_rows
            for r in range(run_rows):
                offset = (start_ref[t, r, NP * sft] >> 3) - MAXD
                start = offset + (RUN * r + NB - 1) + NB * sft
                shift = start & (LANES - 1)
                held = buf[pl.ds(2 * (start >> 7), 8), :]
                rolled = pltpu.roll(held, LANES - shift, 1)
                below = pltpu.roll(rolled, 6, 0)
                seg[base + 8 * r : base + 8 * r + 8, :] = jnp.where(
                    lane < LANES - shift, rolled, below
                )
            coeffs = []
            for r in range(2):
                code = code_t[t, sft, pl.ds(r, run_rows, stride=2), :]
                coeffs.append(
                    lagrange((code & (NFRAC - 1)).astype(jnp.float32) * (1.0 / NFRAC))
                )
            for c in range(2):
                lines = [seg[pl.ds(base + 2 * r + c, run_rows, stride=8), :] for r in range(3)]
                moved = [lines] + [
                    [pltpu.roll(item, LANES - k, 1) for item in lines] for k in range(1, 4)
                ]
                for r in range(2):
                    total = coeffs[r][0] * moved[0][r]
                    for k in range(1, 4):
                        total = total + coeffs[r][k] * jnp.where(
                            lane < LANES - k, moved[k][r], moved[k][r + 1]
                        )
                    line[d, c, pl.ds(r, run_rows, stride=2), :] = total
                r_out[t, pl.ds(sft * share, share), c] = line[d, c].reshape(
                    share, block_rows, LANES
                )

            def send_r(k, carry):
                rank = sft * share + k

                @pl.when(rank != me)
                def _():
                    remote(
                        r_out.at[t, rank],
                        r_got.at[t, me],
                        r_send.at[t, rank],
                        r_recv.at[t, me],
                        rank,
                    ).start()

                return carry

            lax.fori_loop(0, share, send_r, 0)
        if t == 0:
            peers(lambda rank: w_copy(*pairs[-1], rank, me).start())
        r_got[t, me] = r_out[t, me]

    at = lax.broadcasted_iota(jnp.int32, (1, LANES), 1) * me

    def advanced(table, modulus):
        angle = at.astype(jnp.float32) * (2.0 * math.pi / modulus)
        cos_step, sin_step = jnp.cos(angle), jnp.sin(angle)
        cos_base, sin_base = table[0], table[1]
        return (
            cos_base * cos_step - sin_base * sin_step,
            sin_base * cos_step + cos_base * sin_step,
        )

    cos_left, sin_left = advanced(left_ref, NQ * owners)
    parts = [[cos_left, sin_left], [-sin_left, cos_left]]
    for i in range(2):
        for j in range(2):
            spot = (slice(i * NQ, (i + 1) * NQ), slice(j * NQ, (j + 1) * NQ))
            left_hi[spot], left_lo[spot] = split2(parts[i][j])
    right_hi[...], right_lo[...] = split2(right_table_ref[...] * (1.0 / math.sqrt(sample_total)))
    cos_part, sin_part = advanced(twid_ref, sample_total)
    twid[0] = cos_part
    twid[1] = -sin_part

    def arrival(out, got, send, recv, t, rank):
        return remote(out.at[t, rank], got.at[t, rank], send.at[t, rank], recv.at[t, rank], rank)

    for t in range(tmpl_local):
        for w in range(2):
            peers(lambda rank: w_copy(t, w, rank, rank).wait_recv())
        peers(lambda rank: arrival(r_out, r_got, r_send, r_recv, t, rank).wait_recv())
        for w in range(2):
            real = [r_got[t, i, 0] * w_got[t, i, w] for i in range(owners)]
            imag = [r_got[t, i, 1] * w_got[t, i, w] for i in range(owners)]
            real, imag = owner_dft(real, imag)
            for i in range(owners):
                z_out[t, i, 2 * w] = real[i]
                z_out[t, i, 2 * w + 1] = imag[i]

        def send_z(rank):
            remote(
                z_out.at[t, rank], z_got.at[t, me], z_send.at[t, rank], z_recv.at[t, me], rank
            ).start()

        peers(send_z)
        z_got[t, me] = z_out[t, me]

    def sums_arrival(rank):
        remote(sums, sums_got.at[rank], s_send.at[rank], s_recv.at[rank], rank).wait_recv()

    peers(sums_arrival)
    total = jnp.sum(sums_got[...], axis=0)
    total = jnp.sum(total, axis=1, keepdims=True) / sample_total
    for t in range(tmpl_local):
        peers(lambda rank: arrival(z_out, z_got, z_send, z_recv, t, rank).wait_recv())
        value = jnp.concatenate(
            [
                jnp.concatenate(
                    [z_got[t, :, 2 * w + c].reshape(NQ, LANES) for c in range(2)], axis=0
                )
                for w in range(2)
            ],
            axis=1,
        )
        mixed = dot3((left_hi[...], left_lo[...]), split2(value))
        lines = []
        for w in range(2):
            real = mixed[:NQ, w * LANES : (w + 1) * LANES]
            imag = mixed[NQ:, w * LANES : (w + 1) * LANES]
            cos_part, sin_part = twid[0], twid[1]
            lines.append(
                jnp.concatenate(
                    [real * cos_part - imag * sin_part, real * sin_part + imag * cos_part], axis=1
                )
            )
        spectra = dot3(
            split2(jnp.concatenate(lines, axis=0)), (right_hi[...], right_lo[...])
        )
        a_real, a_imag = spectra[:NQ, :LANES], spectra[:NQ, LANES:]
        b_real, b_imag = spectra[NQ:, :LANES], spectra[NQ:, LANES:]
        power_a = total[3 * t : 3 * t + 1] + stat_eps
        power_b = total[3 * t + 1 : 3 * t + 2] + stat_eps
        cross_ab = total[3 * t + 2 : 3 * t + 3]
        det = jnp.maximum(
            power_a * power_b - cross_ab * cross_ab, floor_share * power_a * power_b
        )
        stat = (
            (power_b / det) * (a_real * a_real + a_imag * a_imag)
            + (power_a / det) * (b_real * b_real + b_imag * b_imag)
            - (2.0 * cross_ab / det) * (a_real * b_real + a_imag * b_imag)
        )
        blocks = swap_blocks([stat[i * per : (i + 1) * per] for i in range(SFT_DEV)])
        for j, block in enumerate(blocks):
            out_ref[t, j * per : (j + 1) * per, :] = block

    def departures(rank):
        remote(sums, sums_got.at[rank], s_send.at[rank], s_recv.at[rank], rank).wait_send()
        for t in range(tmpl_local):
            for w in range(2):
                w_copy(t, w, rank, rank).wait_send()
            arrival(r_out, r_got, r_send, r_recv, t, rank).wait_send()
            arrival(z_out, z_got, z_send, z_recv, t, rank).wait_send()

    peers(departures)
    for d in range(1, band_size):
        bins_copy(d).wait_send()
    for e in range(band_size):
        for side in range(2):

            @pl.when(edge_is_sent(e, side))
            def _():
                edge_copy(e, side).wait_send()


def turns(product, modulus):
    angles = 2.0 * np.pi / modulus * (product % modulus)
    return np.cos(angles), np.sin(angles)


def constant_tables():
    per = NQ // SFT_DEV
    at = np.arange(LANES)
    bin_cos, bin_sin = turns(np.arange(NP)[:, None] * np.arange(NP)[None, :], NP)
    same = np.eye(SFT_DEV)
    wide = [
        np.einsum("kp,st->kstp", part, same).reshape(LANES, LANES) for part in (bin_cos, bin_sin)
    ]
    bins = np.block([[wide[0], wide[1]], [-wide[1], wide[0]]])
    bins_twid = np.stack(turns(at[:, None] * (at % NP)[None, :], NB))
    col_order = at // per + SFT_DEV * (at % per)
    col_cos, col_sin = turns(col_order[:, None] * at[None, :], NQ)
    cols = np.block([[col_cos, -col_sin], [col_sin, col_cos]]) / math.sqrt(NB)
    fine = at // NP + SFT_DEV * (at % NP)
    fine_cos, fine_sin = turns(at[:, None] * fine[None, :], LANES)
    right = np.block([[fine_cos, -fine_sin], [fine_sin, fine_cos]])
    left = np.stack(turns(col_order[:, None] * at[None, :], NQ))
    twid = np.stack(turns(col_order[:, None] * at[None, :], NQ * LANES))
    tables = (bins, bins_twid, cols, left, twid, right)
    return tuple(jnp.asarray(table.astype(np.float32)) for table in tables)


def per_device(sft_bins, delay_code, antenna):
    band_size = lax.axis_size("band")
    owners = lax.axis_size("tm") * band_size
    sample_total = SFT_DEV * owners * NB
    tmpl_local = delay_code.shape[0]
    run_cols = RUN // NP
    runs_down = NQ // run_cols
    run_count = SFT_DEV * runs_down
    per = NQ // SFT_DEV
    code = delay_code.reshape(tmpl_local, runs_down, run_cols, LANES)
    operands = tuple(
        pltpu.with_memory_space_constraint(item, pltpu.HBM)
        for item in (sft_bins, antenna, code) + constant_tables()
    )
    bin_width = sft_bins.shape[2]
    pieces = bin_width // LANES
    block_rows = NQ // owners
    f32 = jnp.float32
    dma = pltpu.SemaphoreType.DMA
    count = len(operands)

    def kernel(*refs):
        near = refs[count + 1 : 2 * count + 1]
        search_kernel(
            band_size,
            owners,
            sample_total,
            refs[:count],
            refs[count],
            near,
            *refs[2 * count + 1 :],
        )

    out = pl.pallas_call(
        kernel,
        out_shape=pltpu.VMEM((tmpl_local, NQ, LANES), f32),
        in_specs=[pl.BlockSpec(memory_space=pltpu.HBM)] * count,
        out_specs=pl.BlockSpec(memory_space=pltpu.VMEM),
        scratch_shapes=[pltpu.VMEM(item.shape, item.dtype) for item in operands]
        + [
            pltpu.SMEM((tmpl_local, runs_down, LANES), jnp.int32),
        ]
        + [pltpu.VMEM((2 * NQ, 2 * NQ), jnp.bfloat16)] * 4
        + [
            pltpu.VMEM((2, NQ, LANES), f32),
            pltpu.VMEM((band_size, 2, SFT_DEV, bin_width), f32),
            pltpu.VMEM((band_size, 2, 2, pieces, LANES), f32),
            pltpu.VMEM((2, band_size, 2, pieces, LANES), f32),
            pltpu.VMEM((2 * per * (SFT_DEV + 2), LANES), f32),
            pltpu.VMEM((8 * run_count, LANES), f32),
            pltpu.VMEM((tmpl_local, SFT_DEV, per, LANES), jnp.int32),
            pltpu.VMEM((SFT_DEV, 2, per, LANES), f32),
        ]
        + [pltpu.VMEM((tmpl_local, owners, 2, block_rows, LANES), f32)] * 4
        + [pltpu.VMEM((tmpl_local, owners, 4, block_rows, LANES), f32)] * 2
        + [
            pltpu.VMEM((8, LANES), f32),
            pltpu.VMEM((owners, 8, LANES), f32),
            dma((band_size,)),
            dma((band_size,)),
            dma((band_size, 2)),
            dma((2, band_size)),
            dma((tmpl_local, 2, owners)),
            dma((tmpl_local, 2, owners)),
            dma((owners,)),
            dma((owners,)),
        ]
        + [dma((tmpl_local, owners))] * 4
        + [dma((count,)), dma],
        compiler_params=pltpu.CompilerParams(
            collective_id=0, has_side_effects=True, vmem_limit_bytes=48 * 1024 * 1024
        ),
    )(*operands)
    return out[:, :, None, :]


def solution(mesh):
    in_specs = (
        P(None, ("groups", "tm"), "band"),
        P(("groups", "tmpl"), None, ("tm", "band")),
        P(("groups", "tmpl"), None, None, ("tm", "band")),
    )
    out_specs = P(("groups", "tmpl"), None, ("tm", "band"), None)
    return jax.shard_map(
        per_device, mesh=mesh, in_specs=in_specs, out_specs=out_specs, check_vma=False
    )
```

```python
import functools
import math

import jax
import jax.numpy as jnp
import numpy as np
from jax import lax
from jax.experimental import pallas as pl
from jax.experimental.pallas import tpu as pltpu
from jax.sharding import PartitionSpec as P

NB = 2048
NQ = 128
NP = 16
SFT_DEV = 8
MAXD = 1000
NFRAC = 8
RUN = 256
LANES = 128

stat_eps = 1e-06
floor_share = 0.5
MESH = pl.DeviceIdType.MESH


def lagrange(fraction):
    return (
        -fraction * (fraction - 1.0) * (fraction - 2.0) / 6.0,
        (fraction + 1.0) * (fraction - 1.0) * (fraction - 2.0) / 2.0,
        -(fraction + 1.0) * fraction * (fraction - 2.0) / 2.0,
        (fraction + 1.0) * fraction * (fraction - 1.0) / 6.0,
    )


def split2(value):
    high = value.astype(jnp.bfloat16)
    return high, (value - high.astype(jnp.float32)).astype(jnp.bfloat16)


def dot3(lhs, rhs):
    lhs_hi, lhs_lo = lhs
    rhs_hi, rhs_lo = rhs
    dot = functools.partial(jnp.dot, preferred_element_type=jnp.float32)
    return dot(lhs_hi, rhs_hi) + (dot(lhs_hi, rhs_lo) + dot(lhs_lo, rhs_hi))


def swap_blocks(blocks):
    count = len(blocks)
    width = LANES // count
    blocks = list(blocks)
    lane_block = lax.broadcasted_iota(jnp.int32, blocks[0].shape, 1) // width
    half = count // 2
    while half:
        keep = (lane_block & half) == 0
        for i in range(count):
            if i & half == 0:
                low, high = blocks[i], blocks[i + half]
                blocks[i] = jnp.where(keep, low, pltpu.roll(high, half * width, 1))
                blocks[i + half] = jnp.where(
                    keep, pltpu.roll(low, LANES - half * width, 1), high
                )
        half //= 2
    return blocks


def grid_to_time(plane):
    return jnp.concatenate(swap_blocks([plane(i) for i in range(SFT_DEV)]), axis=0)


def owner_dft(real, imag):
    count = len(real)
    if count == 1:
        return real, imag
    half = count // 2
    sum_real = [real[k] + real[k + half] for k in range(half)]
    sum_imag = [imag[k] + imag[k + half] for k in range(half)]
    dif_real, dif_imag = [], []
    for k in range(half):
        d_real, d_imag = real[k] - real[k + half], imag[k] - imag[k + half]
        if k == 0:
            dif_real.append(d_real)
            dif_imag.append(d_imag)
        elif 2 * k == half:
            dif_real.append(d_imag)
            dif_imag.append(-d_real)
        else:
            cos_part = math.cos(2.0 * math.pi * k / count)
            sin_part = math.sin(2.0 * math.pi * k / count)
            dif_real.append(d_real * cos_part + d_imag * sin_part)
            dif_imag.append(d_imag * cos_part - d_real * sin_part)
    even = owner_dft(sum_real, sum_imag)
    odd = owner_dft(dif_real, dif_imag)
    out_real, out_imag = [], []
    for k in range(half):
        out_real += [even[0][k], odd[0][k]]
        out_imag += [even[1][k], odd[1][k]]
    return out_real, out_imag


def search_kernel(
    band_size,
    owners,
    sample_total,
    far_refs,
    out_ref,
    near_refs,
    start_ref,
    left_hi,
    left_lo,
    right_hi,
    right_lo,
    bins_hi,
    bins_lo,
    cols_hi,
    cols_lo,
    twid,
    grid,
    edge,
    halo,
    buf,
    seg,
    code_t,
    line,
    w_out,
    w_got,
    r_out,
    r_got,
    z_out,
    z_got,
    sums,
    sums_got,
    bin_send,
    bin_recv,
    edge_send,
    edge_recv,
    w_send,
    w_recv,
    s_send,
    s_recv,
    r_send,
    r_recv,
    z_send,
    z_recv,
    load_sem,
    start_sem,
):
    loads = [
        pltpu.make_async_copy(far, near, load_sem.at[k])
        for k, (far, near) in enumerate(zip(far_refs, near_refs))
    ]
    for load in loads:
        load.start()
    (
        bins_ref,
        ant_ref,
        code_ref,
        bins_table_ref,
        bins_twid_ref,
        cols_table_ref,
        left_ref,
        twid_ref,
        right_table_ref,
    ) = near_refs
    tmpl_local, run_rows, run_cols, _ = code_ref.shape
    starts_load = pltpu.make_async_copy(far_refs[2].at[:, :, 0, :], start_ref, start_sem)
    starts_load.start()
    code_flat = code_ref.reshape(tmpl_local, NQ, LANES)
    pieces = edge.shape[3]
    per = NQ // SFT_DEV
    block_rows = NQ // owners
    my_tm = lax.axis_index("tm")
    my_band = lax.axis_index("band")
    me = my_tm * band_size + my_band

    def place(rank):
        return {"tm": rank // band_size, "band": rank % band_size}

    def peers(body):
        def step(d, carry):
            body((me + d) % owners)
            return carry

        if owners <= SFT_DEV:
            for d in range(1, owners):
                body((me + d) % owners)
        else:
            lax.fori_loop(1, owners, step, 0)

    def remote(src, dst, send, recv, rank):
        return pltpu.make_async_remote_copy(
            src_ref=src,
            dst_ref=dst,
            send_sem=send,
            recv_sem=recv,
            device_id=place(rank),
            device_id_type=MESH,
        )

    barrier = pltpu.get_barrier_semaphore()
    peers(
        lambda rank: pl.semaphore_signal(
            barrier, inc=1, device_id=place(rank), device_id_type=MESH
        )
    )

    loads[0].wait()
    for e in range(band_size):
        for side in range(2):
            row = SFT_DEV * e + (SFT_DEV - 1 if side == 0 else 0)
            for c in range(2):
                for k in range(pieces):
                    edge[e, side, c, k : k + 1, :] = bins_ref[
                        c, row : row + 1, k * LANES : (k + 1) * LANES
                    ]

    @pl.when(me == 0)
    def _():
        halo[0] = jnp.zeros(halo.shape[1:], jnp.float32)

    @pl.when(me == owners - 1)
    def _():
        halo[1] = jnp.zeros(halo.shape[1:], jnp.float32)

    def blocked(value):
        return value.reshape(owners, block_rows, LANES)

    pl.semaphore_wait(barrier, owners - 1)

    def bins_rows(band):
        return pl.ds(pl.multiple_of(SFT_DEV * band, SFT_DEV), SFT_DEV)

    def bins_copy(d):
        band = (my_band + d) % band_size
        return remote(
            bins_ref.at[:, bins_rows(band), :],
            grid.at[my_band],
            bin_send.at[band],
            bin_recv.at[my_band],
            my_tm * band_size + band,
        )

    def bins_arrival(d):
        band = (my_band + d) % band_size
        return remote(
            bins_ref.at[:, bins_rows(band), :],
            grid.at[band],
            bin_send.at[band],
            bin_recv.at[band],
            my_tm * band_size + band,
        )

    for d in range(1, band_size):
        bins_copy(d).start()

    def edge_target(e, side):
        return my_tm * band_size + e + (1 if side == 0 else -1)

    def edge_copy(e, side):
        return remote(
            edge.at[e, side],
            halo.at[side, my_band],
            edge_send.at[e, side],
            edge_recv.at[side, my_band],
            edge_target(e, side),
        )

    def edge_is_sent(e, side):
        rank = edge_target(e, side)
        return jnp.logical_and(rank != me, jnp.logical_and(rank >= 0, rank < owners))

    for e in range(band_size):
        for side in range(2):

            @pl.when(edge_is_sent(e, side))
            def _():
                edge_copy(e, side).start()

            @pl.when(edge_target(e, side) == me)
            def _():
                halo[side, my_band] = edge[e, side]

    grid[my_band] = bins_ref[:, bins_rows(my_band), :]

    sums[...] = jnp.zeros_like(sums)
    loads[1].wait()
    for t in range(tmpl_local):
        wts = []
        for w in range(2):
            value = grid_to_time(lambda i: ant_ref[t, w, pl.ds(i, per, stride=SFT_DEV), :])
            w_out[t, :, w] = blocked(value)
            wts.append(value)
        wa, wb = wts
        for k, product in enumerate((wa * wa, wb * wb, wa * wb)):
            sums[3 * t + k : 3 * t + k + 1, :] = jnp.sum(product, axis=0, keepdims=True)
        w_got[t, me] = w_out[t, me]
    sums_got[me] = sums[...]

    def w_copy(t, w, rank, origin):
        return remote(
            w_out.at[t, rank, w],
            w_got.at[t, origin, w],
            w_send.at[t, w, rank],
            w_recv.at[t, w, origin],
            rank,
        )

    pairs = [(t, w) for t in range(tmpl_local) for w in range(2)]
    for t, w in pairs[:2]:
        peers(lambda rank: w_copy(t, w, rank, me).start())

    peers(
        lambda rank: remote(
            sums, sums_got.at[me], s_send.at[rank], s_recv.at[me], rank
        ).start()
    )

    loads[2].wait()
    for t in range(tmpl_local):
        value = grid_to_time(lambda i: code_flat[t, pl.ds(i, per, stride=SFT_DEV), :])
        code_t[t] = value.reshape(SFT_DEV, per, LANES)
    starts_load.wait()
    for load in loads[3:]:
        load.wait()
    bins_hi[...], bins_lo[...] = split2(bins_table_ref[...])
    cols_hi[...], cols_lo[...] = split2(cols_table_ref[...])
    right_hi[...], right_lo[...] = split2(right_table_ref[...] * (1.0 / math.sqrt(sample_total)))

    for d in range(1, band_size):
        bins_arrival(d).wait_recv()
    for side in range(2):
        source = (me - 1 if side == 0 else me + 1) // band_size

        @pl.when(jnp.logical_and(me > 0 if side == 0 else me < owners - 1, source != my_tm))
        def _():
            for band in range(band_size):
                remote(
                    edge.at[0, side],
                    halo.at[side, band],
                    edge_send.at[0, side],
                    edge_recv.at[side, band],
                    source * band_size + band,
                ).wait_recv()

        @pl.when(jnp.logical_and(me > 0 if side == 0 else me < owners - 1, source == my_tm))
        def _():
            for d in range(1, band_size):
                band = (my_band + d) % band_size
                remote(
                    edge.at[0, side],
                    halo.at[side, band],
                    edge_send.at[0, side],
                    edge_recv.at[side, band],
                    my_tm * band_size + band,
                ).wait_recv()

    for t, w in pairs[2:]:
        peers(lambda rank: w_copy(t, w, rank, me).start())
    sub = lax.broadcasted_iota(jnp.int32, (SFT_DEV, LANES), 0)
    main_rows, rim_rows = [], []
    for c in range(2):
        for band in range(band_size):
            for k in range(pieces):
                main_rows.append(grid[band, c, :, k * LANES : (k + 1) * LANES])
                first = jnp.broadcast_to(halo[1, band, c, k : k + 1, :], (SFT_DEV, LANES))
                final = jnp.broadcast_to(halo[0, band, c, k : k + 1, :], (SFT_DEV, LANES))
                rim_rows.append(
                    jnp.where(sub == 0, first, jnp.where(sub == SFT_DEV - 1, final, 0.0))
                )
    turned = jnp.concatenate(
        [
            jnp.transpose(jnp.concatenate(main_rows, axis=0)),
            jnp.transpose(jnp.concatenate(rim_rows, axis=0)),
        ],
        axis=0,
    )
    mixed = dot3(split2(turned), (bins_hi[...], bins_lo[...]))
    halves = []
    for h in range(2):
        real = mixed[h * LANES : (h + 1) * LANES, :LANES]
        imag = mixed[h * LANES : (h + 1) * LANES, LANES:]
        cos_part, sin_part = bins_twid_ref[0], bins_twid_ref[1]
        halves.append(
            jnp.concatenate(
                [real * cos_part - imag * sin_part, real * sin_part + imag * cos_part], axis=0
            )
        )
    series = dot3(
        (cols_hi[...], cols_lo[...]), split2(jnp.concatenate(halves, axis=1))
    )
    for c in range(2):
        for h in range(2):
            part = series[c * NQ : (c + 1) * NQ, h * LANES : (h + 1) * LANES]
            blocks = swap_blocks([part[i * per : (i + 1) * per] for i in range(SFT_DEV)])
            if h == 0:
                for s in range(SFT_DEV):
                    buf[pl.ds(2 * per * (s + 1) + c, per, stride=2), :] = blocks[s]
            else:
                buf[pl.ds(c, per, stride=2), :] = blocks[SFT_DEV - 1]
                buf[pl.ds(2 * per * (SFT_DEV + 1) + c, per, stride=2), :] = blocks[0]

    lane = lax.broadcasted_iota(jnp.int32, (8, LANES), 1)
    share = owners // SFT_DEV
    for t in range(tmpl_local):
        for d in list(range(1, SFT_DEV)) + [0]:
            sft = (me // share + d) % SFT_DEV
            base = d * 8 * run_rows
            for r in range(run_rows):
                offset = (start_ref[t, r, NP * sft] >> 3) - MAXD
                start = offset + (RUN * r + NB - 1) + NB * sft
                shift = start & (LANES - 1)
                held = buf[pl.ds(2 * (start >> 7), 8), :]
                rolled = pltpu.roll(held, LANES - shift, 1)
                below = pltpu.roll(rolled, 6, 0)
                seg[base + 8 * r : base + 8 * r + 8, :] = jnp.where(
                    lane < LANES - shift, rolled, below
                )
            coeffs = []
            for r in range(2):
                code = code_t[t, sft, pl.ds(r, run_rows, stride=2), :]
                coeffs.append(
                    lagrange((code & (NFRAC - 1)).astype(jnp.float32) * (1.0 / NFRAC))
                )
            for c in range(2):
                lines = [seg[pl.ds(base + 2 * r + c, run_rows, stride=8), :] for r in range(3)]
                moved = [lines] + [
                    [pltpu.roll(item, LANES - k, 1) for item in lines] for k in range(1, 4)
                ]
                for r in range(2):
                    total = coeffs[r][0] * moved[0][r]
                    for k in range(1, 4):
                        total = total + coeffs[r][k] * jnp.where(
                            lane < LANES - k, moved[k][r], moved[k][r + 1]
                        )
                    line[d, c, pl.ds(r, run_rows, stride=2), :] = total
                r_out[t, pl.ds(sft * share, share), c] = line[d, c].reshape(
                    share, block_rows, LANES
                )

            def send_r(k, carry):
                rank = sft * share + k

                @pl.when(rank != me)
                def _():
                    remote(
                        r_out.at[t, rank],
                        r_got.at[t, me],
                        r_send.at[t, rank],
                        r_recv.at[t, me],
                        rank,
                    ).start()

                return carry

            lax.fori_loop(0, share, send_r, 0)
        r_got[t, me] = r_out[t, me]

    at = lax.broadcasted_iota(jnp.int32, (1, LANES), 1) * me

    def advanced(table, modulus):
        angle = at.astype(jnp.float32) * (2.0 * math.pi / modulus)
        cos_step, sin_step = jnp.cos(angle), jnp.sin(angle)
        cos_base, sin_base = table[0], table[1]
        return (
            cos_base * cos_step - sin_base * sin_step,
            sin_base * cos_step + cos_base * sin_step,
        )

    cos_left, sin_left = advanced(left_ref, NQ * owners)
    parts = [[cos_left, sin_left], [-sin_left, cos_left]]
    for i in range(2):
        for j in range(2):
            spot = (slice(i * NQ, (i + 1) * NQ), slice(j * NQ, (j + 1) * NQ))
            left_hi[spot], left_lo[spot] = split2(parts[i][j])
    cos_part, sin_part = advanced(twid_ref, sample_total)
    twid[0] = cos_part
    twid[1] = -sin_part

    def arrival(out, got, send, recv, t, rank):
        return remote(out.at[t, rank], got.at[t, rank], send.at[t, rank], recv.at[t, rank], rank)

    for t in range(tmpl_local):
        for w in range(2):
            peers(lambda rank: w_copy(t, w, rank, rank).wait_recv())
        peers(lambda rank: arrival(r_out, r_got, r_send, r_recv, t, rank).wait_recv())
        for w in range(2):
            real = [r_got[t, i, 0] * w_got[t, i, w] for i in range(owners)]
            imag = [r_got[t, i, 1] * w_got[t, i, w] for i in range(owners)]
            real, imag = owner_dft(real, imag)
            for i in range(owners):
                z_out[t, i, 2 * w] = real[i]
                z_out[t, i, 2 * w + 1] = imag[i]

        def send_z(rank):
            remote(
                z_out.at[t, rank], z_got.at[t, me], z_send.at[t, rank], z_recv.at[t, me], rank
            ).start()

        peers(send_z)
        z_got[t, me] = z_out[t, me]

    def sums_arrival(rank):
        remote(sums, sums_got.at[rank], s_send.at[rank], s_recv.at[rank], rank).wait_recv()

    peers(sums_arrival)
    total = jnp.sum(sums_got[...], axis=0)
    total = jnp.sum(total, axis=1, keepdims=True) / sample_total
    for t in range(tmpl_local):
        peers(lambda rank: arrival(z_out, z_got, z_send, z_recv, t, rank).wait_recv())
        value = jnp.concatenate(
            [
                jnp.concatenate(
                    [z_got[t, :, 2 * w + c].reshape(NQ, LANES) for c in range(2)], axis=0
                )
                for w in range(2)
            ],
            axis=1,
        )
        mixed = dot3((left_hi[...], left_lo[...]), split2(value))
        lines = []
        for w in range(2):
            real = mixed[:NQ, w * LANES : (w + 1) * LANES]
            imag = mixed[NQ:, w * LANES : (w + 1) * LANES]
            cos_part, sin_part = twid[0], twid[1]
            lines.append(
                jnp.concatenate(
                    [real * cos_part - imag * sin_part, real * sin_part + imag * cos_part], axis=1
                )
            )
        spectra = dot3(
            split2(jnp.concatenate(lines, axis=0)), (right_hi[...], right_lo[...])
        )
        a_real, a_imag = spectra[:NQ, :LANES], spectra[:NQ, LANES:]
        b_real, b_imag = spectra[NQ:, :LANES], spectra[NQ:, LANES:]
        power_a = total[3 * t : 3 * t + 1] + stat_eps
        power_b = total[3 * t + 1 : 3 * t + 2] + stat_eps
        cross_ab = total[3 * t + 2 : 3 * t + 3]
        det = jnp.maximum(
            power_a * power_b - cross_ab * cross_ab, floor_share * power_a * power_b
        )
        stat = (
            (power_b / det) * (a_real * a_real + a_imag * a_imag)
            + (power_a / det) * (b_real * b_real + b_imag * b_imag)
            - (2.0 * cross_ab / det) * (a_real * b_real + a_imag * b_imag)
        )
        blocks = swap_blocks([stat[i * per : (i + 1) * per] for i in range(SFT_DEV)])
        for j, block in enumerate(blocks):
            out_ref[t, j * per : (j + 1) * per, :] = block

    def departures(rank):
        remote(sums, sums_got.at[rank], s_send.at[rank], s_recv.at[rank], rank).wait_send()
        for t in range(tmpl_local):
            for w in range(2):
                w_copy(t, w, rank, rank).wait_send()
            arrival(r_out, r_got, r_send, r_recv, t, rank).wait_send()
            arrival(z_out, z_got, z_send, z_recv, t, rank).wait_send()

    peers(departures)
    for d in range(1, band_size):
        bins_copy(d).wait_send()
    for e in range(band_size):
        for side in range(2):

            @pl.when(edge_is_sent(e, side))
            def _():
                edge_copy(e, side).wait_send()


def turns(product, modulus):
    angles = 2.0 * np.pi / modulus * (product % modulus)
    return np.cos(angles), np.sin(angles)


def constant_tables():
    per = NQ // SFT_DEV
    at = np.arange(LANES)
    bin_cos, bin_sin = turns(np.arange(NP)[:, None] * np.arange(NP)[None, :], NP)
    same = np.eye(SFT_DEV)
    wide = [
        np.einsum("kp,st->kstp", part, same).reshape(LANES, LANES) for part in (bin_cos, bin_sin)
    ]
    bins = np.block([[wide[0], wide[1]], [-wide[1], wide[0]]])
    bins_twid = np.stack(turns(at[:, None] * (at % NP)[None, :], NB))
    col_order = at // per + SFT_DEV * (at % per)
    col_cos, col_sin = turns(col_order[:, None] * at[None, :], NQ)
    cols = np.block([[col_cos, -col_sin], [col_sin, col_cos]]) / math.sqrt(NB)
    fine = at // NP + SFT_DEV * (at % NP)
    fine_cos, fine_sin = turns(at[:, None] * fine[None, :], LANES)
    right = np.block([[fine_cos, -fine_sin], [fine_sin, fine_cos]])
    left = np.stack(turns(col_order[:, None] * at[None, :], NQ))
    twid = np.stack(turns(col_order[:, None] * at[None, :], NQ * LANES))
    tables = (bins, bins_twid, cols, left, twid, right)
    return tuple(jnp.asarray(table.astype(np.float32)) for table in tables)


def per_device(sft_bins, delay_code, antenna):
    band_size = lax.axis_size("band")
    owners = lax.axis_size("tm") * band_size
    sample_total = SFT_DEV * owners * NB
    tmpl_local = delay_code.shape[0]
    run_cols = RUN // NP
    runs_down = NQ // run_cols
    run_count = SFT_DEV * runs_down
    per = NQ // SFT_DEV
    code = delay_code.reshape(tmpl_local, runs_down, run_cols, LANES)
    operands = tuple(
        pltpu.with_memory_space_constraint(item, pltpu.HBM)
        for item in (sft_bins, antenna, code) + constant_tables()
    )
    bin_width = sft_bins.shape[2]
    pieces = bin_width // LANES
    block_rows = NQ // owners
    f32 = jnp.float32
    dma = pltpu.SemaphoreType.DMA
    count = len(operands)

    def kernel(*refs):
        near = refs[count + 1 : 2 * count + 1]
        search_kernel(
            band_size,
            owners,
            sample_total,
            refs[:count],
            refs[count],
            near,
            *refs[2 * count + 1 :],
        )

    out = pl.pallas_call(
        kernel,
        out_shape=pltpu.VMEM((tmpl_local, NQ, LANES), f32),
        in_specs=[pl.BlockSpec(memory_space=pltpu.HBM)] * count,
        out_specs=pl.BlockSpec(memory_space=pltpu.VMEM),
        scratch_shapes=[pltpu.VMEM(item.shape, item.dtype) for item in operands]
        + [
            pltpu.SMEM((tmpl_local, runs_down, LANES), jnp.int32),
        ]
        + [pltpu.VMEM((2 * NQ, 2 * NQ), jnp.bfloat16)] * 8
        + [
            pltpu.VMEM((2, NQ, LANES), f32),
            pltpu.VMEM((band_size, 2, SFT_DEV, bin_width), f32),
            pltpu.VMEM((band_size, 2, 2, pieces, LANES), f32),
            pltpu.VMEM((2, band_size, 2, pieces, LANES), f32),
            pltpu.VMEM((2 * per * (SFT_DEV + 2), LANES), f32),
            pltpu.VMEM((8 * run_count, LANES), f32),
            pltpu.VMEM((tmpl_local, SFT_DEV, per, LANES), jnp.int32),
            pltpu.VMEM((SFT_DEV, 2, per, LANES), f32),
        ]
        + [pltpu.VMEM((tmpl_local, owners, 2, block_rows, LANES), f32)] * 4
        + [pltpu.VMEM((tmpl_local, owners, 4, block_rows, LANES), f32)] * 2
        + [
            pltpu.VMEM((8, LANES), f32),
            pltpu.VMEM((owners, 8, LANES), f32),
            dma((band_size,)),
            dma((band_size,)),
            dma((band_size, 2)),
            dma((2, band_size)),
            dma((tmpl_local, 2, owners)),
            dma((tmpl_local, 2, owners)),
            dma((owners,)),
            dma((owners,)),
        ]
        + [dma((tmpl_local, owners))] * 4
        + [dma((count,)), dma],
        compiler_params=pltpu.CompilerParams(
            collective_id=0, has_side_effects=True, vmem_limit_bytes=48 * 1024 * 1024
        ),
    )(*operands)
    return out[:, :, None, :]


def solution(mesh):
    in_specs = (
        P(None, ("groups", "tm"), "band"),
        P(("groups", "tmpl"), None, ("tm", "band")),
        P(("groups", "tmpl"), None, None, ("tm", "band")),
    )
    out_specs = P(("groups", "tmpl"), None, ("tm", "band"), None)
    return jax.shard_map(
        per_device, mesh=mesh, in_specs=in_specs, out_specs=out_specs, check_vma=False
    )
```

```python
import functools
import math

import jax
import jax.numpy as jnp
import numpy as np
from jax import lax
from jax.experimental import pallas as pl
from jax.experimental.pallas import tpu as pltpu
from jax.sharding import PartitionSpec as P

NB = 2048
NQ = 128
NP = 16
SFT_DEV = 8
MAXD = 1000
NFRAC = 8
RUN = 256
LANES = 128

stat_eps = 1e-06
floor_share = 0.5
MESH = pl.DeviceIdType.MESH


def lagrange(fraction):
    return (
        -fraction * (fraction - 1.0) * (fraction - 2.0) / 6.0,
        (fraction + 1.0) * (fraction - 1.0) * (fraction - 2.0) / 2.0,
        -(fraction + 1.0) * fraction * (fraction - 2.0) / 2.0,
        (fraction + 1.0) * fraction * (fraction - 1.0) / 6.0,
    )


def split2(value):
    high = value.astype(jnp.bfloat16)
    return high, (value - high.astype(jnp.float32)).astype(jnp.bfloat16)


def dot3(lhs, rhs):
    lhs_hi, lhs_lo = lhs
    rhs_hi, rhs_lo = rhs
    dot = functools.partial(jnp.dot, preferred_element_type=jnp.float32)
    return dot(lhs_hi, rhs_hi) + (dot(lhs_hi, rhs_lo) + dot(lhs_lo, rhs_hi))


def swap_blocks(blocks):
    count = len(blocks)
    width = LANES // count
    blocks = list(blocks)
    lane_block = lax.broadcasted_iota(jnp.int32, blocks[0].shape, 1) // width
    half = count // 2
    while half:
        keep = (lane_block & half) == 0
        for i in range(count):
            if i & half == 0:
                low, high = blocks[i], blocks[i + half]
                blocks[i] = jnp.where(keep, low, pltpu.roll(high, half * width, 1))
                blocks[i + half] = jnp.where(
                    keep, pltpu.roll(low, LANES - half * width, 1), high
                )
        half //= 2
    return blocks


def grid_to_time(plane):
    return jnp.concatenate(swap_blocks([plane(i) for i in range(SFT_DEV)]), axis=0)


def owner_dft(real, imag):
    count = len(real)
    if count == 1:
        return real, imag
    half = count // 2
    sum_real = [real[k] + real[k + half] for k in range(half)]
    sum_imag = [imag[k] + imag[k + half] for k in range(half)]
    dif_real, dif_imag = [], []
    for k in range(half):
        d_real, d_imag = real[k] - real[k + half], imag[k] - imag[k + half]
        if k == 0:
            dif_real.append(d_real)
            dif_imag.append(d_imag)
        elif 2 * k == half:
            dif_real.append(d_imag)
            dif_imag.append(-d_real)
        else:
            cos_part = math.cos(2.0 * math.pi * k / count)
            sin_part = math.sin(2.0 * math.pi * k / count)
            dif_real.append(d_real * cos_part + d_imag * sin_part)
            dif_imag.append(d_imag * cos_part - d_real * sin_part)
    even = owner_dft(sum_real, sum_imag)
    odd = owner_dft(dif_real, dif_imag)
    out_real, out_imag = [], []
    for k in range(half):
        out_real += [even[0][k], odd[0][k]]
        out_imag += [even[1][k], odd[1][k]]
    return out_real, out_imag


def search_kernel(
    band_size,
    owners,
    sample_total,
    far_refs,
    out_ref,
    near_refs,
    start_ref,
    left_hi,
    left_lo,
    right_hi,
    right_lo,
    bins_hi,
    bins_lo,
    cols_hi,
    cols_lo,
    twid,
    grid,
    edge,
    halo,
    buf,
    seg,
    code_t,
    line,
    w_out,
    w_got,
    r_out,
    r_got,
    z_out,
    z_got,
    sums,
    sums_got,
    bin_send,
    bin_recv,
    edge_send,
    edge_recv,
    w_send,
    w_recv,
    s_send,
    s_recv,
    r_send,
    r_recv,
    z_send,
    z_recv,
    load_sem,
    start_sem,
):
    loads = [
        pltpu.make_async_copy(far, near, load_sem.at[k])
        for k, (far, near) in enumerate(zip(far_refs, near_refs))
    ]
    for load in loads:
        load.start()
    (
        bins_ref,
        ant_ref,
        code_ref,
        bins_table_ref,
        bins_twid_ref,
        cols_table_ref,
        left_ref,
        twid_ref,
        right_table_ref,
    ) = near_refs
    tmpl_local, run_rows, run_cols, _ = code_ref.shape
    starts_load = pltpu.make_async_copy(far_refs[2].at[:, :, 0, :], start_ref, start_sem)
    starts_load.start()
    code_flat = code_ref.reshape(tmpl_local, NQ, LANES)
    pieces = edge.shape[3]
    per = NQ // SFT_DEV
    block_rows = NQ // owners
    my_tm = lax.axis_index("tm")
    my_band = lax.axis_index("band")
    me = my_tm * band_size + my_band

    def place(rank):
        return {"tm": rank // band_size, "band": rank % band_size}

    def peers(body):
        def step(d, carry):
            body((me + d) % owners)
            return carry

        if owners <= SFT_DEV:
            for d in range(1, owners):
                body((me + d) % owners)
        else:
            lax.fori_loop(1, owners, step, 0)

    def remote(src, dst, send, recv, rank):
        return pltpu.make_async_remote_copy(
            src_ref=src,
            dst_ref=dst,
            send_sem=send,
            recv_sem=recv,
            device_id=place(rank),
            device_id_type=MESH,
        )

    barrier = pltpu.get_barrier_semaphore()
    peers(
        lambda rank: pl.semaphore_signal(
            barrier, inc=1, device_id=place(rank), device_id_type=MESH
        )
    )

    loads[0].wait()
    for e in range(band_size):
        for side in range(2):
            row = SFT_DEV * e + (SFT_DEV - 1 if side == 0 else 0)
            for c in range(2):
                for k in range(pieces):
                    edge[e, side, c, k : k + 1, :] = bins_ref[
                        c, row : row + 1, k * LANES : (k + 1) * LANES
                    ]

    @pl.when(me == 0)
    def _():
        halo[0] = jnp.zeros(halo.shape[1:], jnp.float32)

    @pl.when(me == owners - 1)
    def _():
        halo[1] = jnp.zeros(halo.shape[1:], jnp.float32)

    def blocked(value):
        return value.reshape(owners, block_rows, LANES)

    sums[...] = jnp.zeros_like(sums)
    loads[1].wait()
    for t in range(tmpl_local):
        wts = []
        for w in range(2):
            value = grid_to_time(lambda i: ant_ref[t, w, pl.ds(i, per, stride=SFT_DEV), :])
            w_out[t, :, w] = blocked(value)
            wts.append(value)
        wa, wb = wts
        for k, product in enumerate((wa * wa, wb * wb, wa * wb)):
            sums[3 * t + k : 3 * t + k + 1, :] = jnp.sum(product, axis=0, keepdims=True)
        w_got[t, me] = w_out[t, me]
    sums_got[me] = sums[...]

    pl.semaphore_wait(barrier, owners - 1)

    def bins_rows(band):
        return pl.ds(pl.multiple_of(SFT_DEV * band, SFT_DEV), SFT_DEV)

    def bins_copy(d):
        band = (my_band + d) % band_size
        return remote(
            bins_ref.at[:, bins_rows(band), :],
            grid.at[my_band],
            bin_send.at[band],
            bin_recv.at[my_band],
            my_tm * band_size + band,
        )

    def bins_arrival(d):
        band = (my_band + d) % band_size
        return remote(
            bins_ref.at[:, bins_rows(band), :],
            grid.at[band],
            bin_send.at[band],
            bin_recv.at[band],
            my_tm * band_size + band,
        )

    for d in range(1, band_size):
        bins_copy(d).start()

    def edge_target(e, side):
        return my_tm * band_size + e + (1 if side == 0 else -1)

    def edge_copy(e, side):
        return remote(
            edge.at[e, side],
            halo.at[side, my_band],
            edge_send.at[e, side],
            edge_recv.at[side, my_band],
            edge_target(e, side),
        )

    def edge_is_sent(e, side):
        rank = edge_target(e, side)
        return jnp.logical_and(rank != me, jnp.logical_and(rank >= 0, rank < owners))

    for e in range(band_size):
        for side in range(2):

            @pl.when(edge_is_sent(e, side))
            def _():
                edge_copy(e, side).start()

            @pl.when(edge_target(e, side) == me)
            def _():
                halo[side, my_band] = edge[e, side]

    grid[my_band] = bins_ref[:, bins_rows(my_band), :]

    def w_copy(t, w, rank, origin):
        return remote(
            w_out.at[t, rank, w],
            w_got.at[t, origin, w],
            w_send.at[t, w, rank],
            w_recv.at[t, w, origin],
            rank,
        )

    pairs = [(t, w) for t in range(tmpl_local) for w in range(2)]
    for t, w in pairs:
        peers(lambda rank: w_copy(t, w, rank, me).start())

    peers(
        lambda rank: remote(
            sums, sums_got.at[me], s_send.at[rank], s_recv.at[me], rank
        ).start()
    )

    loads[2].wait()
    for t in range(tmpl_local):
        value = grid_to_time(lambda i: code_flat[t, pl.ds(i, per, stride=SFT_DEV), :])
        code_t[t] = value.reshape(SFT_DEV, per, LANES)
    starts_load.wait()
    for load in loads[3:]:
        load.wait()
    bins_hi[...], bins_lo[...] = split2(bins_table_ref[...])
    cols_hi[...], cols_lo[...] = split2(cols_table_ref[...])

    for d in range(1, band_size):
        bins_arrival(d).wait_recv()
    for side in range(2):
        source = (me - 1 if side == 0 else me + 1) // band_size

        @pl.when(jnp.logical_and(me > 0 if side == 0 else me < owners - 1, source != my_tm))
        def _():
            for band in range(band_size):
                remote(
                    edge.at[0, side],
                    halo.at[side, band],
                    edge_send.at[0, side],
                    edge_recv.at[side, band],
                    source * band_size + band,
                ).wait_recv()

        @pl.when(jnp.logical_and(me > 0 if side == 0 else me < owners - 1, source == my_tm))
        def _():
            for d in range(1, band_size):
                band = (my_band + d) % band_size
                remote(
                    edge.at[0, side],
                    halo.at[side, band],
                    edge_send.at[0, side],
                    edge_recv.at[side, band],
                    my_tm * band_size + band,
                ).wait_recv()

    sub = lax.broadcasted_iota(jnp.int32, (SFT_DEV, LANES), 0)
    main_rows, rim_rows = [], []
    for c in range(2):
        for band in range(band_size):
            for k in range(pieces):
                main_rows.append(grid[band, c, :, k * LANES : (k + 1) * LANES])
                first = jnp.broadcast_to(halo[1, band, c, k : k + 1, :], (SFT_DEV, LANES))
                final = jnp.broadcast_to(halo[0, band, c, k : k + 1, :], (SFT_DEV, LANES))
                rim_rows.append(
                    jnp.where(sub == 0, first, jnp.where(sub == SFT_DEV - 1, final, 0.0))
                )
    turned = jnp.concatenate(
        [
            jnp.transpose(jnp.concatenate(main_rows, axis=0)),
            jnp.transpose(jnp.concatenate(rim_rows, axis=0)),
        ],
        axis=0,
    )
    mixed = dot3(split2(turned), (bins_hi[...], bins_lo[...]))
    halves = []
    for h in range(2):
        real = mixed[h * LANES : (h + 1) * LANES, :LANES]
        imag = mixed[h * LANES : (h + 1) * LANES, LANES:]
        cos_part, sin_part = bins_twid_ref[0], bins_twid_ref[1]
        halves.append(
            jnp.concatenate(
                [real * cos_part - imag * sin_part, real * sin_part + imag * cos_part], axis=0
            )
        )
    series = dot3(
        (cols_hi[...], cols_lo[...]), split2(jnp.concatenate(halves, axis=1))
    )
    for c in range(2):
        for h in range(2):
            part = series[c * NQ : (c + 1) * NQ, h * LANES : (h + 1) * LANES]
            blocks = swap_blocks([part[i * per : (i + 1) * per] for i in range(SFT_DEV)])
            if h == 0:
                for s in range(SFT_DEV):
                    buf[pl.ds(2 * per * (s + 1) + c, per, stride=2), :] = blocks[s]
            else:
                buf[pl.ds(c, per, stride=2), :] = blocks[SFT_DEV - 1]
                buf[pl.ds(2 * per * (SFT_DEV + 1) + c, per, stride=2), :] = blocks[0]

    lane = lax.broadcasted_iota(jnp.int32, (8, LANES), 1)
    share = owners // SFT_DEV
    for t in range(tmpl_local):
        for d in list(range(1, SFT_DEV)) + [0]:
            sft = (me // share + d) % SFT_DEV
            base = d * 8 * run_rows
            for r in range(run_rows):
                offset = (start_ref[t, r, NP * sft] >> 3) - MAXD
                start = offset + (RUN * r + NB - 1) + NB * sft
                shift = start & (LANES - 1)
                held = buf[pl.ds(2 * (start >> 7), 8), :]
                rolled = pltpu.roll(held, LANES - shift, 1)
                below = pltpu.roll(rolled, 6, 0)
                seg[base + 8 * r : base + 8 * r + 8, :] = jnp.where(
                    lane < LANES - shift, rolled, below
                )
            coeffs = []
            for r in range(2):
                code = code_t[t, sft, pl.ds(r, run_rows, stride=2), :]
                coeffs.append(
                    lagrange((code & (NFRAC - 1)).astype(jnp.float32) * (1.0 / NFRAC))
                )
            for c in range(2):
                lines = [seg[pl.ds(base + 2 * r + c, run_rows, stride=8), :] for r in range(3)]
                moved = [lines] + [
                    [pltpu.roll(item, LANES - k, 1) for item in lines] for k in range(1, 4)
                ]
                for r in range(2):
                    total = coeffs[r][0] * moved[0][r]
                    for k in range(1, 4):
                        total = total + coeffs[r][k] * jnp.where(
                            lane < LANES - k, moved[k][r], moved[k][r + 1]
                        )
                    line[d, c, pl.ds(r, run_rows, stride=2), :] = total
                r_out[t, pl.ds(sft * share, share), c] = line[d, c].reshape(
                    share, block_rows, LANES
                )

            def send_r(k, carry):
                rank = sft * share + k

                @pl.when(rank != me)
                def _():
                    remote(
                        r_out.at[t, rank],
                        r_got.at[t, me],
                        r_send.at[t, rank],
                        r_recv.at[t, me],
                        rank,
                    ).start()

                return carry

            lax.fori_loop(0, share, send_r, 0)
        r_got[t, me] = r_out[t, me]

    at = lax.broadcasted_iota(jnp.int32, (1, LANES), 1) * me

    def advanced(table, modulus):
        angle = at.astype(jnp.float32) * (2.0 * math.pi / modulus)
        cos_step, sin_step = jnp.cos(angle), jnp.sin(angle)
        cos_base, sin_base = table[0], table[1]
        return (
            cos_base * cos_step - sin_base * sin_step,
            sin_base * cos_step + cos_base * sin_step,
        )

    cos_left, sin_left = advanced(left_ref, NQ * owners)
    parts = [[cos_left, sin_left], [-sin_left, cos_left]]
    for i in range(2):
        for j in range(2):
            spot = (slice(i * NQ, (i + 1) * NQ), slice(j * NQ, (j + 1) * NQ))
            left_hi[spot], left_lo[spot] = split2(parts[i][j])
    right_hi[...], right_lo[...] = split2(right_table_ref[...] * (1.0 / math.sqrt(sample_total)))
    cos_part, sin_part = advanced(twid_ref, sample_total)
    twid[0] = cos_part
    twid[1] = -sin_part

    def arrival(out, got, send, recv, t, rank):
        return remote(out.at[t, rank], got.at[t, rank], send.at[t, rank], recv.at[t, rank], rank)

    for t in range(tmpl_local):
        for w in range(2):
            peers(lambda rank: w_copy(t, w, rank, rank).wait_recv())
        peers(lambda rank: arrival(r_out, r_got, r_send, r_recv, t, rank).wait_recv())
        for w in range(2):
            real = [r_got[t, i, 0] * w_got[t, i, w] for i in range(owners)]
            imag = [r_got[t, i, 1] * w_got[t, i, w] for i in range(owners)]
            real, imag = owner_dft(real, imag)
            for i in range(owners):
                z_out[t, i, 2 * w] = real[i]
                z_out[t, i, 2 * w + 1] = imag[i]

        def send_z(rank):
            remote(
                z_out.at[t, rank], z_got.at[t, me], z_send.at[t, rank], z_recv.at[t, me], rank
            ).start()

        peers(send_z)
        z_got[t, me] = z_out[t, me]

    def sums_arrival(rank):
        remote(sums, sums_got.at[rank], s_send.at[rank], s_recv.at[rank], rank).wait_recv()

    peers(sums_arrival)
    total = jnp.sum(sums_got[...], axis=0)
    total = jnp.sum(total, axis=1, keepdims=True) / sample_total
    for t in range(tmpl_local):
        peers(lambda rank: arrival(z_out, z_got, z_send, z_recv, t, rank).wait_recv())
        value = jnp.concatenate(
            [
                jnp.concatenate(
                    [z_got[t, :, 2 * w + c].reshape(NQ, LANES) for c in range(2)], axis=0
                )
                for w in range(2)
            ],
            axis=1,
        )
        mixed = dot3((left_hi[...], left_lo[...]), split2(value))
        lines = []
        for w in range(2):
            real = mixed[:NQ, w * LANES : (w + 1) * LANES]
            imag = mixed[NQ:, w * LANES : (w + 1) * LANES]
            cos_part, sin_part = twid[0], twid[1]
            lines.append(
                jnp.concatenate(
                    [real * cos_part - imag * sin_part, real * sin_part + imag * cos_part], axis=1
                )
            )
        spectra = dot3(
            split2(jnp.concatenate(lines, axis=0)), (right_hi[...], right_lo[...])
        )
        a_real, a_imag = spectra[:NQ, :LANES], spectra[:NQ, LANES:]
        b_real, b_imag = spectra[NQ:, :LANES], spectra[NQ:, LANES:]
        power_a = total[3 * t : 3 * t + 1] + stat_eps
        power_b = total[3 * t + 1 : 3 * t + 2] + stat_eps
        cross_ab = total[3 * t + 2 : 3 * t + 3]
        det = jnp.maximum(
            power_a * power_b - cross_ab * cross_ab, floor_share * power_a * power_b
        )
        stat = (
            (power_b / det) * (a_real * a_real + a_imag * a_imag)
            + (power_a / det) * (b_real * b_real + b_imag * b_imag)
            - (2.0 * cross_ab / det) * (a_real * b_real + a_imag * b_imag)
        )
        blocks = swap_blocks([stat[i * per : (i + 1) * per] for i in range(SFT_DEV)])
        for j, block in enumerate(blocks):
            out_ref[t, j * per : (j + 1) * per, :] = block

    def departures(rank):
        remote(sums, sums_got.at[rank], s_send.at[rank], s_recv.at[rank], rank).wait_send()
        for t in range(tmpl_local):
            for w in range(2):
                w_copy(t, w, rank, rank).wait_send()
            arrival(r_out, r_got, r_send, r_recv, t, rank).wait_send()
            arrival(z_out, z_got, z_send, z_recv, t, rank).wait_send()

    peers(departures)
    for d in range(1, band_size):
        bins_copy(d).wait_send()
    for e in range(band_size):
        for side in range(2):

            @pl.when(edge_is_sent(e, side))
            def _():
                edge_copy(e, side).wait_send()


def turns(product, modulus):
    angles = 2.0 * np.pi / modulus * (product % modulus)
    return np.cos(angles), np.sin(angles)


def constant_tables():
    per = NQ // SFT_DEV
    at = np.arange(LANES)
    bin_cos, bin_sin = turns(np.arange(NP)[:, None] * np.arange(NP)[None, :], NP)
    same = np.eye(SFT_DEV)
    wide = [
        np.einsum("kp,st->kstp", part, same).reshape(LANES, LANES) for part in (bin_cos, bin_sin)
    ]
    bins = np.block([[wide[0], wide[1]], [-wide[1], wide[0]]])
    bins_twid = np.stack(turns(at[:, None] * (at % NP)[None, :], NB))
    col_order = at // per + SFT_DEV * (at % per)
    col_cos, col_sin = turns(col_order[:, None] * at[None, :], NQ)
    cols = np.block([[col_cos, -col_sin], [col_sin, col_cos]]) / math.sqrt(NB)
    fine = at // NP + SFT_DEV * (at % NP)
    fine_cos, fine_sin = turns(at[:, None] * fine[None, :], LANES)
    right = np.block([[fine_cos, -fine_sin], [fine_sin, fine_cos]])
    left = np.stack(turns(col_order[:, None] * at[None, :], NQ))
    twid = np.stack(turns(col_order[:, None] * at[None, :], NQ * LANES))
    tables = (bins, bins_twid, cols, left, twid, right)
    return tuple(jnp.asarray(table.astype(np.float32)) for table in tables)


def per_device(sft_bins, delay_code, antenna):
    band_size = lax.axis_size("band")
    owners = lax.axis_size("tm") * band_size
    sample_total = SFT_DEV * owners * NB
    tmpl_local = delay_code.shape[0]
    run_cols = RUN // NP
    runs_down = NQ // run_cols
    run_count = SFT_DEV * runs_down
    per = NQ // SFT_DEV
    code = delay_code.reshape(tmpl_local, runs_down, run_cols, LANES)
    operands = tuple(
        pltpu.with_memory_space_constraint(item, pltpu.HBM)
        for item in (sft_bins, antenna, code) + constant_tables()
    )
    bin_width = sft_bins.shape[2]
    pieces = bin_width // LANES
    block_rows = NQ // owners
    f32 = jnp.float32
    dma = pltpu.SemaphoreType.DMA
    count = len(operands)

    def kernel(*refs):
        near = refs[count + 1 : 2 * count + 1]
        search_kernel(
            band_size,
            owners,
            sample_total,
            refs[:count],
            refs[count],
            near,
            *refs[2 * count + 1 :],
        )

    out = pl.pallas_call(
        kernel,
        out_shape=pltpu.VMEM((tmpl_local, NQ, LANES), f32),
        in_specs=[pl.BlockSpec(memory_space=pltpu.HBM)] * count,
        out_specs=pl.BlockSpec(memory_space=pltpu.VMEM),
        scratch_shapes=[pltpu.VMEM(item.shape, item.dtype) for item in operands]
        + [
            pltpu.SMEM((tmpl_local, runs_down, LANES), jnp.int32),
        ]
        + [pltpu.VMEM((2 * NQ, 2 * NQ), jnp.bfloat16)] * 8
        + [
            pltpu.VMEM((2, NQ, LANES), f32),
            pltpu.VMEM((band_size, 2, SFT_DEV, bin_width), f32),
            pltpu.VMEM((band_size, 2, 2, pieces, LANES), f32),
            pltpu.VMEM((2, band_size, 2, pieces, LANES), f32),
            pltpu.VMEM((2 * per * (SFT_DEV + 2), LANES), f32),
            pltpu.VMEM((8 * run_count, LANES), f32),
            pltpu.VMEM((tmpl_local, SFT_DEV, per, LANES), jnp.int32),
            pltpu.VMEM((SFT_DEV, 2, per, LANES), f32),
        ]
        + [pltpu.VMEM((tmpl_local, owners, 2, block_rows, LANES), f32)] * 4
        + [pltpu.VMEM((tmpl_local, owners, 4, block_rows, LANES), f32)] * 2
        + [
            pltpu.VMEM((8, LANES), f32),
            pltpu.VMEM((owners, 8, LANES), f32),
            dma((band_size,)),
            dma((band_size,)),
            dma((band_size, 2)),
            dma((2, band_size)),
            dma((tmpl_local, 2, owners)),
            dma((tmpl_local, 2, owners)),
            dma((owners,)),
            dma((owners,)),
        ]
        + [dma((tmpl_local, owners))] * 4
        + [dma((count,)), dma],
        compiler_params=pltpu.CompilerParams(
            collective_id=0, has_side_effects=True, vmem_limit_bytes=48 * 1024 * 1024
        ),
    )(*operands)
    return out[:, :, None, :]


def solution(mesh):
    in_specs = (
        P(None, ("groups", "tm"), "band"),
        P(("groups", "tmpl"), None, ("tm", "band")),
        P(("groups", "tmpl"), None, None, ("tm", "band")),
    )
    out_specs = P(("groups", "tmpl"), None, ("tm", "band"), None)
    return jax.shard_map(
        per_device, mesh=mesh, in_specs=in_specs, out_specs=out_specs, check_vma=False
    )
```
